128 devices in a mesh: rep: 16 (over z, y_lo, core), dom: 8 (over y_hi, x).
Axes of the slice: x: 4, y: 4 (y_hi: 2, y_lo: 2; y = y_hi * 2 + y_lo), z: 4, core: 2. Of those that a mesh axis runs over, the one named last changes fastest.
Arguments:
- positions: float32 [16, 3, 524288], P('rep', None, 'dom'), may hold values from -6 to 6
- velocities: float32 [16, 3, 524288], P('rep', None, 'dom'), may hold values from -6 to 6
- charges: float32 [524288], P('dom'), may hold values from -5 to 5
- inv_mass: float32 [524288], P('dom'), may hold values from 0.05 to 1
- path_weight: float32 [524288], P('dom'), may hold values from -0.0078125 to 0.0078125
- halo_index: int32 [2, 131072], P(None, 'dom'), may hold values from 0 to 65535, as said below
- tile_pairs: int32 [4096, 2], P('dom'), may hold values from 0 to 767, as said below
- partner: int32 [16], P('rep'), may hold values from 0 to 15, as said below
- bias_center: float32 [16], P('rep'), may hold values from -1.5 to 1.5
- bias_spring: float32 [16], P('rep'), may hold values from 0.5 to 5
Outputs:
- new_positions: float32 [16, 3, 524288], P('rep', None, 'dom')
- new_velocities: float32 [16, 3, 524288], P('rep', None, 'dom')
- bias_energy: float32 [16], P('rep')
The draws below stay inside these ranges and needn't reach their ends.
Inputs may be any that keep to these rules, and one draw needn't show every extreme that they name: partner[partner[w]] = w, and partner[w] differs from w by at most one. `halo_index`: within one domain's block the 32768 indices of both rows are different atoms of that domain. `tile_pairs`: entries name tiles of a domain's extended list (512 own tiles, then 128 from the domain below, then 128 from the domain above); the 2 entries of one row differ.
All inputs are finite; a program needn't handle non-finite values.
Results may differ from the reference program's by a relative error of at most 0.0001.
Values sent between devices are 32-bit elements; how exact they have to be, the bound alone decides.
A program may use at most 128 MiB of HBM per device.

```python
import math
import jax
import jax.numpy as jnp
from jax import lax

ATOMS_DEV = 65536
TILE = 128
NBR = 2
STEPS = 2
GHOST = 16384
GHOST_TILES = 128
TILES_DEV = 512
WINDOWS = 16
DOMAINS = 8
ATOMS = 524288


def ensure_value(row, value):
    present = jnp.any(row == value)
    return jnp.where(present, row, row.at[row.shape[0] - 1].set(value))


def draw_partner(key, part):
    key = jax.random.fold_in(key, 11)
    phase_key, accept_key = jax.random.split(key)
    phase_value = jax.random.randint(phase_key, (), 0, 2)
    accepted = jax.random.randint(accept_key, (WINDOWS,), 0, 2)
    window_index = jnp.arange(WINDOWS, dtype=jnp.int32)
    leader = ((window_index - phase_value) % 2 == 0) & (window_index + 1 < WINDOWS) & (accepted == 1)
    follower = jnp.concatenate([jnp.zeros((1,), dtype=bool), leader[:-1]])
    chosen = jnp.where(leader, window_index + 1, jnp.where(follower, window_index - 1, window_index))
    return chosen.astype(jnp.int32)


def draw_halo_index(key, part):
    key = jax.random.fold_in(key, 5)
    domain_keys = jax.random.split(key, DOMAINS)
    chosen = jax.vmap(lambda sub_key: jax.random.permutation(sub_key, ATOMS_DEV)[:2 * GHOST])(domain_keys)
    chosen = chosen.astype(jnp.int32)
    first_row = ensure_value(chosen[0], ATOMS_DEV - 1)
    last_row = ensure_value(chosen[DOMAINS - 1], 0)
    chosen = chosen.at[0].set(first_row).at[DOMAINS - 1].set(last_row)
    return chosen.reshape(DOMAINS, 2, GHOST).transpose(1, 0, 2).reshape(2, DOMAINS * GHOST).astype(jnp.int32)


def draw_tile_pairs(key, part):
    key = jax.random.fold_in(key, 7)
    span = TILES_DEV + 2 * GHOST_TILES
    row_keys = jax.random.split(key, DOMAINS * TILES_DEV)
    chosen = jax.vmap(lambda sub_key: jax.random.permutation(sub_key, span)[:NBR])(row_keys)
    chosen = chosen.astype(jnp.int32)
    first_row = ensure_value(chosen[0], span - 1)
    last_row = ensure_value(chosen[DOMAINS * TILES_DEV - 1], 0)
    chosen = chosen.at[0].set(first_row).at[DOMAINS * TILES_DEV - 1].set(last_row)
    return chosen.astype(jnp.int32)


def block_scale(stream_key, shape, cuts, smallest, largest):
    factor_of = 1.0
    for axis_at, parts in cuts:
        steps = jax.random.uniform(jax.random.fold_in(jax.random.fold_in(stream_key, 6), axis_at), (parts,), jnp.float32, smallest / len(cuts), largest / len(cuts))
        factor_of = factor_of * jnp.repeat(jnp.exp(steps), shape[axis_at] // parts).reshape((-1,) + (1,) * (len(shape) - 1 - axis_at))
    return factor_of


def scatter_about(rng, shape, scale, reach, cuts=(), held_as=jnp.bfloat16):
    factor_of = block_scale(rng, shape, cuts, -0.22, 0.18) if cuts else 1.0
    entries = jax.random.normal(rng, shape, jnp.float32) * scale * factor_of
    return jnp.minimum(jnp.maximum(entries, -reach), reach).astype(held_as)


def setup_inputs(seed: int = 0) -> dict:
    arg_keys = jax.random.split(jax.random.key(seed), 11)
    positions = scatter_about(arg_keys[0], (WINDOWS, 3, ATOMS), 1.0, 6.0, ((0, 16), (2, 8)), jnp.float32)
    velocities = scatter_about(arg_keys[1], (WINDOWS, 3, ATOMS), 1.0, 6.0, ((0, 16), (2, 8)), jnp.float32)
    charges = scatter_about(arg_keys[2], (ATOMS,), 1.0, 5.0, ((0, 8),), jnp.float32)
    inv_mass = jnp.clip(jnp.exp(math.log(1.0) - 2.9957323 * jax.random.uniform(arg_keys[3], (ATOMS,), jnp.float32) ** block_scale(arg_keys[3], (ATOMS,), ((0, 8),), -0.2, 0.2)), 0.05, 1.0)
    path_weight = scatter_about(arg_keys[4], (ATOMS,), ATOMS ** -0.5, 0.0078125, ((0, 8),), jnp.float32)
    halo_index = draw_halo_index(jax.random.fold_in(arg_keys[10], 71), 0)
    tile_pairs = draw_tile_pairs(jax.random.fold_in(arg_keys[10], 71), 0)
    partner = draw_partner(jax.random.fold_in(arg_keys[10], 71), 0)
    bias_center = jnp.clip(jax.random.uniform(arg_keys[8], (WINDOWS,), jnp.float32, -1.5, 1.5) * block_scale(arg_keys[8], (WINDOWS,), ((0, 16),), -0.4, 0.0), -1.5, 1.5)
    bias_spring = jnp.clip(jnp.exp(math.log(5.0) - 2.3025851 * jax.random.uniform(arg_keys[9], (WINDOWS,), jnp.float32) ** block_scale(arg_keys[9], (WINDOWS,), ((0, 16),), -0.2, 0.2)), 0.5, 5.0)
    return dict(positions=positions, velocities=velocities, charges=charges, inv_mass=inv_mass, path_weight=path_weight, halo_index=halo_index, tile_pairs=tile_pairs, partner=partner, bias_center=bias_center, bias_spring=bias_spring)


time_step = 0.1


def tile_forces(extended, pairs):
    tile_count = pairs.shape[0]
    neighbours = pairs.shape[1]
    group_size = math.gcd(tile_count, 16)
    tiles_major = extended.reshape(4, extended.shape[1] // TILE, TILE).transpose(1, 0, 2)
    nearby_all = jnp.take(tiles_major, pairs.reshape(-1), axis=0)
    nearby_all = nearby_all.reshape(tile_count, neighbours, 4, TILE).transpose(0, 2, 1, 3)
    nearby_all = nearby_all.reshape(tile_count // group_size, group_size, 4, neighbours * TILE)
    own_tiles = tiles_major[:tile_count].reshape(tile_count // group_size, group_size, 4, TILE)

    def one_block(block_item):
        own_block, nearby = block_item
        offset = own_block[:, :3, :, None] - nearby[:, :3, None, :]
        spread = jnp.sum(offset * offset, axis=1) + 1.0
        weight = own_block[:, 3, :, None] * nearby[:, 3, None, :] / (spread * spread)
        return jnp.sum(offset * weight[:, None], axis=-1)

    result = lax.map(one_block, (own_tiles, nearby_all))
    return result.reshape(tile_count, 3, TILE).transpose(1, 0, 2).reshape(3, tile_count * TILE)


def reference(positions, velocities, charges, inv_mass, path_weight, halo_index, tile_pairs, partner, bias_center, bias_spring):
    moved_position = positions[partner]
    moved_velocity = velocities[partner]
    halo_blocks = halo_index.reshape(2, DOMAINS, GHOST)
    pair_blocks = tile_pairs.reshape(DOMAINS, TILES_DEV, NBR)

    def take_columns(domain_state, columns):
        return domain_state[:, columns]

    def extend(atom_state):
        by_domain = atom_state.reshape(4, DOMAINS, ATOMS_DEV).transpose(1, 0, 2)
        send_down = jax.vmap(take_columns)(by_domain, halo_blocks[0])
        send_up = jax.vmap(take_columns)(by_domain, halo_blocks[1])
        from_lower = jnp.roll(send_up, 1, axis=0)
        from_upper = jnp.roll(send_down, -1, axis=0)
        return jnp.concatenate([by_domain, from_lower, from_upper], axis=2)

    def domain_forces(domain_item):
        return tile_forces(domain_item[0], domain_item[1])

    def one_window(window_item):
        position, velocity, center, spring = window_item
        for step_index in range(STEPS):
            atom_state = jnp.concatenate([position, charges[None]], axis=0)
            extended = extend(atom_state)
            forces = lax.map(domain_forces, (extended, pair_blocks))
            forces = forces.transpose(1, 0, 2).reshape(3, ATOMS)
            progress = jnp.sum(path_weight * position[2])
            forces = forces.at[2].add(-spring * (progress - center) * path_weight)
            velocity = velocity + time_step * inv_mass * forces
            position = position + time_step * velocity
        progress = jnp.sum(path_weight * position[2])
        energy = 0.5 * spring * (progress - center) ** 2
        return position, velocity, energy

    new_positions, new_velocities, bias_energy = lax.map(one_window, (moved_position, moved_velocity, bias_center, bias_spring))
    return new_positions, new_velocities, bias_energy
```

```python
import jax
import jax.numpy as jnp
from jax import lax
from jax.experimental import pallas as pl
from jax.experimental.pallas import tpu as pltpu
from jax.sharding import PartitionSpec as P

LANES = 128
STEPS = 2
TILES = 512
GHOST_ROWS = 256
GROUPS = 16
GROUP_ROWS = 32
CELLS = 32
TILES_AT_ONCE = 8
time_step = 0.1
f32 = jnp.float32
bf16 = jnp.bfloat16
VMEM = pl.BlockSpec(memory_space=pltpu.VMEM)
SMEM = pl.BlockSpec(memory_space=pltpu.SMEM)


def params():
    return pltpu.CompilerParams(vmem_limit_bytes=58 * 1024 * 1024)


def plan_halo(halo_index):
    index = halo_index.reshape(-1)
    count = index.shape[0]
    slot = lax.iota(jnp.int32, count)
    key = ((index >> 12) << 27) | (slot << 12) | (index & 4095)
    (key,) = lax.sort((key,), num_keys=1, is_stable=False)
    group = key >> 27
    source = (group << 12) | (key & 4095)
    back = (((key >> 12) & (count - 1)) << 15) | slot
    (back,) = lax.sort((back,), num_keys=1, is_stable=False)
    place = back & (count - 1)
    block_group = (index >> 12).reshape(CELLS, count // CELLS)
    counts = jnp.sum(
        (block_group[None] == lax.iota(jnp.int32, GROUPS)[:, None, None]).astype(jnp.int32), axis=2
    ).reshape(-1)
    cells = GROUPS * CELLS
    before = (lax.iota(jnp.int32, cells)[:, None] > lax.iota(jnp.int32, cells)[None, :]).astype(jnp.int32)
    starts = jnp.sum(before * counts[None, :], axis=1)
    first_row = jnp.minimum(starts >> 7, GHOST_ROWS - 1)
    last_row = jnp.maximum(starts + counts - 1, starts) >> 7
    last_row = jnp.minimum(last_row, GHOST_ROWS - 1)
    ranges = group.reshape(GHOST_ROWS // 8, 1024)
    return (
        source.reshape(GHOST_ROWS, LANES),
        place.reshape(GHOST_ROWS, LANES),
        jnp.stack([ranges[:, 0], ranges[:, -1]]),
        jnp.stack([first_row, last_row]),
    )


def gather_stages(comps, read_row, source, place, span, cell_rows, listed, out):
    def list_block(v, carry):
        base = pl.multiple_of(v * 8, 8)
        src = source[pl.ds(base, 8), :]
        lane = src & 127
        row = src >> 7

        def one_group(group, accs):
            first = pl.multiple_of(group * GROUP_ROWS, GROUP_ROWS)
            accs = list(accs)
            for u in range(GROUP_ROWS):
                here = row == first + u
                for c in range(comps):
                    line = jnp.broadcast_to(read_row(c, first + u), (8, LANES))
                    accs[c] = jnp.where(here, jnp.take_along_axis(line, lane, axis=1), accs[c])
            return tuple(accs)

        zero = jnp.zeros((8, LANES), f32)
        accs = lax.fori_loop(span[0, v], span[1, v] + 1, one_group, (zero,) * comps)
        for c in range(comps):
            listed[c, pl.ds(base, 8), :] = accs[c]
        return carry

    lax.fori_loop(0, GHOST_ROWS // 8, list_block, 0)

    def slot_block(t, carry):
        base = pl.multiple_of(t * 8, 8)
        at = place[pl.ds(base, 8), :]
        lane = at & 127
        row = at >> 7

        def visit(r, accs):
            here = row == r
            return tuple(
                jnp.where(
                    here,
                    jnp.take_along_axis(jnp.broadcast_to(listed[c, pl.ds(r, 1), :], (8, LANES)), lane, axis=1),
                    accs[c],
                )
                for c in range(comps)
            )

        accs = (jnp.zeros((8, LANES), f32),) * comps
        widest = 0
        for g in range(GROUPS):
            first = cell_rows[0, g * CELLS + t]
            last = cell_rows[1, g * CELLS + t]
            accs = visit(first, accs)
            accs = visit(last, accs)
            widest = jnp.maximum(widest, last - first)
        for c in range(comps):
            out[c, pl.ds(base, 8), :] = accs[c]

        @pl.when(widest > 1)
        def _():
            def rest(g, accs):
                return lax.fori_loop(cell_rows[0, g * CELLS + t], cell_rows[1, g * CELLS + t] + 1, visit, accs)

            more = lax.fori_loop(0, GROUPS, rest, tuple(out[c, pl.ds(base, 8), :] for c in range(comps)))
            for c in range(comps):
                out[c, pl.ds(base, 8), :] = more[c]

        return carry

    lax.fori_loop(0, GHOST_ROWS // 8, slot_block, 0)


def first_gather_kernel(position, charges, path_weight, source, place, span, cell_rows, ghosts, partial, listed):
    def read_row(c, r):
        if c == 3:
            return charges[pl.ds(r, 1), :]
        return position[c, pl.ds(r, 1), :]

    partial[...] = jnp.sum((path_weight[...] * position[2]).reshape(64, 8, LANES), axis=0)
    gather_stages(4, read_row, source, place, span, cell_rows, listed, ghosts)


def first_gather(position, charges, path_weight, plan):
    return pl.pallas_call(
        first_gather_kernel,
        out_shape=(
            jax.ShapeDtypeStruct((4, GHOST_ROWS, LANES), f32),
            jax.ShapeDtypeStruct((8, LANES), f32),
        ),
        in_specs=[VMEM] * 5 + [SMEM] * 2,
        out_specs=(VMEM, VMEM),
        scratch_shapes=[pltpu.VMEM((4, GHOST_ROWS, LANES), f32)],
        compiler_params=params(),
        name="first_gather",
    )(position, charges, path_weight, *plan)


def parts3(value):
    high = value.astype(bf16).astype(f32)
    rest = value - high
    middle = rest.astype(bf16).astype(f32)
    return high, middle, rest - middle


def force_kernel(pairs, position, charges, lower, upper, lower_q, upper_q, force, rows_j, rows_i, rows_a, feat_j, feat_i, feat_a, sums):
    zero8 = jnp.zeros((8, LANES), f32)
    one8 = jnp.ones((8, LANES), f32)
    for f in (13, 14, 15):
        rows_j[pl.ds(f, 8, stride=16), :] = zero8
    rows_j[pl.ds(12, 8, stride=16), :] = one8
    for f in (12, 13, 14, 15):
        rows_a[pl.ds(f, 8, stride=16), :] = zero8
    rows_i[...] = jnp.zeros_like(rows_i)
    for f in (9, 10, 11):
        rows_i[pl.ds(f, 8, stride=48), :] = one8

    def build(first_tile, x, y, z, q, own):
        norm = x * x + y * y + z * z
        split = [parts3(value) for value in (x, y, z)]
        for c in range(3):
            for s in range(3):
                rows_j[pl.ds(3 * s + c, 8, stride=16), :] = split[c][s]
        for s, value in enumerate(parts3(norm)):
            rows_j[pl.ds(9 + s, 8, stride=16), :] = value
        for k, value in enumerate((q, q * x, q * y, q * z)):
            for s, piece in enumerate(parts3(value)):
                rows_a[pl.ds(4 * s + k, 8, stride=16), :] = piece
        for n in range(8):
            feat_j[first_tile + n] = rows_j[16 * n : 16 * n + 16, :].astype(bf16)
            feat_a[first_tile + n] = rows_a[16 * n : 16 * n + 16, :].astype(bf16)
        if own:
            for c in range(3):
                for s in range(3):
                    value = -2.0 * split[c][s]
                    for j in range(3 - s):
                        rows_i[pl.ds(16 * s + 3 * j + c, 8, stride=48), :] = value
            for s, value in enumerate(parts3(norm + 1.0)):
                rows_i[pl.ds(16 * s + 12, 8, stride=48), :] = value
            for n in range(8):
                feat_i[first_tile + n] = rows_i[48 * n : 48 * n + 48, :].astype(bf16)

    def own_block(b, carry):
        base = pl.multiple_of(b * 8, 8)
        here = pl.ds(base, 8)
        build(base, position[0, here, :], position[1, here, :], position[2, here, :], charges[here, :], True)
        return carry

    lax.fori_loop(0, TILES // 8, own_block, 0)

    def ghost_block(values, charge, offset):
        def block(b, carry):
            base = pl.multiple_of(b * 8, 8)
            here = pl.ds(base, 8)
            build(offset + base, values[0, here, :], values[1, here, :], values[2, here, :], charge[here, :], False)
            return carry

        return block

    lax.fori_loop(0, 16, ghost_block(lower, lower_q, TILES), 0)
    lax.fori_loop(0, 16, ghost_block(upper, upper_q, TILES + 128), 0)

    def contract(a, b, left, right):
        return lax.dot_general(a, b, (((left,), (right,)), ((), ())), preferred_element_type=f32)

    def tiles(n, carry):
        found = []
        for u in range(TILES_AT_ONCE):
            tile = n * TILES_AT_ONCE + u
            one, two = pairs[2 * tile], pairs[2 * tile + 1]
            near = jnp.concatenate([feat_j[one], feat_j[two]], axis=1)
            spread = contract(jnp.concatenate([near] * 3, axis=0), feat_i[tile], 0, 0)
            found.append((tile, one, two, spread))
        done = []
        for tile, one, two, spread in found:
            weight = pl.reciprocal(spread * spread, approx=True)
            high = weight.astype(bf16)
            low = (weight - high.astype(f32)).astype(bf16)
            near = jnp.concatenate([feat_a[one], feat_a[two]], axis=1)
            done.append(
                (
                    tile,
                    contract(
                        jnp.concatenate([near, near], axis=1), jnp.concatenate([high, low], axis=0), 1, 0
                    ),
                )
            )
        for tile, value in done:
            sums[pl.ds(pl.multiple_of(tile * 16, 16), 16), :] = value
        return carry

    lax.fori_loop(0, TILES // TILES_AT_ONCE, tiles, 0)

    def combine(b, carry):
        base = pl.multiple_of(b * 8, 8)
        here = pl.ds(base, 8)
        total = []
        for k in range(4):
            value = sums[pl.ds(base * 16 + k, 8, stride=16), :]
            value = value + sums[pl.ds(base * 16 + 4 + k, 8, stride=16), :]
            value = value + sums[pl.ds(base * 16 + 8 + k, 8, stride=16), :]
            total.append(value)
        q = charges[here, :]
        for c in range(3):
            force[c, here, :] = q * (position[c, here, :] * total[0] - total[c + 1])
        return carry

    lax.fori_loop(0, TILES // 8, combine, 0)


def pair_forces(pairs, position, charges, lower, upper, lower_q, upper_q):
    return pl.pallas_call(
        force_kernel,
        out_shape=jax.ShapeDtypeStruct((3, TILES, LANES), f32),
        in_specs=[SMEM] + [VMEM] * 6,
        out_specs=VMEM,
        scratch_shapes=[
            pltpu.VMEM((8 * 16, LANES), f32),
            pltpu.VMEM((8 * 48, LANES), f32),
            pltpu.VMEM((8 * 16, LANES), f32),
            pltpu.VMEM((TILES + 256, 16, LANES), bf16),
            pltpu.VMEM((TILES, 48, LANES), bf16),
            pltpu.VMEM((TILES + 256, 16, LANES), bf16),
            pltpu.VMEM((TILES * 16, LANES), f32),
        ],
        compiler_params=params(),
        name="pair_forces",
    )(pairs, position, charges, lower, upper, lower_q, upper_q)


def advance(scalars, position, velocity, force, inv_mass, path_weight, new_position, new_velocity):
    weight = path_weight[...]
    rate = time_step * inv_mass[...]
    pull = scalars[0] * (scalars[1] - scalars[2])
    for c in range(3):
        total = force[c]
        if c == 2:
            total = total - pull * weight
        moved = velocity[c] + rate * total
        new_velocity[c] = moved
        new_position[c] = position[c] + time_step * moved
    return jnp.sum((weight * new_position[2]).reshape(64, 8, LANES), axis=0)


def middle_kernel(
    scalars, position, velocity, force, inv_mass, path_weight, source, place, span, cell_rows,
    new_position, new_velocity, ghosts, partial, listed,
):
    partial[...] = advance(scalars, position, velocity, force, inv_mass, path_weight, new_position, new_velocity)

    def read_row(c, r):
        return new_position[c, pl.ds(r, 1), :]

    gather_stages(3, read_row, source, place, span, cell_rows, listed, ghosts)


def last_kernel(scalars, position, velocity, force, inv_mass, path_weight, new_position, new_velocity, partial):
    partial[...] = advance(scalars, position, velocity, force, inv_mass, path_weight, new_position, new_velocity)


def middle_update(scalars, position, velocity, force, inv_mass, path_weight, plan):
    whole = jax.ShapeDtypeStruct((3, TILES, LANES), f32)
    return pl.pallas_call(
        middle_kernel,
        out_shape=(
            whole,
            whole,
            jax.ShapeDtypeStruct((3, GHOST_ROWS, LANES), f32),
            jax.ShapeDtypeStruct((8, LANES), f32),
        ),
        in_specs=[SMEM] + [VMEM] * 7 + [SMEM] * 2,
        out_specs=(VMEM,) * 4,
        scratch_shapes=[pltpu.VMEM((3, GHOST_ROWS, LANES), f32)],
        compiler_params=params(),
        name="middle_update",
    )(scalars, position, velocity, force, inv_mass, path_weight, *plan)


def last_update(scalars, position, velocity, force, inv_mass, path_weight):
    whole = jax.ShapeDtypeStruct((3, TILES, LANES), f32)
    return pl.pallas_call(
        last_kernel,
        out_shape=(whole, whole, jax.ShapeDtypeStruct((8, LANES), f32)),
        in_specs=[SMEM] + [VMEM] * 5,
        out_specs=(VMEM,) * 3,
        compiler_params=params(),
        name="last_update",
    )(scalars, position, velocity, force, inv_mass, path_weight)


def passed_along(shard, axis, by):
    count = lax.axis_size(axis)
    return lax.ppermute(shard, axis, [(i, (i + by) % count) for i in range(count)])


def shifted(shard, axis, by):
    count = lax.axis_size(axis)
    pairs = [(i, i + by) for i in range(count) if 0 <= i + by < count]
    return lax.ppermute(shard, axis, pairs)


def body(positions, velocities, charges, inv_mass, path_weight, halo_index, tile_pairs, partner, bias_center, bias_spring):
    position = positions[0].reshape(3, TILES, LANES)
    velocity = velocities[0].reshape(3, TILES, LANES)
    charges = charges.reshape(TILES, LANES)
    inv_mass = inv_mass.reshape(TILES, LANES)
    path_weight = path_weight.reshape(TILES, LANES)
    pairs = tile_pairs.reshape(-1)
    partner_now = partner[0]
    window = lax.axis_index("rep")

    def choose(own, below, above):
        return jnp.where(partner_now == window - 1, below, jnp.where(partner_now == window + 1, above, own))

    position_below = shifted(position, "rep", 1)
    position_above = shifted(position, "rep", -1)
    velocity_below = shifted(velocity, "rep", 1)
    velocity_above = shifted(velocity, "rep", -1)
    plan = plan_halo(halo_index)
    position = choose(position, position_below, position_above)
    velocity = choose(velocity, velocity_below, velocity_above)
    center = bias_center[0]
    spring = bias_spring[0]

    half = GHOST_ROWS // 2
    ghosts, partial = first_gather(position, charges, path_weight, plan)
    lower = passed_along(ghosts[:, half:], "dom", 1)
    upper = passed_along(ghosts[:, :half], "dom", -1)
    lower_q, upper_q = lower[3], upper[3]
    for step_index in range(STEPS):
        progress = lax.psum(jnp.sum(partial), "dom")
        force = pair_forces(pairs, position, charges, lower, upper, lower_q, upper_q)
        scalars = jnp.stack([spring, progress, center])
        if step_index < STEPS - 1:
            position, velocity, ghosts, partial = middle_update(
                scalars, position, velocity, force, inv_mass, path_weight, plan
            )
            lower = passed_along(ghosts[:, half:], "dom", 1)
            upper = passed_along(ghosts[:, :half], "dom", -1)
        else:
            position, velocity, partial = last_update(scalars, position, velocity, force, inv_mass, path_weight)
    progress = lax.psum(jnp.sum(partial), "dom")
    energy = 0.5 * spring * (progress - center) ** 2
    atoms = TILES * LANES
    return position.reshape(1, 3, atoms), velocity.reshape(1, 3, atoms), energy[None]


def solution(mesh):
    in_specs = (
        P("rep", None, "dom"),
        P("rep", None, "dom"),
        P("dom"),
        P("dom"),
        P("dom"),
        P(None, "dom"),
        P("dom", None),
        P("rep"),
        P("rep"),
        P("rep"),
    )
    out_specs = (P("rep", None, "dom"), P("rep", None, "dom"), P("rep"))
    return jax.shard_map(body, mesh=mesh, in_specs=in_specs, out_specs=out_specs, check_vma=False)
```

```python
import jax
import jax.numpy as jnp
from jax import lax
from jax.experimental import pallas as pl
from jax.experimental.pallas import tpu as pltpu
from jax.sharding import PartitionSpec as P

LANES = 128
STEPS = 2
TILES = 512
GHOST_ROWS = 256
GROUPS = 16
GROUP_ROWS = 32
CELLS = 32
TILES_AT_ONCE = 16
time_step = 0.1
f32 = jnp.float32
bf16 = jnp.bfloat16
VMEM = pl.BlockSpec(memory_space=pltpu.VMEM)
SMEM = pl.BlockSpec(memory_space=pltpu.SMEM)


def params():
    return pltpu.CompilerParams(vmem_limit_bytes=58 * 1024 * 1024)


def plan_halo(halo_index):
    index = halo_index.reshape(-1)
    count = index.shape[0]
    slot = lax.iota(jnp.int32, count)
    key = ((index >> 12) << 27) | (slot << 12) | (index & 4095)
    (key,) = lax.sort((key,), num_keys=1, is_stable=False)
    group = key >> 27
    source = (group << 12) | (key & 4095)
    back = (((key >> 12) & (count - 1)) << 15) | slot
    (back,) = lax.sort((back,), num_keys=1, is_stable=False)
    place = back & (count - 1)
    block_group = (index >> 12).reshape(CELLS, count // CELLS)
    counts = jnp.sum(
        (block_group[None] == lax.iota(jnp.int32, GROUPS)[:, None, None]).astype(jnp.int32), axis=2
    ).reshape(-1)
    cells = GROUPS * CELLS
    before = (lax.iota(jnp.int32, cells)[:, None] > lax.iota(jnp.int32, cells)[None, :]).astype(jnp.int32)
    starts = jnp.sum(before * counts[None, :], axis=1)
    first_row = jnp.minimum(starts >> 7, GHOST_ROWS - 1)
    last_row = jnp.maximum(starts + counts - 1, starts) >> 7
    last_row = jnp.minimum(last_row, GHOST_ROWS - 1)
    ranges = group.reshape(GHOST_ROWS // 8, 1024)
    return (
        source.reshape(GHOST_ROWS, LANES),
        place.reshape(GHOST_ROWS, LANES),
        jnp.stack([ranges[:, 0], ranges[:, -1]]),
        jnp.stack([first_row, last_row]),
    )


def gather_stages(comps, read_row, source, place, span, cell_rows, listed, out):
    def list_block(v, carry):
        base = pl.multiple_of(v * 8, 8)
        src = source[pl.ds(base, 8), :]
        lane = src & 127
        row = src >> 7

        def one_group(group, accs):
            first = pl.multiple_of(group * GROUP_ROWS, GROUP_ROWS)
            accs = list(accs)
            for u in range(GROUP_ROWS):
                here = row == first + u
                for c in range(comps):
                    line = jnp.broadcast_to(read_row(c, first + u), (8, LANES))
                    accs[c] = jnp.where(here, jnp.take_along_axis(line, lane, axis=1), accs[c])
            return tuple(accs)

        zero = jnp.zeros((8, LANES), f32)
        accs = lax.fori_loop(span[0, v], span[1, v] + 1, one_group, (zero,) * comps)
        for c in range(comps):
            listed[c, pl.ds(base, 8), :] = accs[c]
        return carry

    lax.fori_loop(0, GHOST_ROWS // 8, list_block, 0)

    def slot_block(t, carry):
        base = pl.multiple_of(t * 8, 8)
        at = place[pl.ds(base, 8), :]
        lane = at & 127
        row = at >> 7

        def visit(r, accs):
            here = row == r
            return tuple(
                jnp.where(
                    here,
                    jnp.take_along_axis(jnp.broadcast_to(listed[c, pl.ds(r, 1), :], (8, LANES)), lane, axis=1),
                    accs[c],
                )
                for c in range(comps)
            )

        accs = (jnp.zeros((8, LANES), f32),) * comps
        widest = 0
        for g in range(GROUPS):
            first = cell_rows[0, g * CELLS + t]
            last = cell_rows[1, g * CELLS + t]
            accs = visit(first, accs)
            accs = visit(last, accs)
            widest = jnp.maximum(widest, last - first)
        for c in range(comps):
            out[c, pl.ds(base, 8), :] = accs[c]

        @pl.when(widest > 1)
        def _():
            def rest(g, accs):
                return lax.fori_loop(cell_rows[0, g * CELLS + t], cell_rows[1, g * CELLS + t] + 1, visit, accs)

            more = lax.fori_loop(0, GROUPS, rest, tuple(out[c, pl.ds(base, 8), :] for c in range(comps)))
            for c in range(comps):
                out[c, pl.ds(base, 8), :] = more[c]

        return carry

    lax.fori_loop(0, GHOST_ROWS // 8, slot_block, 0)


def first_gather_kernel(position, charges, path_weight, source, place, span, cell_rows, ghosts, partial, listed):
    def read_row(c, r):
        if c == 3:
            return charges[pl.ds(r, 1), :]
        return position[c, pl.ds(r, 1), :]

    partial[...] = jnp.sum((path_weight[...] * position[2]).reshape(64, 8, LANES), axis=0)
    gather_stages(4, read_row, source, place, span, cell_rows, listed, ghosts)


def first_gather(position, charges, path_weight, plan):
    return pl.pallas_call(
        first_gather_kernel,
        out_shape=(
            jax.ShapeDtypeStruct((4, GHOST_ROWS, LANES), f32),
            jax.ShapeDtypeStruct((8, LANES), f32),
        ),
        in_specs=[VMEM] * 5 + [SMEM] * 2,
        out_specs=(VMEM, VMEM),
        scratch_shapes=[pltpu.VMEM((4, GHOST_ROWS, LANES), f32)],
        compiler_params=params(),
        name="first_gather",
    )(position, charges, path_weight, *plan)


def parts3(value):
    high = value.astype(bf16).astype(f32)
    rest = value - high
    middle = rest.astype(bf16).astype(f32)
    return high, middle, rest - middle


def force_kernel(pairs, position, charges, lower, upper, lower_q, upper_q, force, rows_j, rows_i, rows_a, feat_j, feat_i, feat_a, sums, spread_a, spread_b):
    zero8 = jnp.zeros((8, LANES), f32)
    one8 = jnp.ones((8, LANES), f32)
    for f in (13, 14, 15):
        rows_j[pl.ds(f, 8, stride=16), :] = zero8
    rows_j[pl.ds(12, 8, stride=16), :] = one8
    for f in (12, 13, 14, 15):
        rows_a[pl.ds(f, 8, stride=16), :] = zero8
    rows_i[...] = jnp.zeros_like(rows_i)
    for f in (9, 10, 11):
        rows_i[pl.ds(f, 8, stride=48), :] = one8

    def build(first_tile, x, y, z, q, own):
        norm = x * x + y * y + z * z
        split = [parts3(value) for value in (x, y, z)]
        for c in range(3):
            for s in range(3):
                rows_j[pl.ds(3 * s + c, 8, stride=16), :] = split[c][s]
        for s, value in enumerate(parts3(norm)):
            rows_j[pl.ds(9 + s, 8, stride=16), :] = value
        for k, value in enumerate((q, q * x, q * y, q * z)):
            for s, piece in enumerate(parts3(value)):
                rows_a[pl.ds(4 * s + k, 8, stride=16), :] = piece
        for n in range(8):
            feat_j[first_tile + n] = rows_j[16 * n : 16 * n + 16, :].astype(bf16)
            feat_a[first_tile + n] = rows_a[16 * n : 16 * n + 16, :].astype(bf16)
        if own:
            for c in range(3):
                for s in range(3):
                    value = -2.0 * split[c][s]
                    for j in range(3 - s):
                        rows_i[pl.ds(16 * s + 3 * j + c, 8, stride=48), :] = value
            for s, value in enumerate(parts3(norm + 1.0)):
                rows_i[pl.ds(16 * s + 12, 8, stride=48), :] = value
            for n in range(8):
                feat_i[first_tile + n] = rows_i[48 * n : 48 * n + 48, :].astype(bf16)

    def own_block(b, carry):
        base = pl.multiple_of(b * 8, 8)
        here = pl.ds(base, 8)
        build(base, position[0, here, :], position[1, here, :], position[2, here, :], charges[here, :], True)
        return carry

    lax.fori_loop(0, TILES // 8, own_block, 0)

    def ghost_block(values, charge, offset):
        def block(b, carry):
            base = pl.multiple_of(b * 8, 8)
            here = pl.ds(base, 8)
            build(offset + base, values[0, here, :], values[1, here, :], values[2, here, :], charge[here, :], False)
            return carry

        return block

    lax.fori_loop(0, 16, ghost_block(lower, lower_q, TILES), 0)
    lax.fori_loop(0, 16, ghost_block(upper, upper_q, TILES + 128), 0)

    def contract(a, b, left, right):
        return lax.dot_general(a, b, (((left,), (right,)), ((), ())), preferred_element_type=f32)

    def listed(tile):
        tile = jnp.minimum(tile, TILES - 1)
        return tile, pairs[2 * tile], pairs[2 * tile + 1]

    def spread_of(tile):
        tile, one, two = listed(tile)
        near = jnp.concatenate([feat_j[one], feat_j[two]], axis=1)
        return contract(jnp.concatenate([near] * 3, axis=0), feat_i[tile], 0, 0)

    def force_of(tile, spread):
        tile, one, two = listed(tile)
        weight = pl.reciprocal(spread * spread, approx=True)
        high = weight.astype(bf16)
        low = (weight - high.astype(f32)).astype(bf16)
        near = jnp.concatenate([feat_a[one], feat_a[two]], axis=1)
        return contract(jnp.concatenate([near, near], axis=1), jnp.concatenate([high, low], axis=0), 1, 0)

    many = TILES_AT_ONCE
    for u in range(many):
        spread_a[u] = spread_of(u)

    def tiles(m, carry):
        for now, later, n in ((spread_a, spread_b, 2 * m), (spread_b, spread_a, 2 * m + 1)):
            done = []
            for u in range(many):
                later[u] = spread_of((n + 1) * many + u)
                done.append(force_of(n * many + u, now[u]))
            for u in range(many):
                sums[pl.ds(pl.multiple_of((n * many + u) * 16, 16), 16), :] = done[u]
        return carry

    lax.fori_loop(0, TILES // many // 2, tiles, 0)

    def combine(b, carry):
        base = pl.multiple_of(b * 8, 8)
        here = pl.ds(base, 8)
        total = []
        for k in range(4):
            value = sums[pl.ds(base * 16 + k, 8, stride=16), :]
            value = value + sums[pl.ds(base * 16 + 4 + k, 8, stride=16), :]
            value = value + sums[pl.ds(base * 16 + 8 + k, 8, stride=16), :]
            total.append(value)
        q = charges[here, :]
        for c in range(3):
            force[c, here, :] = q * (position[c, here, :] * total[0] - total[c + 1])
        return carry

    lax.fori_loop(0, TILES // 8, combine, 0)


def pair_forces(pairs, position, charges, lower, upper, lower_q, upper_q):
    return pl.pallas_call(
        force_kernel,
        out_shape=jax.ShapeDtypeStruct((3, TILES, LANES), f32),
        in_specs=[SMEM] + [VMEM] * 6,
        out_specs=VMEM,
        scratch_shapes=[
            pltpu.VMEM((8 * 16, LANES), f32),
            pltpu.VMEM((8 * 48, LANES), f32),
            pltpu.VMEM((8 * 16, LANES), f32),
            pltpu.VMEM((TILES + 256, 16, LANES), bf16),
            pltpu.VMEM((TILES, 48, LANES), bf16),
            pltpu.VMEM((TILES + 256, 16, LANES), bf16),
            pltpu.VMEM((TILES * 16, LANES), f32),
            pltpu.VMEM((TILES_AT_ONCE, 2 * LANES, LANES), f32),
            pltpu.VMEM((TILES_AT_ONCE, 2 * LANES, LANES), f32),
        ],
        compiler_params=params(),
        name="pair_forces",
    )(pairs, position, charges, lower, upper, lower_q, upper_q)


def advance(scalars, parts, position, velocity, force, inv_mass, path_weight, new_position, new_velocity):
    weight = path_weight[...]
    rate = time_step * inv_mass[...]
    pull = scalars[0] * (jnp.sum(parts[...]) - scalars[1])
    for c in range(3):
        total = force[c]
        if c == 2:
            total = total - pull * weight
        moved = velocity[c] + rate * total
        new_velocity[c] = moved
        new_position[c] = position[c] + time_step * moved
    return jnp.sum((weight * new_position[2]).reshape(64, 8, LANES), axis=0)


def middle_kernel(
    scalars, parts, position, velocity, force, inv_mass, path_weight, source, place, span, cell_rows,
    new_position, new_velocity, ghosts, partial, listed,
):
    partial[...] = advance(scalars, parts, position, velocity, force, inv_mass, path_weight, new_position, new_velocity)

    def read_row(c, r):
        return new_position[c, pl.ds(r, 1), :]

    gather_stages(3, read_row, source, place, span, cell_rows, listed, ghosts)


def last_kernel(scalars, parts, position, velocity, force, inv_mass, path_weight, new_position, new_velocity, partial):
    partial[...] = advance(scalars, parts, position, velocity, force, inv_mass, path_weight, new_position, new_velocity)


def middle_update(scalars, parts, position, velocity, force, inv_mass, path_weight, plan):
    whole = jax.ShapeDtypeStruct((3, TILES, LANES), f32)
    return pl.pallas_call(
        middle_kernel,
        out_shape=(
            whole,
            whole,
            jax.ShapeDtypeStruct((3, GHOST_ROWS, LANES), f32),
            jax.ShapeDtypeStruct((8, LANES), f32),
        ),
        in_specs=[SMEM] + [VMEM] * 8 + [SMEM] * 2,
        out_specs=(VMEM,) * 4,
        scratch_shapes=[pltpu.VMEM((3, GHOST_ROWS, LANES), f32)],
        compiler_params=params(),
        name="middle_update",
    )(scalars, parts, position, velocity, force, inv_mass, path_weight, *plan)


def last_update(scalars, parts, position, velocity, force, inv_mass, path_weight):
    whole = jax.ShapeDtypeStruct((3, TILES, LANES), f32)
    return pl.pallas_call(
        last_kernel,
        out_shape=(whole, whole, jax.ShapeDtypeStruct((8, LANES), f32)),
        in_specs=[SMEM] + [VMEM] * 6,
        out_specs=(VMEM,) * 3,
        compiler_params=params(),
        name="last_update",
    )(scalars, parts, position, velocity, force, inv_mass, path_weight)


def exchange_kernel(count, half, ghosts, partial, lower, upper, parts, sent, got, local):
    me = lax.axis_index("dom")
    barrier = pltpu.get_barrier_semaphore()
    for k in range(1, count):
        pl.semaphore_signal(
            barrier, inc=1, device_id={"dom": lax.rem(me + k, count)}, device_id_type=pl.DeviceIdType.MESH
        )
    pl.semaphore_wait(barrier, count - 1)
    copies = []

    def send(source, target, k, n):
        copy = pltpu.make_async_remote_copy(
            src_ref=source,
            dst_ref=target,
            send_sem=sent.at[n],
            recv_sem=got.at[n],
            device_id={"dom": lax.rem(me + k, count)},
            device_id_type=pl.DeviceIdType.MESH,
        )
        copy.start()
        copies.append(copy)

    if half:
        send(ghosts.at[:, pl.ds(half, half)], lower, 1, 0)
        send(ghosts.at[:, pl.ds(0, half)], upper, count - 1, count)
    for k in range(1, count):
        send(partial, parts.at[me], k, k)
    own = pltpu.make_async_copy(partial, parts.at[me], local)
    own.start()
    own.wait()
    for copy in copies:
        copy.wait()


def exchange(ghosts, partial, number):
    count = lax.axis_size("dom")
    comps, rows = ghosts.shape[:2]
    side = jax.ShapeDtypeStruct((comps, rows // 2, LANES), f32)

    def kernel(*refs):
        exchange_kernel(count, rows // 2, *refs)

    return pl.pallas_call(
        kernel,
        out_shape=(side, side, jax.ShapeDtypeStruct((count, 8, LANES), f32)),
        in_specs=[VMEM] * 2,
        out_specs=(VMEM,) * 3,
        scratch_shapes=[
            pltpu.SemaphoreType.DMA((count + 1,)),
            pltpu.SemaphoreType.DMA((count + 1,)),
            pltpu.SemaphoreType.DMA,
        ],
        compiler_params=pltpu.CompilerParams(collective_id=number, has_side_effects=True),
        name="exchange",
    )(ghosts, partial)


def share_energy(partial, scalars, number):
    count = lax.axis_size("dom")

    def kernel(partial, scalars, energy, parts, sent, got, local):
        exchange_kernel(count, 0, None, partial, None, None, parts, sent, got, local)
        off = jnp.sum(parts[...]) - scalars[1]
        energy[...] = jnp.full((8, LANES), 0.5 * scalars[0] * off * off, f32)

    return pl.pallas_call(
        kernel,
        out_shape=jax.ShapeDtypeStruct((8, LANES), f32),
        in_specs=[VMEM, SMEM],
        out_specs=VMEM,
        scratch_shapes=[
            pltpu.VMEM((count, 8, LANES), f32),
            pltpu.SemaphoreType.DMA((count,)),
            pltpu.SemaphoreType.DMA((count,)),
            pltpu.SemaphoreType.DMA,
        ],
        compiler_params=pltpu.CompilerParams(collective_id=number, has_side_effects=True),
        name="share_energy",
    )(partial, scalars)


def shifted(shard, axis, by):
    count = lax.axis_size(axis)
    pairs = [(i, i + by) for i in range(count) if 0 <= i + by < count]
    return lax.ppermute(shard, axis, pairs)


def body(positions, velocities, charges, inv_mass, path_weight, halo_index, tile_pairs, partner, bias_center, bias_spring):
    position = positions[0].reshape(3, TILES, LANES)
    velocity = velocities[0].reshape(3, TILES, LANES)
    charges = charges.reshape(TILES, LANES)
    inv_mass = inv_mass.reshape(TILES, LANES)
    path_weight = path_weight.reshape(TILES, LANES)
    pairs = tile_pairs.reshape(-1)
    partner_now = partner[0]
    window = lax.axis_index("rep")

    def choose(own, below, above):
        return jnp.where(partner_now == window - 1, below, jnp.where(partner_now == window + 1, above, own))

    position_below = shifted(position, "rep", 1)
    position_above = shifted(position, "rep", -1)
    velocity_below = shifted(velocity, "rep", 1)
    velocity_above = shifted(velocity, "rep", -1)
    plan = plan_halo(halo_index)
    position = choose(position, position_below, position_above)
    velocity = choose(velocity, velocity_below, velocity_above)
    center = bias_center[0]
    spring = bias_spring[0]

    scalars = jnp.stack([spring, center])
    ghosts, partial = first_gather(position, charges, path_weight, plan)
    for step_index in range(STEPS):
        lower, upper, parts = exchange(ghosts, partial, step_index)
        if step_index == 0:
            lower_q, upper_q = lower[3], upper[3]
        force = pair_forces(pairs, position, charges, lower, upper, lower_q, upper_q)
        if step_index < STEPS - 1:
            position, velocity, ghosts, partial = middle_update(
                scalars, parts, position, velocity, force, inv_mass, path_weight, plan
            )
        else:
            position, velocity, partial = last_update(scalars, parts, position, velocity, force, inv_mass, path_weight)
    energy = share_energy(partial, scalars, STEPS)[0, :1]
    atoms = TILES * LANES
    return position.reshape(1, 3, atoms), velocity.reshape(1, 3, atoms), energy


def solution(mesh):
    in_specs = (
        P("rep", None, "dom"),
        P("rep", None, "dom"),
        P("dom"),
        P("dom"),
        P("dom"),
        P(None, "dom"),
        P("dom", None),
        P("rep"),
        P("rep"),
        P("rep"),
    )
    out_specs = (P("rep", None, "dom"), P("rep", None, "dom"), P("rep"))
    return jax.shard_map(body, mesh=mesh, in_specs=in_specs, out_specs=out_specs, check_vma=False)
```

```python
import jax
import jax.numpy as jnp
from jax import lax
from jax.experimental import pallas as pl
from jax.experimental.pallas import tpu as pltpu
from jax.sharding import PartitionSpec as P

LANES = 128
STEPS = 2
TILES = 512
GHOST_ROWS = 256
GROUPS = 16
GROUP_ROWS = 32
CELLS = 32
TILES_AT_ONCE = 16
time_step = 0.1
f32 = jnp.float32
bf16 = jnp.bfloat16
VMEM = pl.BlockSpec(memory_space=pltpu.VMEM)
SMEM = pl.BlockSpec(memory_space=pltpu.SMEM)


def params():
    return pltpu.CompilerParams(vmem_limit_bytes=58 * 1024 * 1024)


def plan_halo(halo_index):
    index = halo_index.reshape(-1)
    count = index.shape[0]
    slot = lax.iota(jnp.int32, count)
    key = ((index >> 12) << 27) | (slot << 12) | (index & 4095)
    (key,) = lax.sort((key,), num_keys=1, is_stable=False)
    group = key >> 27
    source = (group << 12) | (key & 4095)
    back = (((key >> 12) & (count - 1)) << 15) | slot
    (back,) = lax.sort((back,), num_keys=1, is_stable=False)
    place = back & (count - 1)
    block_group = (index >> 12).reshape(CELLS, count // CELLS)
    counts = jnp.sum(
        (block_group[None] == lax.iota(jnp.int32, GROUPS)[:, None, None]).astype(jnp.int32), axis=2
    ).reshape(-1)
    cells = GROUPS * CELLS
    before = (lax.iota(jnp.int32, cells)[:, None] > lax.iota(jnp.int32, cells)[None, :]).astype(jnp.int32)
    starts = jnp.sum(before * counts[None, :], axis=1)
    first_row = jnp.minimum(starts >> 7, GHOST_ROWS - 1)
    last_row = jnp.maximum(starts + counts - 1, starts) >> 7
    last_row = jnp.minimum(last_row, GHOST_ROWS - 1)
    ranges = group.reshape(GHOST_ROWS // 8, 1024)
    return (
        source.reshape(GHOST_ROWS, LANES),
        place.reshape(GHOST_ROWS, LANES),
        jnp.stack([ranges[:, 0], ranges[:, -1]]),
        jnp.stack([first_row, last_row]),
    )


def gather_stages(comps, read_row, source, place, span, cell_rows, listed, out):
    def list_block(v, carry):
        base = pl.multiple_of(v * 8, 8)
        src = source[pl.ds(base, 8), :]
        lane = src & 127
        row = src >> 7

        def one_group(group, accs):
            first = pl.multiple_of(group * GROUP_ROWS, GROUP_ROWS)
            accs = list(accs)
            for u in range(GROUP_ROWS):
                here = row == first + u
                for c in range(comps):
                    line = jnp.broadcast_to(read_row(c, first + u), (8, LANES))
                    accs[c] = jnp.where(here, jnp.take_along_axis(line, lane, axis=1), accs[c])
            return tuple(accs)

        zero = jnp.zeros((8, LANES), f32)
        accs = lax.fori_loop(span[0, v], span[1, v] + 1, one_group, (zero,) * comps)
        for c in range(comps):
            listed[c, pl.ds(base, 8), :] = accs[c]
        return carry

    lax.fori_loop(0, GHOST_ROWS // 8, list_block, 0)

    def slot_block(t, carry):
        base = pl.multiple_of(t * 8, 8)
        at = place[pl.ds(base, 8), :]
        lane = at & 127
        row = at >> 7

        def visit(r, accs):
            here = row == r
            return tuple(
                jnp.where(
                    here,
                    jnp.take_along_axis(jnp.broadcast_to(listed[c, pl.ds(r, 1), :], (8, LANES)), lane, axis=1),
                    accs[c],
                )
                for c in range(comps)
            )

        accs = (jnp.zeros((8, LANES), f32),) * comps
        widest = 0
        for g in range(GROUPS):
            first = cell_rows[0, g * CELLS + t]
            last = cell_rows[1, g * CELLS + t]
            accs = visit(first, accs)
            accs = visit(last, accs)
            widest = jnp.maximum(widest, last - first)
        for c in range(comps):
            out[c, pl.ds(base, 8), :] = accs[c]

        @pl.when(widest > 1)
        def _():
            def rest(g, accs):
                return lax.fori_loop(cell_rows[0, g * CELLS + t], cell_rows[1, g * CELLS + t] + 1, visit, accs)

            more = lax.fori_loop(0, GROUPS, rest, tuple(out[c, pl.ds(base, 8), :] for c in range(comps)))
            for c in range(comps):
                out[c, pl.ds(base, 8), :] = more[c]

        return carry

    lax.fori_loop(0, GHOST_ROWS // 8, slot_block, 0)


def first_gather_kernel(position, charges, path_weight, source, place, span, cell_rows, ghosts, partial, listed):
    def read_row(c, r):
        if c == 3:
            return charges[pl.ds(r, 1), :]
        return position[c, pl.ds(r, 1), :]

    partial[...] = jnp.sum((path_weight[...] * position[2]).reshape(64, 8, LANES), axis=0)
    gather_stages(4, read_row, source, place, span, cell_rows, listed, ghosts)


def first_gather(position, charges, path_weight, plan):
    return pl.pallas_call(
        first_gather_kernel,
        out_shape=(
            jax.ShapeDtypeStruct((4, GHOST_ROWS, LANES), f32),
            jax.ShapeDtypeStruct((8, LANES), f32),
        ),
        in_specs=[VMEM] * 5 + [SMEM] * 2,
        out_specs=(VMEM, VMEM),
        scratch_shapes=[pltpu.VMEM((4, GHOST_ROWS, LANES), f32)],
        compiler_params=params(),
        name="first_gather",
    )(position, charges, path_weight, *plan)


def parts3(value):
    high = value.astype(bf16).astype(f32)
    rest = value - high
    middle = rest.astype(bf16).astype(f32)
    return high, middle, rest - middle


def step_kernel(
    count, last, scalars, pairs, ghosts, partial, position, velocity, charges, lower_q, upper_q, inv_mass, path_weight,
    new_position, new_velocity, result, *rest,
):
    if last:
        kept_q = ()
    else:
        kept_q, rest = rest[:2], rest[2:]
    (
        rows_j, rows_i, rows_a, feat_j, feat_i, feat_a, sums, spread_a, spread_b,
        lower, upper, parts, final, sent, got, sent_last, got_last,
    ) = rest
    me = lax.axis_index("dom")
    half = GHOST_ROWS // 2
    barrier = pltpu.get_barrier_semaphore()
    for k in range(1, count):
        pl.semaphore_signal(
            barrier, inc=1, device_id={"dom": lax.rem(me + k, count)}, device_id_type=pl.DeviceIdType.MESH
        )
    pl.semaphore_wait(barrier, count - 1)

    def send(source, target, k, sent_now, got_now):
        copy = pltpu.make_async_remote_copy(
            src_ref=source,
            dst_ref=target,
            send_sem=sent_now,
            recv_sem=got_now,
            device_id={"dom": lax.rem(me + k, count)},
            device_id_type=pl.DeviceIdType.MESH,
        )
        copy.start()
        return copy

    ghost_copies = [
        send(ghosts.at[:, pl.ds(half, half)], lower, 1, sent.at[0], got.at[0]),
        send(ghosts.at[:, pl.ds(0, half)], upper, count - 1, sent.at[count], got.at[count]),
    ]
    term_copies = [send(partial, parts.at[me], k, sent.at[k], got.at[k]) for k in range(1, count)]

    zero8 = jnp.zeros((8, LANES), f32)
    one8 = jnp.ones((8, LANES), f32)
    for f in (13, 14, 15):
        rows_j[pl.ds(f, 8, stride=16), :] = zero8
    rows_j[pl.ds(12, 8, stride=16), :] = one8
    for f in (12, 13, 14, 15):
        rows_a[pl.ds(f, 8, stride=16), :] = zero8
    rows_i[...] = jnp.zeros_like(rows_i)
    for f in (9, 10, 11):
        rows_i[pl.ds(f, 8, stride=48), :] = one8

    def build(first_tile, x, y, z, q, own):
        norm = x * x + y * y + z * z
        split = [parts3(value) for value in (x, y, z)]
        for c in range(3):
            for s in range(3):
                rows_j[pl.ds(3 * s + c, 8, stride=16), :] = split[c][s]
        for s, value in enumerate(parts3(norm)):
            rows_j[pl.ds(9 + s, 8, stride=16), :] = value
        for k, value in enumerate((q, q * x, q * y, q * z)):
            for s, piece in enumerate(parts3(value)):
                rows_a[pl.ds(4 * s + k, 8, stride=16), :] = piece
        for n in range(8):
            feat_j[first_tile + n] = rows_j[16 * n : 16 * n + 16, :].astype(bf16)
            feat_a[first_tile + n] = rows_a[16 * n : 16 * n + 16, :].astype(bf16)
        if own:
            for c in range(3):
                for s in range(3):
                    value = -2.0 * split[c][s]
                    for j in range(3 - s):
                        rows_i[pl.ds(16 * s + 3 * j + c, 8, stride=48), :] = value
            for s, value in enumerate(parts3(norm + 1.0)):
                rows_i[pl.ds(16 * s + 12, 8, stride=48), :] = value
            for n in range(8):
                feat_i[first_tile + n] = rows_i[48 * n : 48 * n + 48, :].astype(bf16)

    def own_block(b, carry):
        base = pl.multiple_of(b * 8, 8)
        here = pl.ds(base, 8)
        build(base, position[0, here, :], position[1, here, :], position[2, here, :], charges[here, :], True)
        return carry

    lax.fori_loop(0, TILES // 8, own_block, 0)

    def ghost_block(values, charge, offset):
        def block(b, carry):
            base = pl.multiple_of(b * 8, 8)
            here = pl.ds(base, 8)
            build(offset + base, values[0, here, :], values[1, here, :], values[2, here, :], charge[here, :], False)
            return carry

        return block

    for copy in ghost_copies:
        copy.wait()
    if last:
        charge_of = (lower_q, upper_q)
    else:
        charge_of = (lower.at[3], upper.at[3])
        kept_q[0][...] = lower[3]
        kept_q[1][...] = upper[3]
    lax.fori_loop(0, 16, ghost_block(lower, charge_of[0], TILES), 0)
    lax.fori_loop(0, 16, ghost_block(upper, charge_of[1], TILES + 128), 0)

    def contract(a, b, left, right):
        return lax.dot_general(a, b, (((left,), (right,)), ((), ())), preferred_element_type=f32)

    def listed(tile):
        tile = jnp.minimum(tile, TILES - 1)
        return tile, pairs[2 * tile], pairs[2 * tile + 1]

    def spread_of(tile):
        tile, one, two = listed(tile)
        near = jnp.concatenate([feat_j[one], feat_j[two]], axis=1)
        return contract(jnp.concatenate([near] * 3, axis=0), feat_i[tile], 0, 0)

    def force_of(tile, spread):
        tile, one, two = listed(tile)
        weight = pl.reciprocal(spread * spread, approx=True)
        high = weight.astype(bf16)
        low = (weight - high.astype(f32)).astype(bf16)
        near = jnp.concatenate([feat_a[one], feat_a[two]], axis=1)
        return contract(jnp.concatenate([near, near], axis=1), jnp.concatenate([high, low], axis=0), 1, 0)

    many = TILES_AT_ONCE
    for u in range(many):
        spread_a[u] = spread_of(u)

    def tiles(m, carry):
        for now, later, n in ((spread_a, spread_b, 2 * m), (spread_b, spread_a, 2 * m + 1)):
            done = []
            for u in range(many):
                later[u] = spread_of((n + 1) * many + u)
                done.append(force_of(n * many + u, now[u]))
            for u in range(many):
                sums[pl.ds(pl.multiple_of((n * many + u) * 16, 16), 16), :] = done[u]
        return carry

    lax.fori_loop(0, TILES // many // 2, tiles, 0)

    def total_of(terms, own, copies):
        for copy in copies:
            copy.wait()
        terms[me] = own[...]
        return jnp.sum(terms[...])

    progress = total_of(parts, partial, term_copies)
    pull = scalars[0] * (progress - scalars[1])

    def combine(b, part):
        base = pl.multiple_of(b * 8, 8)
        here = pl.ds(base, 8)
        total = []
        for k in range(4):
            value = sums[pl.ds(base * 16 + k, 8, stride=16), :]
            value = value + sums[pl.ds(base * 16 + 4 + k, 8, stride=16), :]
            value = value + sums[pl.ds(base * 16 + 8 + k, 8, stride=16), :]
            total.append(value)
        q = charges[here, :]
        weight = path_weight[here, :]
        rate = time_step * inv_mass[here, :]
        for c in range(3):
            old = position[c, here, :]
            force = q * (old * total[0] - total[c + 1])
            if c == 2:
                force = force - pull * weight
            moved = velocity[c, here, :] + rate * force
            placed = old + time_step * moved
            new_velocity[c, here, :] = moved
            new_position[c, here, :] = placed
        return part + weight * placed

    ending = lax.fori_loop(0, TILES // 8, combine, jnp.zeros((8, LANES), f32))
    if last:
        partial_last = spread_a.at[0, pl.ds(0, 8), :]
        spread_a[0, pl.ds(0, 8), :] = ending
        final_copies = [
            send(partial_last, final.at[me], k, sent_last.at[k], got_last.at[k]) for k in range(1, count)
        ]
        off = total_of(final, partial_last, final_copies) - scalars[1]
        result[...] = jnp.full((8, LANES), 0.5 * scalars[0] * off * off, f32)
    else:
        result[...] = ending


def step(number, last, scalars, pairs, ghosts, partial, position, velocity, charges, lower_q, upper_q, inv_mass, path_weight):
    count = lax.axis_size("dom")
    comps, rows = ghosts.shape[:2]
    whole = jax.ShapeDtypeStruct((3, TILES, LANES), f32)
    side_q = jax.ShapeDtypeStruct((rows // 2, LANES), f32)
    kept = () if last else (side_q, side_q)

    def kernel(*refs):
        step_kernel(count, last, *refs)

    return pl.pallas_call(
        kernel,
        out_shape=(whole, whole, jax.ShapeDtypeStruct((8, LANES), f32)) + kept,
        in_specs=[SMEM] * 2 + [VMEM] * 9,
        out_specs=(VMEM,) * (3 + len(kept)),
        scratch_shapes=[
            pltpu.VMEM((8 * 16, LANES), f32),
            pltpu.VMEM((8 * 48, LANES), f32),
            pltpu.VMEM((8 * 16, LANES), f32),
            pltpu.VMEM((TILES + 256, 16, LANES), bf16),
            pltpu.VMEM((TILES, 48, LANES), bf16),
            pltpu.VMEM((TILES + 256, 16, LANES), bf16),
            pltpu.VMEM((TILES * 16, LANES), f32),
            pltpu.VMEM((TILES_AT_ONCE, 2 * LANES, LANES), f32),
            pltpu.VMEM((TILES_AT_ONCE, 2 * LANES, LANES), f32),
            pltpu.VMEM((comps, rows // 2, LANES), f32),
            pltpu.VMEM((comps, rows // 2, LANES), f32),
            pltpu.VMEM((count, 8, LANES), f32),
            pltpu.VMEM((count, 8, LANES), f32),
            pltpu.SemaphoreType.DMA((count + 1,)),
            pltpu.SemaphoreType.DMA((count + 1,)),
            pltpu.SemaphoreType.DMA((count,)),
            pltpu.SemaphoreType.DMA((count,)),
        ],
        compiler_params=pltpu.CompilerParams(
            vmem_limit_bytes=58 * 1024 * 1024, collective_id=number, has_side_effects=True
        ),
        name="step",
    )(scalars, pairs, ghosts, partial, position, velocity, charges, lower_q, upper_q, inv_mass, path_weight)


def second_gather_kernel(position, source, place, span, cell_rows, ghosts, listed):
    def read_row(c, r):
        return position[c, pl.ds(r, 1), :]

    gather_stages(3, read_row, source, place, span, cell_rows, listed, ghosts)


def second_gather(position, plan):
    return pl.pallas_call(
        second_gather_kernel,
        out_shape=jax.ShapeDtypeStruct((3, GHOST_ROWS, LANES), f32),
        in_specs=[VMEM] * 3 + [SMEM] * 2,
        out_specs=VMEM,
        scratch_shapes=[pltpu.VMEM((3, GHOST_ROWS, LANES), f32)],
        compiler_params=params(),
        name="second_gather",
    )(position, *plan)


def shifted(shard, axis, by):
    count = lax.axis_size(axis)
    pairs = [(i, i + by) for i in range(count) if 0 <= i + by < count]
    return lax.ppermute(shard, axis, pairs)


def body(positions, velocities, charges, inv_mass, path_weight, halo_index, tile_pairs, partner, bias_center, bias_spring):
    position = positions[0].reshape(3, TILES, LANES)
    velocity = velocities[0].reshape(3, TILES, LANES)
    charges = charges.reshape(TILES, LANES)
    inv_mass = inv_mass.reshape(TILES, LANES)
    path_weight = path_weight.reshape(TILES, LANES)
    pairs = tile_pairs.reshape(-1)
    partner_now = partner[0]
    window = lax.axis_index("rep")

    def choose(own, below, above):
        return jnp.where(partner_now == window - 1, below, jnp.where(partner_now == window + 1, above, own))

    position_below = shifted(position, "rep", 1)
    position_above = shifted(position, "rep", -1)
    velocity_below = shifted(velocity, "rep", 1)
    velocity_above = shifted(velocity, "rep", -1)
    plan = plan_halo(halo_index)
    position = choose(position, position_below, position_above)
    velocity = choose(velocity, velocity_below, velocity_above)
    center = bias_center[0]
    spring = bias_spring[0]

    scalars = jnp.stack([spring, center])
    ghosts, partial = first_gather(position, charges, path_weight, plan)
    lower_q = upper_q = jnp.zeros((GHOST_ROWS // 2, LANES), f32)
    for step_index in range(STEPS):
        last = step_index == STEPS - 1
        position, velocity, partial, *kept_q = step(
            step_index, last, scalars, pairs, ghosts, partial, position, velocity,
            charges, lower_q, upper_q, inv_mass, path_weight,
        )
        if not last:
            lower_q, upper_q = kept_q
            ghosts = second_gather(position, plan)
    energy = partial[0, :1]
    atoms = TILES * LANES
    return position.reshape(1, 3, atoms), velocity.reshape(1, 3, atoms), energy


def solution(mesh):
    in_specs = (
        P("rep", None, "dom"),
        P("rep", None, "dom"),
        P("dom"),
        P("dom"),
        P("dom"),
        P(None, "dom"),
        P("dom", None),
        P("rep"),
        P("rep"),
        P("rep"),
    )
    out_specs = (P("rep", None, "dom"), P("rep", None, "dom"), P("rep"))
    return jax.shard_map(body, mesh=mesh, in_specs=in_specs, out_specs=out_specs, check_vma=False)
```

```python
import jax
import jax.numpy as jnp
from jax import lax
from jax.experimental import pallas as pl
from jax.experimental.pallas import tpu as pltpu
from jax.sharding import PartitionSpec as P

LANES = 128
STEPS = 2
TILES = 512
GHOST_ROWS = 256
GROUPS = 16
GROUP_ROWS = 32
CELLS = 32
CAPACITY = 4096
TILES_AT_ONCE = 16
time_step = 0.1
f32 = jnp.float32
bf16 = jnp.bfloat16
VMEM = pl.BlockSpec(memory_space=pltpu.VMEM)
SMEM = pl.BlockSpec(memory_space=pltpu.SMEM)


def params():
    return pltpu.CompilerParams(vmem_limit_bytes=58 * 1024 * 1024)


def start_kernel(
    count, position, halo, below, above, source, place, cells, sent, got,
):
    me = lax.axis_index("rep")
    ahead, behind = lax.rem(me + 1, count), lax.rem(me + count - 1, count)
    barrier = pltpu.get_barrier_semaphore()
    for other in (ahead, behind):
        pl.semaphore_signal(barrier, inc=1, device_id={"rep": other}, device_id_type=pl.DeviceIdType.MESH)
    pl.semaphore_wait(barrier, 2)
    copies = []
    for n, (other, target) in enumerate(((ahead, below), (behind, above))):
        copy = pltpu.make_async_remote_copy(
            src_ref=position,
            dst_ref=target,
            send_sem=sent.at[n],
            recv_sem=got.at[n],
            device_id={"rep": other},
            device_id_type=pl.DeviceIdType.MESH,
        )
        copy.start()
        copies.append(copy)

    shape = (GHOST_ROWS, LANES)
    row = lax.broadcasted_iota(jnp.int32, shape, 0)
    lane = lax.broadcasted_iota(jnp.int32, shape, 1)
    wide = (LANES, 2 * LANES)
    across = lax.broadcasted_iota(jnp.int32, wide, 1)
    ahead_lane = (lax.broadcasted_iota(jnp.int32, wide, 0) < across) | (across >= LANES)
    ahead_lane = jnp.where(ahead_lane, 1.0, 0.0).astype(bf16)
    square = (GHOST_ROWS, GHOST_ROWS)
    ahead_row = lax.broadcasted_iota(jnp.int32, square, 1) < lax.broadcasted_iota(jnp.int32, square, 0)
    ahead_row = jnp.where(ahead_row, 1.0, 0.0).astype(bf16)
    place[...] = jnp.zeros(shape, jnp.int32)

    def one_group(group, carry):
        index = halo[...]
        member = (index >> 12) == group
        flag = jnp.where(member, 1.0, 0.0).astype(bf16)
        within = jnp.dot(flag, ahead_lane, preferred_element_type=f32)
        in_row = within[:, LANES:]
        earlier = jnp.dot(ahead_row, in_row.astype(bf16), preferred_element_type=f32)
        rank = (within[:, :LANES] + earlier).astype(jnp.int32)
        place[...] = jnp.where(member, rank + group * CAPACITY, place[...])
        marks = jnp.where(lane * 8 == row, earlier, 0.0)
        marks = marks + jnp.where((lane == CELLS) & (row == GHOST_ROWS - 1), earlier + in_row, 0.0)
        marks = jnp.sum(marks.reshape(GHOST_ROWS // 8, 8, LANES), axis=0)
        cells[pl.ds(pl.multiple_of(group * 8, 8), 8), :] = jnp.broadcast_to(
            jnp.sum(marks, axis=0, keepdims=True), (8, LANES)
        ).astype(jnp.int32)
        shift = row * LANES + lane - rank
        items = jnp.where(member, (1 << 28) | (shift << 12) | (index & 4095), 0)
        for bit in range(15):
            step_by = 1 << bit
            if step_by < LANES:
                following = pltpu.roll(items, items.shape[0] - 1, 0)
                mixed = jnp.where(lane < step_by, following, items)
                moved = pltpu.roll(mixed, LANES - step_by, 1)
                held = items
            else:
                rows = step_by // LANES
                if rows < 32:
                    if rows < 8:
                        moved = pltpu.roll(items, items.shape[0] - rows, 0)
                    else:
                        moved = jnp.concatenate([items[rows:], items[:rows]], axis=0)
                    held = items
                else:
                    blocks = items.reshape(items.shape[0] // 64, 2, 32, LANES)
                    held = blocks[:, 0].reshape(-1, LANES)
                    moved = blocks[:, 1].reshape(-1, LANES)
            mask = 1 << (12 + bit)
            items = jnp.where((moved & mask) != 0, moved, jnp.where((held & mask) != 0, 0, held))
        source[pl.ds(pl.multiple_of(group * 32, 32), 32), :] = items & 4095
        return carry

    lax.fori_loop(0, GROUPS, one_group, 0)
    for copy in copies:
        copy.wait()


def start(position, halo, number):
    count = lax.axis_size("rep")
    whole = jax.ShapeDtypeStruct(position.shape, f32)

    def kernel(*refs):
        start_kernel(count, *refs)

    anywhere = pl.BlockSpec(memory_space=pl.ANY)
    return pl.pallas_call(
        kernel,
        out_shape=(
            whole,
            whole,
            jax.ShapeDtypeStruct((GROUPS * 32, LANES), jnp.int32),
            jax.ShapeDtypeStruct((GHOST_ROWS, LANES), jnp.int32),
            jax.ShapeDtypeStruct((GROUPS * 8, LANES), jnp.int32),
        ),
        in_specs=[anywhere, VMEM],
        out_specs=(anywhere, anywhere, VMEM, VMEM, VMEM),
        scratch_shapes=[pltpu.SemaphoreType.DMA((2,)), pltpu.SemaphoreType.DMA((2,))],
        compiler_params=pltpu.CompilerParams(
            vmem_limit_bytes=32 * 1024 * 1024, collective_id=number, has_side_effects=True
        ),
        name="start",
    )(position, halo)


def gather_stages(comps, read_row, source, place, cells, listed, out):
    zeros = (jnp.zeros((8, LANES), f32),) * comps

    def one_group(group, carry):
        first = pl.multiple_of(group * GROUP_ROWS, GROUP_ROWS)

        def list_block(v, carry):
            here = pl.ds(pl.multiple_of(first + v * 8, 8), 8)
            src = source[here, :]
            lane = src & 127
            row = src >> 7
            accs = list(zeros)
            for u in range(GROUP_ROWS):
                mine = row == u
                for c in range(comps):
                    line = jnp.broadcast_to(read_row(c, first + u), (8, LANES))
                    accs[c] = jnp.where(mine, jnp.take_along_axis(line, lane, axis=1), accs[c])
            for c in range(comps):
                listed[c, here, :] = accs[c]
            return carry

        return lax.fori_loop(0, (cells[group * 8, CELLS] + 1023) >> 10, list_block, carry)

    lax.fori_loop(0, GROUPS, one_group, 0)

    def slot_block(t, carry):
        here = pl.ds(pl.multiple_of(t * 8, 8), 8)
        at = place[here, :]
        lane = at & 127
        row = at >> 7

        def visit(r, accs):
            mine = row == r
            return tuple(
                jnp.where(
                    mine,
                    jnp.take_along_axis(jnp.broadcast_to(listed[c, pl.ds(r, 1), :], (8, LANES)), lane, axis=1),
                    accs[c],
                )
                for c in range(comps)
            )

        def rows_of(g):
            begin, end = cells[g * 8, t], cells[g * 8, t + 1]
            return g * 32 + jnp.minimum(begin >> 7, 31), g * 32 + (jnp.maximum(end - 1, begin) >> 7)

        accs = zeros
        widest = 0
        for g in range(GROUPS):
            first, last = rows_of(g)
            last = jnp.minimum(last, g * 32 + 31)
            accs = visit(first, accs)
            accs = visit(last, accs)
            widest = jnp.maximum(widest, last - first)
        for c in range(comps):
            out[c, here, :] = accs[c]

        @pl.when(widest > 1)
        def _():
            def rest(g, accs):
                first, last = rows_of(g)
                return lax.fori_loop(first, jnp.minimum(last, g * 32 + 31) + 1, visit, accs)

            more = lax.fori_loop(0, GROUPS, rest, tuple(out[c, here, :] for c in range(comps)))
            for c in range(comps):
                out[c, here, :] = more[c]

        return carry

    lax.fori_loop(0, GHOST_ROWS // 8, slot_block, 0)


def pick(partner, window, own, below, above):
    wanted = jnp.full(own.shape, partner, jnp.int32)
    return jnp.where(wanted == window - 1, below, jnp.where(wanted == window + 1, above, own))


def first_gather_kernel(
    partner, cells, own, below, above, charges, path_weight, source, place, position, ghosts, partial, listed
):
    window = lax.axis_index("rep")
    for c in range(3):
        position[c] = pick(partner[0], window, own[c], below[c], above[c])

    def read_row(c, r):
        if c == 3:
            return charges[pl.ds(r, 1), :]
        return position[c, pl.ds(r, 1), :]

    partial[...] = jnp.sum((path_weight[...] * position[2]).reshape(64, 8, LANES), axis=0)
    gather_stages(4, read_row, source, place, cells, listed, ghosts)


def first_gather(partner, own, below, above, charges, path_weight, source, place, cells):
    return pl.pallas_call(
        first_gather_kernel,
        out_shape=(
            jax.ShapeDtypeStruct((3, TILES, LANES), f32),
            jax.ShapeDtypeStruct((4, GHOST_ROWS, LANES), f32),
            jax.ShapeDtypeStruct((8, LANES), f32),
        ),
        in_specs=[SMEM] * 2 + [VMEM] * 7,
        out_specs=(VMEM,) * 3,
        scratch_shapes=[pltpu.VMEM((4, GROUPS * 32, LANES), f32)],
        compiler_params=params(),
        name="first_gather",
    )(partner, cells, own, below, above, charges, path_weight, source, place)


def parts3(value):
    high = value.astype(bf16).astype(f32)
    rest = value - high
    middle = rest.astype(bf16).astype(f32)
    return high, middle, rest - middle


def step_kernel(
    count, windows, last, scalars, partner, pairs, ghosts, partial, position, velocity, charges, lower_q, upper_q, inv_mass, path_weight,
    new_position, new_velocity, result, *rest,
):
    if last:
        kept_q = ()
    else:
        kept_q, rest = rest[:2], rest[2:]
        rest, velocity_below, velocity_above, sent_v, got_v = rest[:-4], *rest[-4:]
    (
        rows_j, rows_i, rows_a, feat_j, feat_i, feat_a, sums, spread_a, spread_b,
        lower, upper, parts, final, sent, got, sent_last, got_last,
    ) = rest
    me = lax.axis_index("dom")
    half = GHOST_ROWS // 2
    barrier = pltpu.get_barrier_semaphore()
    for k in range(1, count):
        pl.semaphore_signal(
            barrier, inc=1, device_id={"dom": lax.rem(me + k, count)}, device_id_type=pl.DeviceIdType.MESH
        )
    if last:
        pl.semaphore_wait(barrier, count - 1)
    else:
        window = lax.axis_index("rep")
        ahead, behind = lax.rem(window + 1, windows), lax.rem(window + windows - 1, windows)
        for other in (ahead, behind):
            pl.semaphore_signal(barrier, inc=1, device_id={"rep": other}, device_id_type=pl.DeviceIdType.MESH)
        pl.semaphore_wait(barrier, count + 1)

    def send(source, target, k, sent_now, got_now):
        copy = pltpu.make_async_remote_copy(
            src_ref=source,
            dst_ref=target,
            send_sem=sent_now,
            recv_sem=got_now,
            device_id={"dom": lax.rem(me + k, count)},
            device_id_type=pl.DeviceIdType.MESH,
        )
        copy.start()
        return copy

    ghost_copies = [
        send(ghosts.at[:, pl.ds(half, half)], lower, 1, sent.at[0], got.at[0]),
        send(ghosts.at[:, pl.ds(0, half)], upper, count - 1, sent.at[count], got.at[count]),
    ]
    term_copies = [send(partial, parts.at[me], k, sent.at[k], got.at[k]) for k in range(1, count)]
    velocity_copies = []
    if not last:
        for n, (other, target) in enumerate(((ahead, velocity_below), (behind, velocity_above))):
            copy = pltpu.make_async_remote_copy(
                src_ref=velocity,
                dst_ref=target,
                send_sem=sent_v.at[n],
                recv_sem=got_v.at[n],
                device_id={"rep": other},
                device_id_type=pl.DeviceIdType.MESH,
            )
            copy.start()
            velocity_copies.append(copy)

    zero8 = jnp.zeros((8, LANES), f32)
    one8 = jnp.ones((8, LANES), f32)
    for f in (13, 14, 15):
        rows_j[pl.ds(f, 8, stride=16), :] = zero8
    rows_j[pl.ds(12, 8, stride=16), :] = one8
    for f in (12, 13, 14, 15):
        rows_a[pl.ds(f, 8, stride=16), :] = zero8
    rows_i[...] = jnp.zeros_like(rows_i)
    for f in (9, 10, 11):
        rows_i[pl.ds(f, 8, stride=48), :] = one8

    def build(first_tile, x, y, z, q, own):
        norm = x * x + y * y + z * z
        split = [parts3(value) for value in (x, y, z)]
        for c in range(3):
            for s in range(3):
                rows_j[pl.ds(3 * s + c, 8, stride=16), :] = split[c][s]
        for s, value in enumerate(parts3(norm)):
            rows_j[pl.ds(9 + s, 8, stride=16), :] = value
        for k, value in enumerate((q, q * x, q * y, q * z)):
            for s, piece in enumerate(parts3(value)):
                rows_a[pl.ds(4 * s + k, 8, stride=16), :] = piece
        for n in range(8):
            feat_j[first_tile + n] = rows_j[16 * n : 16 * n + 16, :].astype(bf16)
            feat_a[first_tile + n] = rows_a[16 * n : 16 * n + 16, :].astype(bf16)
        if own:
            for c in range(3):
                for s in range(3):
                    value = -2.0 * split[c][s]
                    for j in range(3 - s):
                        rows_i[pl.ds(16 * s + 3 * j + c, 8, stride=48), :] = value
            for s, value in enumerate(parts3(norm + 1.0)):
                rows_i[pl.ds(16 * s + 12, 8, stride=48), :] = value
            for n in range(8):
                feat_i[first_tile + n] = rows_i[48 * n : 48 * n + 48, :].astype(bf16)

    def own_block(b, carry):
        base = pl.multiple_of(b * 8, 8)
        here = pl.ds(base, 8)
        build(base, position[0, here, :], position[1, here, :], position[2, here, :], charges[here, :], True)
        return carry

    lax.fori_loop(0, TILES // 8, own_block, 0)

    def ghost_block(values, charge, offset):
        def block(b, carry):
            base = pl.multiple_of(b * 8, 8)
            here = pl.ds(base, 8)
            build(offset + base, values[0, here, :], values[1, here, :], values[2, here, :], charge[here, :], False)
            return carry

        return block

    for copy in ghost_copies:
        copy.wait()
    if last:
        charge_of = (lower_q, upper_q)
    else:
        charge_of = (lower.at[3], upper.at[3])
        kept_q[0][...] = lower[3]
        kept_q[1][...] = upper[3]
    lax.fori_loop(0, 16, ghost_block(lower, charge_of[0], TILES), 0)
    lax.fori_loop(0, 16, ghost_block(upper, charge_of[1], TILES + 128), 0)

    def contract(a, b, left, right):
        return lax.dot_general(a, b, (((left,), (right,)), ((), ())), preferred_element_type=f32)

    def listed(tile):
        tile = jnp.minimum(tile, TILES - 1)
        return tile, pairs[2 * tile], pairs[2 * tile + 1]

    def spread_of(tile):
        tile, one, two = listed(tile)
        near = jnp.concatenate([feat_j[one], feat_j[two]], axis=1)
        return contract(jnp.concatenate([near] * 3, axis=0), feat_i[tile], 0, 0)

    def force_of(tile, spread):
        tile, one, two = listed(tile)
        weight = pl.reciprocal(spread * spread, approx=True)
        high = weight.astype(bf16)
        low = (weight - high.astype(f32)).astype(bf16)
        near = jnp.concatenate([feat_a[one], feat_a[two]], axis=1)
        return contract(jnp.concatenate([near, near], axis=1), jnp.concatenate([high, low], axis=0), 1, 0)

    many = TILES_AT_ONCE
    for u in range(many):
        spread_a[u] = spread_of(u)

    def tiles(m, carry):
        for now, later, n in ((spread_a, spread_b, 2 * m), (spread_b, spread_a, 2 * m + 1)):
            done = []
            for u in range(many):
                later[u] = spread_of((n + 1) * many + u)
                done.append(force_of(n * many + u, now[u]))
            for u in range(many):
                sums[pl.ds(pl.multiple_of((n * many + u) * 16, 16), 16), :] = done[u]
        return carry

    lax.fori_loop(0, TILES // many // 2, tiles, 0)

    def total_of(terms, own, copies):
        for copy in copies:
            copy.wait()
        terms[me] = own[...]
        return jnp.sum(terms[...])

    progress = total_of(parts, partial, term_copies)
    pull = scalars[0] * (progress - scalars[1])
    for copy in velocity_copies:
        copy.wait()

    def velocity_at(c, here):
        own = velocity[c, here, :]
        if last:
            return own
        return pick(partner[0], window, own, velocity_below[c, here, :], velocity_above[c, here, :])

    def combine(b, part):
        base = pl.multiple_of(b * 8, 8)
        here = pl.ds(base, 8)
        total = []
        for k in range(4):
            value = sums[pl.ds(base * 16 + k, 8, stride=16), :]
            value = value + sums[pl.ds(base * 16 + 4 + k, 8, stride=16), :]
            value = value + sums[pl.ds(base * 16 + 8 + k, 8, stride=16), :]
            total.append(value)
        q = charges[here, :]
        weight = path_weight[here, :]
        rate = time_step * inv_mass[here, :]
        for c in range(3):
            old = position[c, here, :]
            force = q * (old * total[0] - total[c + 1])
            if c == 2:
                force = force - pull * weight
            moved = velocity_at(c, here) + rate * force
            placed = old + time_step * moved
            new_velocity[c, here, :] = moved
            new_position[c, here, :] = placed
        return part + weight * placed

    ending = lax.fori_loop(0, TILES // 8, combine, jnp.zeros((8, LANES), f32))
    if last:
        partial_last = spread_a.at[0, pl.ds(0, 8), :]
        spread_a[0, pl.ds(0, 8), :] = ending
        final_copies = [
            send(partial_last, final.at[me], k, sent_last.at[k], got_last.at[k]) for k in range(1, count)
        ]
        off = total_of(final, partial_last, final_copies) - scalars[1]
        result[...] = jnp.full((8, LANES), 0.5 * scalars[0] * off * off, f32)
    else:
        result[...] = ending


def step(number, last, scalars, partner, pairs, ghosts, partial, position, velocity, charges, lower_q, upper_q, inv_mass, path_weight):
    count, windows = lax.axis_size("dom"), lax.axis_size("rep")
    comps, rows = ghosts.shape[:2]
    whole = jax.ShapeDtypeStruct((3, TILES, LANES), f32)
    side_q = jax.ShapeDtypeStruct((rows // 2, LANES), f32)
    kept = () if last else (side_q, side_q)
    carried = () if last else (
        pltpu.VMEM(velocity.shape, f32),
        pltpu.VMEM(velocity.shape, f32),
        pltpu.SemaphoreType.DMA((2,)),
        pltpu.SemaphoreType.DMA((2,)),
    )

    def kernel(*refs):
        step_kernel(count, windows, last, *refs)

    return pl.pallas_call(
        kernel,
        out_shape=(whole, whole, jax.ShapeDtypeStruct((8, LANES), f32)) + kept,
        in_specs=[SMEM] * 3 + [VMEM] * 9,
        out_specs=(VMEM,) * (3 + len(kept)),
        scratch_shapes=[
            pltpu.VMEM((8 * 16, LANES), f32),
            pltpu.VMEM((8 * 48, LANES), f32),
            pltpu.VMEM((8 * 16, LANES), f32),
            pltpu.VMEM((TILES + 256, 16, LANES), bf16),
            pltpu.VMEM((TILES, 48, LANES), bf16),
            pltpu.VMEM((TILES + 256, 16, LANES), bf16),
            pltpu.VMEM((TILES * 16, LANES), f32),
            pltpu.VMEM((TILES_AT_ONCE, 2 * LANES, LANES), f32),
            pltpu.VMEM((TILES_AT_ONCE, 2 * LANES, LANES), f32),
            pltpu.VMEM((comps, rows // 2, LANES), f32),
            pltpu.VMEM((comps, rows // 2, LANES), f32),
            pltpu.VMEM((count, 8, LANES), f32),
            pltpu.VMEM((count, 8, LANES), f32),
            pltpu.SemaphoreType.DMA((count + 1,)),
            pltpu.SemaphoreType.DMA((count + 1,)),
            pltpu.SemaphoreType.DMA((count,)),
            pltpu.SemaphoreType.DMA((count,)),
            *carried,
        ],
        compiler_params=pltpu.CompilerParams(
            vmem_limit_bytes=58 * 1024 * 1024, collective_id=number, has_side_effects=True
        ),
        name="step",
    )(scalars, partner, pairs, ghosts, partial, position, velocity, charges, lower_q, upper_q, inv_mass, path_weight)


def second_gather_kernel(cells, position, source, place, ghosts, listed):
    def read_row(c, r):
        return position[c, pl.ds(r, 1), :]

    gather_stages(3, read_row, source, place, cells, listed, ghosts)


def second_gather(position, source, place, cells):
    return pl.pallas_call(
        second_gather_kernel,
        out_shape=jax.ShapeDtypeStruct((3, GHOST_ROWS, LANES), f32),
        in_specs=[SMEM] + [VMEM] * 3,
        out_specs=VMEM,
        scratch_shapes=[pltpu.VMEM((3, GROUPS * 32, LANES), f32)],
        compiler_params=params(),
        name="second_gather",
    )(cells, position, source, place)


def body(positions, velocities, charges, inv_mass, path_weight, halo_index, tile_pairs, partner, bias_center, bias_spring):
    position = positions[0].reshape(3, TILES, LANES)
    velocity = velocities[0].reshape(3, TILES, LANES)
    charges = charges.reshape(TILES, LANES)
    inv_mass = inv_mass.reshape(TILES, LANES)
    path_weight = path_weight.reshape(TILES, LANES)
    pairs = tile_pairs.reshape(-1)
    halo = halo_index.reshape(GHOST_ROWS, LANES)
    scalars = jnp.stack([bias_spring[0], bias_center[0]])
    below, above, source, place, cells = start(position, halo, STEPS)
    position, ghosts, partial = first_gather(
        partner, position, below, above, charges, path_weight, source, place, cells
    )
    lower_q = upper_q = jnp.zeros((GHOST_ROWS // 2, LANES), f32)
    for step_index in range(STEPS):
        last = step_index == STEPS - 1
        position, velocity, partial, *kept_q = step(
            step_index, last, scalars, partner, pairs, ghosts, partial, position, velocity,
            charges, lower_q, upper_q, inv_mass, path_weight,
        )
        if not last:
            lower_q, upper_q = kept_q
            ghosts = second_gather(position, source, place, cells)
    energy = partial[0, :1]
    atoms = TILES * LANES
    return position.reshape(1, 3, atoms), velocity.reshape(1, 3, atoms), energy


def solution(mesh):
    in_specs = (
        P("rep", None, "dom"),
        P("rep", None, "dom"),
        P("dom"),
        P("dom"),
        P("dom"),
        P(None, "dom"),
        P("dom", None),
        P("rep"),
        P("rep"),
        P("rep"),
    )
    out_specs = (P("rep", None, "dom"), P("rep", None, "dom"), P("rep"))
    return jax.shard_map(body, mesh=mesh, in_specs=in_specs, out_specs=out_specs, check_vma=False)
```

```python
import jax
import jax.numpy as jnp
from jax import lax
from jax.experimental import pallas as pl
from jax.experimental.pallas import tpu as pltpu
from jax.sharding import PartitionSpec as P

LANES = 128
STEPS = 2
TILES = 512
GHOST_ROWS = 256
GROUPS = 16
GROUP_ROWS = 32
CELLS = 32
CAPACITY = 4096
TILES_AT_ONCE = 16
time_step = 0.1
f32 = jnp.float32
bf16 = jnp.bfloat16
VMEM = pl.BlockSpec(memory_space=pltpu.VMEM)
SMEM = pl.BlockSpec(memory_space=pltpu.SMEM)


def params():
    return pltpu.CompilerParams(vmem_limit_bytes=58 * 1024 * 1024)


def plan_kernel(halo, charges, source, place, cells, ghost_q, counts, listed, raw, arrived):
    shape = (GHOST_ROWS, LANES)
    row = lax.broadcasted_iota(jnp.int32, shape, 0)
    lane = lax.broadcasted_iota(jnp.int32, shape, 1)
    wide = (LANES, 2 * LANES)
    across = lax.broadcasted_iota(jnp.int32, wide, 1)
    ahead_lane = (lax.broadcasted_iota(jnp.int32, wide, 0) < across) | (across >= LANES)
    ahead_lane = jnp.where(ahead_lane, 1.0, 0.0).astype(bf16)
    square = (GHOST_ROWS, GHOST_ROWS)
    ahead_row = lax.broadcasted_iota(jnp.int32, square, 1) < lax.broadcasted_iota(jnp.int32, square, 0)
    ahead_row = jnp.where(ahead_row, 1.0, 0.0).astype(bf16)
    place[...] = jnp.zeros(shape, jnp.int32)

    def one_group(group, carry):
        index = halo[...]
        member = (index >> 12) == group
        flag = jnp.where(member, 1.0, 0.0).astype(bf16)
        within = jnp.dot(flag, ahead_lane, preferred_element_type=f32)
        in_row = within[:, LANES:]
        earlier = jnp.dot(ahead_row, in_row.astype(bf16), preferred_element_type=f32)
        rank = (within[:, :LANES] + earlier).astype(jnp.int32)
        place[...] = jnp.where(member, rank + group * CAPACITY, place[...])
        marks = jnp.where(lane * 8 == row, earlier, 0.0)
        marks = marks + jnp.where((lane == CELLS) & (row == GHOST_ROWS - 1), earlier + in_row, 0.0)
        marks = jnp.sum(marks.reshape(GHOST_ROWS // 8, 8, LANES), axis=0)
        cells[pl.ds(pl.multiple_of(group * 8, 8), 8), :] = jnp.broadcast_to(
            jnp.sum(marks, axis=0, keepdims=True), (8, LANES)
        ).astype(jnp.int32)
        shift = row * LANES + lane - rank
        items = jnp.where(member, (1 << 28) | (shift << 12) | (index & 4095), 0)
        for bit in range(15):
            step_by = 1 << bit
            if step_by < LANES:
                following = pltpu.roll(items, items.shape[0] - 1, 0)
                mixed = jnp.where(lane < step_by, following, items)
                moved = pltpu.roll(mixed, LANES - step_by, 1)
                held = items
            else:
                rows = step_by // LANES
                if rows < 32:
                    if rows < 8:
                        moved = pltpu.roll(items, items.shape[0] - rows, 0)
                    else:
                        moved = jnp.concatenate([items[rows:], items[:rows]], axis=0)
                    held = items
                else:
                    blocks = items.reshape(items.shape[0] // 64, 2, 32, LANES)
                    held = blocks[:, 0].reshape(-1, LANES)
                    moved = blocks[:, 1].reshape(-1, LANES)
            mask = 1 << (12 + bit)
            items = jnp.where((moved & mask) != 0, moved, jnp.where((held & mask) != 0, 0, held))
        source[pl.ds(pl.multiple_of(group * 32, 32), 32), :] = items & 4095
        return carry

    lax.fori_loop(0, GROUPS, one_group, 0)
    copy = pltpu.make_async_copy(cells, counts, arrived)
    copy.start()
    copy.wait()

    def read_rows(c, rows):
        return charges[rows, :]

    gather_stages(1, read_rows, source, place, counts, listed, raw)
    unmix(1, raw, lambda c, rows, value: ghost_q.__setitem__((rows, slice(None)), value))


def plan(halo, charges):
    table = (GROUPS * 8, LANES)
    return pl.pallas_call(
        plan_kernel,
        out_shape=(
            jax.ShapeDtypeStruct((GROUPS * 32, LANES), jnp.int32),
            jax.ShapeDtypeStruct((GHOST_ROWS, LANES), jnp.int32),
            jax.ShapeDtypeStruct(table, jnp.int32),
            jax.ShapeDtypeStruct((GHOST_ROWS, LANES), f32),
        ),
        in_specs=[VMEM] * 2,
        out_specs=(VMEM,) * 4,
        scratch_shapes=[
            pltpu.SMEM(table, jnp.int32),
            pltpu.VMEM((1, GROUPS * 32, LANES), f32),
            pltpu.VMEM((1, GHOST_ROWS, LANES), f32),
            pltpu.SemaphoreType.DMA,
        ],
        compiler_params=params(),
        name="plan",
    )(halo, charges)


def unmix(comps, raw, store):
    for c in range(comps):
        for side in range(2):
            for b in range(GHOST_ROWS // 16):
                store(c, pl.ds(side * (GHOST_ROWS // 2) + b * 8, 8), raw[c, pl.ds(b * 16 + side, 8, stride=2), :])


def gather_stages(comps, read_rows, source, place, cells, listed, out):
    zeros = (jnp.zeros((8, LANES), f32),) * comps

    for half in range(GROUPS // 8):
        first = half * 8 * GROUP_ROWS
        most = cells[half * 64, CELLS]
        for k in range(1, 8):
            most = jnp.maximum(most, cells[half * 64 + k * 8, CELLS])

        def list_rows(pair, carry, first=first):
            spots = [pl.ds(first + 2 * pair + k, 8, stride=32) for k in range(2)]
            src = [source[spot, :] for spot in spots]
            lane = [item & 127 for item in src]
            row = [item >> 7 for item in src]
            accs = [list(zeros), list(zeros)]
            for u in range(GROUP_ROWS):
                mine = [item == u for item in row]
                for c in range(comps):
                    lines = read_rows(c, pl.ds(first + u, 8, stride=GROUP_ROWS))
                    for k in range(2):
                        accs[k][c] = jnp.where(mine[k], jnp.take_along_axis(lines, lane[k], axis=1), accs[k][c])
            for k in range(2):
                for c in range(comps):
                    listed[c, spots[k], :] = accs[k][c]
            return carry

        lax.fori_loop(0, (most + 255) >> 8, list_rows, 0)

    def slot_block(t, carry):
        here = pl.ds(pl.multiple_of(t * 8, 8), 8)
        at = place[here, :]
        lane = at & 127
        row = at >> 7

        def visit(r, accs):
            mine = row == r
            return tuple(
                jnp.where(
                    mine,
                    jnp.take_along_axis(jnp.broadcast_to(listed[c, pl.ds(r, 1), :], (8, LANES)), lane, axis=1),
                    accs[c],
                )
                for c in range(comps)
            )

        def rows_of(g):
            begin, end = cells[g * 8, t], cells[g * 8, t + 1]
            return g * 32 + jnp.minimum(begin >> 7, 31), g * 32 + (jnp.maximum(end - 1, begin) >> 7)

        accs = zeros
        widest = 0
        for g in range(GROUPS):
            first, last = rows_of(g)
            last = jnp.minimum(last, g * 32 + 31)
            accs = visit(first, accs)
            accs = visit(last, accs)
            widest = jnp.maximum(widest, last - first)
        for c in range(comps):
            out[c, here, :] = accs[c]

        @pl.when(widest > 1)
        def _():
            def rest(g, accs):
                first, last = rows_of(g)
                return lax.fori_loop(first, jnp.minimum(last, g * 32 + 31) + 1, visit, accs)

            more = lax.fori_loop(0, GROUPS, rest, tuple(out[c, here, :] for c in range(comps)))
            for c in range(comps):
                out[c, here, :] = more[c]

        return carry

    lax.fori_loop(0, GHOST_ROWS // 8, slot_block, 0)


def pick(partner, window, own, below, above):
    wanted = jnp.full(own.shape, partner, jnp.int32)
    return jnp.where(wanted == window - 1, below, jnp.where(wanted == window + 1, above, own))


def first_gather_kernel(
    partner, cells, own, below, above, ghost_q, path_weight, source, place, position, ghosts, partial, listed, raw
):
    window = lax.axis_index("rep")
    for c in range(3):
        position[c] = pick(partner[0], window, own[c], below[c], above[c])
    partial[...] = jnp.sum((path_weight[...] * position[2]).reshape(64, 8, LANES), axis=0)
    ghosts[3] = ghost_q[...]
    gather_positions(position, source, place, cells, ghosts, listed, raw)


def gather_positions(position, source, place, cells, ghosts, listed, raw):
    def read_rows(c, rows):
        return position[c, rows, :]

    def store(c, rows, value):
        ghosts[c, rows, :] = value

    gather_stages(3, read_rows, source, place, cells, listed, raw)
    unmix(3, raw, store)


GATHER_SCRATCH = [pltpu.VMEM((3, GROUPS * 32, LANES), f32), pltpu.VMEM((3, GHOST_ROWS, LANES), f32)]


def first_gather(partner, cells, own, below, above, ghost_q, path_weight, source, place):
    return pl.pallas_call(
        first_gather_kernel,
        out_shape=(
            jax.ShapeDtypeStruct((3, TILES, LANES), f32),
            jax.ShapeDtypeStruct((4, GHOST_ROWS, LANES), f32),
            jax.ShapeDtypeStruct((8, LANES), f32),
        ),
        in_specs=[SMEM] * 2 + [VMEM] * 7,
        out_specs=(VMEM,) * 3,
        scratch_shapes=GATHER_SCRATCH,
        compiler_params=params(),
        name="first_gather",
    )(partner, cells, own, below, above, ghost_q, path_weight, source, place)


def parts3(value):
    high = value.astype(bf16).astype(f32)
    rest = value - high
    middle = rest.astype(bf16).astype(f32)
    return high, middle, rest - middle


def step_kernel(
    count, windows, last, spring, center, partner, pairs, ghosts, partial, position, velocity, charges, inv_mass,
    path_weight, *rest,
):
    if last:
        lower_q, upper_q, *rest = rest
    new_position, new_velocity, result, *rest = rest
    if last:
        kept_q = ()
    else:
        kept_q, rest = rest[:2], rest[2:]
        rest, velocity_below, velocity_above, sent_v, got_v = rest[:-4], *rest[-4:]
    (
        rows_j, rows_i, rows_a, feat_j, feat_i, feat_a, sums, spread_a, spread_b,
        lower, upper, parts, final, sent, got, sent_last, got_last,
    ) = rest
    me = lax.axis_index("dom")
    half = GHOST_ROWS // 2
    barrier = pltpu.get_barrier_semaphore()
    for k in range(1, count):
        pl.semaphore_signal(
            barrier, inc=1, device_id={"dom": lax.rem(me + k, count)}, device_id_type=pl.DeviceIdType.MESH
        )
    if last:
        pl.semaphore_wait(barrier, count - 1)
    else:
        window = lax.axis_index("rep")
        ahead, behind = lax.rem(window + 1, windows), lax.rem(window + windows - 1, windows)
        for other in (ahead, behind):
            pl.semaphore_signal(barrier, inc=1, device_id={"rep": other}, device_id_type=pl.DeviceIdType.MESH)
        pl.semaphore_wait(barrier, count + 1)

    def send(source, target, k, sent_now, got_now):
        copy = pltpu.make_async_remote_copy(
            src_ref=source,
            dst_ref=target,
            send_sem=sent_now,
            recv_sem=got_now,
            device_id={"dom": lax.rem(me + k, count)},
            device_id_type=pl.DeviceIdType.MESH,
        )
        copy.start()
        return copy

    ghost_copies = [
        send(ghosts.at[:, pl.ds(half, half)], lower, 1, sent.at[0], got.at[0]),
        send(ghosts.at[:, pl.ds(0, half)], upper, count - 1, sent.at[count], got.at[count]),
    ]
    term_copies = [send(partial, parts.at[me], k, sent.at[k], got.at[k]) for k in range(1, count)]
    velocity_copies = []
    if not last:
        for n, (other, target) in enumerate(((ahead, velocity_below), (behind, velocity_above))):
            copy = pltpu.make_async_remote_copy(
                src_ref=velocity,
                dst_ref=target,
                send_sem=sent_v.at[n],
                recv_sem=got_v.at[n],
                device_id={"rep": other},
                device_id_type=pl.DeviceIdType.MESH,
            )
            copy.start()
            velocity_copies.append(copy)

    zero8 = jnp.zeros((8, LANES), f32)
    one8 = jnp.ones((8, LANES), f32)
    for f in (13, 14, 15):
        rows_j[pl.ds(f, 8, stride=16), :] = zero8
    rows_j[pl.ds(12, 8, stride=16), :] = one8
    for f in (12, 13, 14, 15):
        rows_a[pl.ds(f, 8, stride=16), :] = zero8
    rows_i[...] = jnp.zeros_like(rows_i)
    for f in (9, 10, 11):
        rows_i[pl.ds(f, 8, stride=48), :] = one8

    def build(first_tile, x, y, z, q, own):
        norm = x * x + y * y + z * z
        split = [parts3(value) for value in (x, y, z)]
        for c in range(3):
            for s in range(3):
                rows_j[pl.ds(3 * s + c, 8, stride=16), :] = split[c][s]
        for s, value in enumerate(parts3(norm)):
            rows_j[pl.ds(9 + s, 8, stride=16), :] = value
        for k, value in enumerate((q, q * x, q * y, q * z)):
            for s, piece in enumerate(parts3(value)):
                rows_a[pl.ds(4 * s + k, 8, stride=16), :] = piece
        for n in range(8):
            feat_j[first_tile + n] = rows_j[16 * n : 16 * n + 16, :].astype(bf16)
            feat_a[first_tile + n] = rows_a[16 * n : 16 * n + 16, :].astype(bf16)
        if own:
            for c in range(3):
                for s in range(3):
                    value = -2.0 * split[c][s]
                    for j in range(3 - s):
                        rows_i[pl.ds(16 * s + 3 * j + c, 8, stride=48), :] = value
            for s, value in enumerate(parts3(norm + 1.0)):
                rows_i[pl.ds(16 * s + 12, 8, stride=48), :] = value
            for n in range(8):
                feat_i[first_tile + n] = rows_i[48 * n : 48 * n + 48, :].astype(bf16)

    def own_block(b, carry):
        base = pl.multiple_of(b * 8, 8)
        here = pl.ds(base, 8)
        build(base, position[0, here, :], position[1, here, :], position[2, here, :], charges[here, :], True)
        return carry

    lax.fori_loop(0, TILES // 8, own_block, 0)

    def ghost_block(values, charge, offset):
        def block(b, carry):
            base = pl.multiple_of(b * 8, 8)
            here = pl.ds(base, 8)
            build(offset + base, values[0, here, :], values[1, here, :], values[2, here, :], charge[here, :], False)
            return carry

        return block

    for copy in ghost_copies:
        copy.wait()
    if last:
        charge_of = (lower_q, upper_q)
    else:
        charge_of = (lower.at[3], upper.at[3])
        kept_q[0][...] = lower[3]
        kept_q[1][...] = upper[3]
    lax.fori_loop(0, 16, ghost_block(lower, charge_of[0], TILES), 0)
    lax.fori_loop(0, 16, ghost_block(upper, charge_of[1], TILES + 128), 0)

    def contract(a, b, left, right):
        return lax.dot_general(a, b, (((left,), (right,)), ((), ())), preferred_element_type=f32)

    def listed(tile):
        tile = jnp.minimum(tile, TILES - 1)
        return tile, pairs[0, tile], pairs[1, tile]

    def spread_of(tile):
        tile, one, two = listed(tile)
        near = jnp.concatenate([feat_j[one], feat_j[two]], axis=1)
        return contract(jnp.concatenate([near] * 3, axis=0), feat_i[tile], 0, 0)

    def force_of(tile, spread):
        tile, one, two = listed(tile)
        weight = pl.reciprocal(spread * spread, approx=True)
        high = weight.astype(bf16)
        low = (weight - high.astype(f32)).astype(bf16)
        near = jnp.concatenate([feat_a[one], feat_a[two]], axis=1)
        return contract(jnp.concatenate([near, near], axis=1), jnp.concatenate([high, low], axis=0), 1, 0)

    many = TILES_AT_ONCE
    for u in range(many):
        spread_a[u] = spread_of(u)

    def tiles(m, carry):
        for now, later, n in ((spread_a, spread_b, 2 * m), (spread_b, spread_a, 2 * m + 1)):
            done = []
            for u in range(many):
                later[u] = spread_of((n + 1) * many + u)
                done.append(force_of(n * many + u, now[u]))
            for u in range(many):
                sums[pl.ds(pl.multiple_of((n * many + u) * 16, 16), 16), :] = done[u]
        return carry

    lax.fori_loop(0, TILES // many // 2, tiles, 0)

    def total_of(terms, own, copies):
        for copy in copies:
            copy.wait()
        terms[me] = own[...]
        return jnp.sum(terms[...])

    progress = total_of(parts, partial, term_copies)
    pull = spring[0] * (progress - center[0])
    for copy in velocity_copies:
        copy.wait()

    def velocity_at(c, here):
        own = velocity[c, here, :]
        if last:
            return own
        return pick(partner[0], window, own, velocity_below[c, here, :], velocity_above[c, here, :])

    def combine(b, part):
        base = pl.multiple_of(b * 8, 8)
        here = pl.ds(base, 8)
        total = []
        for k in range(4):
            value = sums[pl.ds(base * 16 + k, 8, stride=16), :]
            value = value + sums[pl.ds(base * 16 + 4 + k, 8, stride=16), :]
            value = value + sums[pl.ds(base * 16 + 8 + k, 8, stride=16), :]
            total.append(value)
        q = charges[here, :]
        weight = path_weight[here, :]
        rate = time_step * inv_mass[here, :]
        for c in range(3):
            old = position[c, here, :]
            force = q * (old * total[0] - total[c + 1])
            if c == 2:
                force = force - pull * weight
            moved = velocity_at(c, here) + rate * force
            placed = old + time_step * moved
            new_velocity[c, here, :] = moved
            new_position[c, here, :] = placed
        return part + weight * placed

    ending = lax.fori_loop(0, TILES // 8, combine, jnp.zeros((8, LANES), f32))
    if last:
        partial_last = spread_a.at[0, pl.ds(0, 8), :]
        spread_a[0, pl.ds(0, 8), :] = ending
        final_copies = [
            send(partial_last, final.at[me], k, sent_last.at[k], got_last.at[k]) for k in range(1, count)
        ]
        off = total_of(final, partial_last, final_copies) - center[0]
        result[0] = 0.5 * spring[0] * off * off
    else:
        result[...] = ending


def step(
    number, last, spring, center, partner, pairs, ghosts, partial, position, velocity, charges, inv_mass, path_weight, *kept_q
):
    count, windows = lax.axis_size("dom"), lax.axis_size("rep")
    comps, rows = ghosts.shape[:2]
    whole = jax.ShapeDtypeStruct((3, TILES, LANES), f32)
    side_q = jax.ShapeDtypeStruct((rows // 2, LANES), f32)
    kept = () if last else (side_q, side_q)
    carried = () if last else (
        pltpu.VMEM(velocity.shape, f32),
        pltpu.VMEM(velocity.shape, f32),
        pltpu.SemaphoreType.DMA((2,)),
        pltpu.SemaphoreType.DMA((2,)),
    )

    def kernel(*refs):
        step_kernel(count, windows, last, *refs)

    return pl.pallas_call(
        kernel,
        out_shape=(whole, whole, jax.ShapeDtypeStruct((1,) if last else (8, LANES), f32)) + kept,
        in_specs=[SMEM] * 4 + [VMEM] * (7 + len(kept_q)),
        out_specs=(VMEM, VMEM, SMEM if last else VMEM) + (VMEM,) * len(kept),
        scratch_shapes=[
            pltpu.VMEM((8 * 16, LANES), f32),
            pltpu.VMEM((8 * 48, LANES), f32),
            pltpu.VMEM((8 * 16, LANES), f32),
            pltpu.VMEM((TILES + 256, 16, LANES), bf16),
            pltpu.VMEM((TILES, 48, LANES), bf16),
            pltpu.VMEM((TILES + 256, 16, LANES), bf16),
            pltpu.VMEM((TILES * 16, LANES), f32),
            pltpu.VMEM((TILES_AT_ONCE, 2 * LANES, LANES), f32),
            pltpu.VMEM((TILES_AT_ONCE, 2 * LANES, LANES), f32),
            pltpu.VMEM((comps, rows // 2, LANES), f32),
            pltpu.VMEM((comps, rows // 2, LANES), f32),
            pltpu.VMEM((count, 8, LANES), f32),
            pltpu.VMEM((count, 8, LANES), f32),
            pltpu.SemaphoreType.DMA((count + 1,)),
            pltpu.SemaphoreType.DMA((count + 1,)),
            pltpu.SemaphoreType.DMA((count,)),
            pltpu.SemaphoreType.DMA((count,)),
            *carried,
        ],
        compiler_params=pltpu.CompilerParams(
            vmem_limit_bytes=58 * 1024 * 1024, collective_id=number, has_side_effects=True
        ),
        name="step",
    )(
        spring, center, partner, pairs, ghosts, partial, position, velocity, charges, inv_mass, path_weight, *kept_q
    )


def second_gather_kernel(cells, *refs):
    position, source, place, ghosts, listed, raw = refs
    gather_positions(position, source, place, cells, ghosts, listed, raw)


def second_gather(cells, position, source, place):
    return pl.pallas_call(
        second_gather_kernel,
        out_shape=jax.ShapeDtypeStruct((3, GHOST_ROWS, LANES), f32),
        in_specs=[SMEM] + [VMEM] * 3,
        out_specs=VMEM,
        scratch_shapes=GATHER_SCRATCH,
        compiler_params=params(),
        name="second_gather",
    )(cells, position, source, place)


def shifted(shard, axis, by):
    count = lax.axis_size(axis)
    pairs = [(i, i + by) for i in range(count) if 0 <= i + by < count]
    return lax.ppermute(shard, axis, pairs)


def body(positions, velocities, charges, inv_mass, path_weight, halo_index, tile_pairs, partner, bias_center, bias_spring):
    position = positions[0].reshape(3, TILES, LANES)
    velocity = velocities[0].reshape(3, TILES, LANES)
    charges = charges.reshape(TILES, LANES)
    inv_mass = inv_mass.reshape(TILES, LANES)
    path_weight = path_weight.reshape(TILES, LANES)
    pairs = tile_pairs.T
    halo = halo_index.reshape(2, GHOST_ROWS // 2, LANES).transpose(1, 0, 2).reshape(GHOST_ROWS, LANES)
    below = shifted(position, "rep", 1)
    above = shifted(position, "rep", -1)
    source, place, cells, ghost_q = plan(halo, charges)
    position, ghosts, partial = first_gather(
        partner, cells, position, below, above, ghost_q, path_weight, source, place
    )
    kept_q = ()
    for step_index in range(STEPS):
        last = step_index == STEPS - 1
        position, velocity, partial, *kept_q = step(
            step_index, last, bias_spring, bias_center, partner, pairs, ghosts, partial, position, velocity,
            charges, inv_mass, path_weight, *kept_q,
        )
        if not last:
            ghosts = second_gather(cells, position, source, place)
    atoms = TILES * LANES
    return position.reshape(1, 3, atoms), velocity.reshape(1, 3, atoms), partial


def solution(mesh):
    in_specs = (
        P("rep", None, "dom"),
        P("rep", None, "dom"),
        P("dom"),
        P("dom"),
        P("dom"),
        P(None, "dom"),
        P("dom", None),
        P("rep"),
        P("rep"),
        P("rep"),
    )
    out_specs = (P("rep", None, "dom"), P("rep", None, "dom"), P("rep"))
    return jax.shard_map(body, mesh=mesh, in_specs=in_specs, out_specs=out_specs, check_vma=False)
```

```python
import jax
import jax.numpy as jnp
from jax import lax
from jax.experimental import pallas as pl
from jax.experimental.pallas import tpu as pltpu
from jax.sharding import PartitionSpec as P

LANES = 128
STEPS = 2
TILES = 512
GHOST_ROWS = 256
GROUPS = 16
GROUP_ROWS = 32
CELLS = 32
CAPACITY = 4096
TILES_AT_ONCE = 16
time_step = 0.1
f32 = jnp.float32
bf16 = jnp.bfloat16
VMEM = pl.BlockSpec(memory_space=pltpu.VMEM)
SMEM = pl.BlockSpec(memory_space=pltpu.SMEM)


def params():
    return pltpu.CompilerParams(vmem_limit_bytes=58 * 1024 * 1024)


def plan_kernel(halo, source, place, cells):
    shape = (GHOST_ROWS, LANES)
    row = lax.broadcasted_iota(jnp.int32, shape, 0)
    lane = lax.broadcasted_iota(jnp.int32, shape, 1)
    wide = (LANES, 2 * LANES)
    across = lax.broadcasted_iota(jnp.int32, wide, 1)
    ahead_lane = (lax.broadcasted_iota(jnp.int32, wide, 0) < across) | (across >= LANES)
    ahead_lane = jnp.where(ahead_lane, 1.0, 0.0).astype(bf16)
    square = (GHOST_ROWS, GHOST_ROWS)
    ahead_row = lax.broadcasted_iota(jnp.int32, square, 1) < lax.broadcasted_iota(jnp.int32, square, 0)
    ahead_row = jnp.where(ahead_row, 1.0, 0.0).astype(bf16)
    place[...] = jnp.zeros(shape, jnp.int32)

    def one_group(group, carry):
        index = halo[...]
        member = (index >> 12) == group
        flag = jnp.where(member, 1.0, 0.0).astype(bf16)
        within = jnp.dot(flag, ahead_lane, preferred_element_type=f32)
        in_row = within[:, LANES:]
        earlier = jnp.dot(ahead_row, in_row.astype(bf16), preferred_element_type=f32)
        rank = (within[:, :LANES] + earlier).astype(jnp.int32)
        place[...] = jnp.where(member, rank + group * CAPACITY, place[...])
        marks = jnp.where(lane * 8 == row, earlier, 0.0)
        marks = marks + jnp.where((lane == CELLS) & (row == GHOST_ROWS - 1), earlier + in_row, 0.0)
        marks = jnp.sum(marks.reshape(GHOST_ROWS // 8, 8, LANES), axis=0)
        cells[pl.ds(pl.multiple_of(group * 8, 8), 8), :] = jnp.broadcast_to(
            jnp.sum(marks, axis=0, keepdims=True), (8, LANES)
        ).astype(jnp.int32)
        shift = row * LANES + lane - rank
        items = jnp.where(member, (1 << 28) | (shift << 12) | (index & 4095), 0)
        for bit in range(15):
            step_by = 1 << bit
            if step_by < LANES:
                following = pltpu.roll(items, items.shape[0] - 1, 0)
                mixed = jnp.where(lane < step_by, following, items)
                moved = pltpu.roll(mixed, LANES - step_by, 1)
                held = items
            else:
                rows = step_by // LANES
                if rows < 32:
                    if rows < 8:
                        moved = pltpu.roll(items, items.shape[0] - rows, 0)
                    else:
                        moved = jnp.concatenate([items[rows:], items[:rows]], axis=0)
                    held = items
                else:
                    blocks = items.reshape(items.shape[0] // 64, 2, 32, LANES)
                    held = blocks[:, 0].reshape(-1, LANES)
                    moved = blocks[:, 1].reshape(-1, LANES)
            mask = 1 << (12 + bit)
            items = jnp.where((moved & mask) != 0, moved, jnp.where((held & mask) != 0, 0, held))
        source[pl.ds(pl.multiple_of(group * 32, 32), 32), :] = items & 4095
        return carry

    lax.fori_loop(0, GROUPS, one_group, 0)


def plan(halo):
    return pl.pallas_call(
        plan_kernel,
        out_shape=(
            jax.ShapeDtypeStruct((GROUPS * 32, LANES), jnp.int32),
            jax.ShapeDtypeStruct((GHOST_ROWS, LANES), jnp.int32),
            jax.ShapeDtypeStruct((GROUPS * 8, LANES), jnp.int32),
        ),
        in_specs=[VMEM],
        out_specs=(VMEM,) * 3,
        compiler_params=params(),
        name="plan",
    )(halo)


def unmix(comps, raw, store):
    for c in range(comps):
        for side in range(2):
            for b in range(GHOST_ROWS // 16):
                store(c, pl.ds(side * (GHOST_ROWS // 2) + b * 8, 8), raw[c, pl.ds(b * 16 + side, 8, stride=2), :])


def gather_stages(comps, read_rows, source, place, cells, listed, out):
    zeros = (jnp.zeros((8, LANES), f32),) * comps

    for half in range(GROUPS // 8):
        first = half * 8 * GROUP_ROWS
        most = cells[half * 64, CELLS]
        for k in range(1, 8):
            most = jnp.maximum(most, cells[half * 64 + k * 8, CELLS])

        def list_rows(pair, carry, first=first):
            spots = [pl.ds(first + 2 * pair + k, 8, stride=32) for k in range(2)]
            src = [source[spot, :] for spot in spots]
            lane = [item & 127 for item in src]
            row = [item >> 7 for item in src]
            accs = [list(zeros), list(zeros)]
            for u in range(GROUP_ROWS):
                mine = [item == u for item in row]
                for c in range(comps):
                    lines = read_rows(c, pl.ds(first + u, 8, stride=GROUP_ROWS))
                    for k in range(2):
                        accs[k][c] = jnp.where(mine[k], jnp.take_along_axis(lines, lane[k], axis=1), accs[k][c])
            for k in range(2):
                for c in range(comps):
                    listed[c, spots[k], :] = accs[k][c]
            return carry

        lax.fori_loop(0, (most + 255) >> 8, list_rows, 0)

    def slot_block(t, carry):
        here = pl.ds(pl.multiple_of(t * 8, 8), 8)
        at = place[here, :]
        lane = at & 127
        row = at >> 7

        def visit(r, accs):
            mine = row == r
            return tuple(
                jnp.where(
                    mine,
                    jnp.take_along_axis(jnp.broadcast_to(listed[c, pl.ds(r, 1), :], (8, LANES)), lane, axis=1),
                    accs[c],
                )
                for c in range(comps)
            )

        def rows_of(g):
            begin, end = cells[g * 8, t], cells[g * 8, t + 1]
            return g * 32 + jnp.minimum(begin >> 7, 31), g * 32 + (jnp.maximum(end - 1, begin) >> 7)

        accs = zeros
        widest = 0
        for g in range(GROUPS):
            first, last = rows_of(g)
            last = jnp.minimum(last, g * 32 + 31)
            accs = visit(first, accs)
            accs = visit(last, accs)
            widest = jnp.maximum(widest, last - first)
        for c in range(comps):
            out[c, here, :] = accs[c]

        @pl.when(widest > 1)
        def _():
            def rest(g, accs):
                first, last = rows_of(g)
                return lax.fori_loop(first, jnp.minimum(last, g * 32 + 31) + 1, visit, accs)

            more = lax.fori_loop(0, GROUPS, rest, tuple(out[c, here, :] for c in range(comps)))
            for c in range(comps):
                out[c, here, :] = more[c]

        return carry

    lax.fori_loop(0, GHOST_ROWS // 8, slot_block, 0)


def pick(partner, window, own, below, above):
    wanted = jnp.full(own.shape, partner, jnp.int32)
    return jnp.where(wanted == window - 1, below, jnp.where(wanted == window + 1, above, own))


def first_gather_kernel(
    partner, cells, own, below, above, charges, path_weight, source, place, position, ghosts, partial, listed, raw
):
    window = lax.axis_index("rep")
    for c in range(3):
        position[c] = pick(partner[0], window, own[c], below[c], above[c])
    partial[...] = jnp.sum((path_weight[...] * position[2]).reshape(64, 8, LANES), axis=0)
    gather_positions(4, (position, charges), source, place, cells, ghosts, listed, raw)


def gather_positions(comps, tables, source, place, cells, ghosts, listed, raw):
    def read_rows(c, rows):
        return tables[1][rows, :] if c == 3 else tables[0][c, rows, :]

    def store(c, rows, value):
        ghosts[c, rows, :] = value

    gather_stages(comps, read_rows, source, place, cells, listed, raw)
    unmix(comps, raw, store)


def gather_scratch(comps):
    return [pltpu.VMEM((comps, GROUPS * 32, LANES), f32), pltpu.VMEM((comps, GHOST_ROWS, LANES), f32)]


def first_gather(partner, cells, own, below, above, charges, path_weight, source, place):
    return pl.pallas_call(
        first_gather_kernel,
        out_shape=(
            jax.ShapeDtypeStruct((3, TILES, LANES), f32),
            jax.ShapeDtypeStruct((4, GHOST_ROWS, LANES), f32),
            jax.ShapeDtypeStruct((8, LANES), f32),
        ),
        in_specs=[SMEM] * 2 + [VMEM] * 7,
        out_specs=(VMEM,) * 3,
        scratch_shapes=gather_scratch(4),
        compiler_params=params(),
        name="first_gather",
    )(partner, cells, own, below, above, charges, path_weight, source, place)


def parts3(value):
    high = value.astype(bf16).astype(f32)
    rest = value - high
    middle = rest.astype(bf16).astype(f32)
    return high, middle, rest - middle


def step_kernel(
    count, windows, last, spring, center, partner, pairs, ghosts, partial, position, velocity, charges, inv_mass,
    path_weight, *rest,
):
    if last:
        lower_q, upper_q, *rest = rest
    new_position, new_velocity, result, *rest = rest
    if last:
        kept_q = ()
    else:
        kept_q, rest = rest[:2], rest[2:]
        rest, velocity_below, velocity_above, sent_v, got_v = rest[:-4], *rest[-4:]
    (
        rows_j, rows_i, rows_a, feat_j, feat_i, feat_a, sums, spread_a, spread_b,
        lower, upper, parts, final, sent, got, sent_last, got_last,
    ) = rest
    me = lax.axis_index("dom")
    half = GHOST_ROWS // 2
    barrier = pltpu.get_barrier_semaphore()
    for k in range(1, count):
        pl.semaphore_signal(
            barrier, inc=1, device_id={"dom": lax.rem(me + k, count)}, device_id_type=pl.DeviceIdType.MESH
        )
    if not last:
        window = lax.axis_index("rep")
        ahead, behind = lax.rem(window + 1, windows), lax.rem(window + windows - 1, windows)
        for other in (ahead, behind):
            pl.semaphore_signal(barrier, inc=1, device_id={"rep": other}, device_id_type=pl.DeviceIdType.MESH)

    zero8 = jnp.zeros((8, LANES), f32)
    one8 = jnp.ones((8, LANES), f32)
    for f in (13, 14, 15):
        rows_j[pl.ds(f, 8, stride=16), :] = zero8
    rows_j[pl.ds(12, 8, stride=16), :] = one8
    for f in (12, 13, 14, 15):
        rows_a[pl.ds(f, 8, stride=16), :] = zero8
    rows_i[...] = jnp.zeros_like(rows_i)
    for f in (9, 10, 11):
        rows_i[pl.ds(f, 8, stride=48), :] = one8

    def build(first_tile, x, y, z, q, own):
        norm = x * x + y * y + z * z
        split = [parts3(value) for value in (x, y, z)]
        for c in range(3):
            for s in range(3):
                rows_j[pl.ds(3 * s + c, 8, stride=16), :] = split[c][s]
        for s, value in enumerate(parts3(norm)):
            rows_j[pl.ds(9 + s, 8, stride=16), :] = value
        for k, value in enumerate((q, q * x, q * y, q * z)):
            for s, piece in enumerate(parts3(value)):
                rows_a[pl.ds(4 * s + k, 8, stride=16), :] = piece
        for n in range(8):
            feat_j[first_tile + n] = rows_j[16 * n : 16 * n + 16, :].astype(bf16)
            feat_a[first_tile + n] = rows_a[16 * n : 16 * n + 16, :].astype(bf16)
        if own:
            for c in range(3):
                for s in range(3):
                    value = -2.0 * split[c][s]
                    for j in range(3 - s):
                        rows_i[pl.ds(16 * s + 3 * j + c, 8, stride=48), :] = value
            for s, value in enumerate(parts3(norm + 1.0)):
                rows_i[pl.ds(16 * s + 12, 8, stride=48), :] = value
            for n in range(8):
                feat_i[first_tile + n] = rows_i[48 * n : 48 * n + 48, :].astype(bf16)

    def own_block(b, carry):
        base = pl.multiple_of(b * 8, 8)
        here = pl.ds(base, 8)
        build(base, position[0, here, :], position[1, here, :], position[2, here, :], charges[here, :], True)
        return carry

    lax.fori_loop(0, TILES // 16, own_block, 0)
    pl.semaphore_wait(barrier, count - 1 if last else count + 1)

    def send(source, target, k, sent_now, got_now):
        copy = pltpu.make_async_remote_copy(
            src_ref=source,
            dst_ref=target,
            send_sem=sent_now,
            recv_sem=got_now,
            device_id={"dom": lax.rem(me + k, count)},
            device_id_type=pl.DeviceIdType.MESH,
        )
        copy.start()
        return copy

    ghost_copies = [
        send(ghosts.at[:, pl.ds(half, half)], lower, 1, sent.at[0], got.at[0]),
        send(ghosts.at[:, pl.ds(0, half)], upper, count - 1, sent.at[count], got.at[count]),
    ]
    term_copies = [send(partial, parts.at[me], k, sent.at[k], got.at[k]) for k in range(1, count)]
    velocity_copies = []
    if not last:
        for n, (other, target) in enumerate(((ahead, velocity_below), (behind, velocity_above))):
            copy = pltpu.make_async_remote_copy(
                src_ref=velocity,
                dst_ref=target,
                send_sem=sent_v.at[n],
                recv_sem=got_v.at[n],
                device_id={"rep": other},
                device_id_type=pl.DeviceIdType.MESH,
            )
            copy.start()
            velocity_copies.append(copy)

    lax.fori_loop(TILES // 16, TILES // 8, own_block, 0)

    def ghost_block(values, charge, offset):
        def block(b, carry):
            base = pl.multiple_of(b * 8, 8)
            here = pl.ds(base, 8)
            build(offset + base, values[0, here, :], values[1, here, :], values[2, here, :], charge[here, :], False)
            return carry

        return block

    for copy in ghost_copies:
        copy.wait()
    if last:
        charge_of = (lower_q, upper_q)
    else:
        charge_of = (lower.at[3], upper.at[3])
        kept_q[0][...] = lower[3]
        kept_q[1][...] = upper[3]
    lax.fori_loop(0, 16, ghost_block(lower, charge_of[0], TILES), 0)
    lax.fori_loop(0, 16, ghost_block(upper, charge_of[1], TILES + 128), 0)

    def contract(a, b, left, right):
        return lax.dot_general(a, b, (((left,), (right,)), ((), ())), preferred_element_type=f32)

    def listed(tile):
        tile = jnp.minimum(tile, TILES - 1)
        return tile, pairs[0, tile], pairs[1, tile]

    def spread_of(tile):
        tile, one, two = listed(tile)
        near = jnp.concatenate([feat_j[one], feat_j[two]], axis=1)
        return contract(jnp.concatenate([near] * 3, axis=0), feat_i[tile], 0, 0)

    def force_of(tile, spread):
        tile, one, two = listed(tile)
        weight = pl.reciprocal(spread * spread, approx=True)
        high = weight.astype(bf16)
        low = (weight - high.astype(f32)).astype(bf16)
        near = jnp.concatenate([feat_a[one], feat_a[two]], axis=1)
        return contract(jnp.concatenate([near, near], axis=1), jnp.concatenate([high, low], axis=0), 1, 0)

    many = TILES_AT_ONCE
    for u in range(many):
        spread_a[u] = spread_of(u)

    def tiles(m, carry):
        for now, later, n in ((spread_a, spread_b, 2 * m), (spread_b, spread_a, 2 * m + 1)):
            done = []
            for u in range(many):
                later[u] = spread_of((n + 1) * many + u)
                done.append(force_of(n * many + u, now[u]))
            for u in range(many):
                sums[pl.ds(pl.multiple_of((n * many + u) * 16, 16), 16), :] = done[u]
        return carry

    lax.fori_loop(0, TILES // many // 2, tiles, 0)

    def total_of(terms, own, copies):
        for copy in copies:
            copy.wait()
        terms[me] = own[...]
        return jnp.sum(terms[...])

    progress = total_of(parts, partial, term_copies)
    pull = spring[0] * (progress - center[0])
    for copy in velocity_copies:
        copy.wait()

    def velocity_at(c, here):
        own = velocity[c, here, :]
        if last:
            return own
        return pick(partner[0], window, own, velocity_below[c, here, :], velocity_above[c, here, :])

    def combine(b, part):
        base = pl.multiple_of(b * 8, 8)
        here = pl.ds(base, 8)
        total = []
        for k in range(4):
            value = sums[pl.ds(base * 16 + k, 8, stride=16), :]
            value = value + sums[pl.ds(base * 16 + 4 + k, 8, stride=16), :]
            value = value + sums[pl.ds(base * 16 + 8 + k, 8, stride=16), :]
            total.append(value)
        q = charges[here, :]
        weight = path_weight[here, :]
        rate = time_step * inv_mass[here, :]
        for c in range(3):
            old = position[c, here, :]
            force = q * (old * total[0] - total[c + 1])
            if c == 2:
                force = force - pull * weight
            moved = velocity_at(c, here) + rate * force
            placed = old + time_step * moved
            new_velocity[c, here, :] = moved
            new_position[c, here, :] = placed
        return part + weight * placed

    ending = lax.fori_loop(0, TILES // 8, combine, jnp.zeros((8, LANES), f32))
    if last:
        partial_last = spread_a.at[0, pl.ds(0, 8), :]
        spread_a[0, pl.ds(0, 8), :] = ending
        final_copies = [
            send(partial_last, final.at[me], k, sent_last.at[k], got_last.at[k]) for k in range(1, count)
        ]
        off = total_of(final, partial_last, final_copies) - center[0]
        result[0] = 0.5 * spring[0] * off * off
    else:
        result[...] = ending


def step(
    number, last, spring, center, partner, pairs, ghosts, partial, position, velocity, charges, inv_mass, path_weight, *kept_q
):
    count, windows = lax.axis_size("dom"), lax.axis_size("rep")
    comps, rows = ghosts.shape[:2]
    whole = jax.ShapeDtypeStruct((3, TILES, LANES), f32)
    side_q = jax.ShapeDtypeStruct((rows // 2, LANES), f32)
    kept = () if last else (side_q, side_q)
    carried = () if last else (
        pltpu.VMEM(velocity.shape, f32),
        pltpu.VMEM(velocity.shape, f32),
        pltpu.SemaphoreType.DMA((2,)),
        pltpu.SemaphoreType.DMA((2,)),
    )

    def kernel(*refs):
        step_kernel(count, windows, last, *refs)

    return pl.pallas_call(
        kernel,
        out_shape=(whole, whole, jax.ShapeDtypeStruct((1,) if last else (8, LANES), f32)) + kept,
        in_specs=[SMEM] * 4 + [VMEM] * (7 + len(kept_q)),
        out_specs=(VMEM, VMEM, SMEM if last else VMEM) + (VMEM,) * len(kept),
        scratch_shapes=[
            pltpu.VMEM((8 * 16, LANES), f32),
            pltpu.VMEM((8 * 48, LANES), f32),
            pltpu.VMEM((8 * 16, LANES), f32),
            pltpu.VMEM((TILES + 256, 16, LANES), bf16),
            pltpu.VMEM((TILES, 48, LANES), bf16),
            pltpu.VMEM((TILES + 256, 16, LANES), bf16),
            pltpu.VMEM((TILES * 16, LANES), f32),
            pltpu.VMEM((TILES_AT_ONCE, 2 * LANES, LANES), f32),
            pltpu.VMEM((TILES_AT_ONCE, 2 * LANES, LANES), f32),
            pltpu.VMEM((comps, rows // 2, LANES), f32),
            pltpu.VMEM((comps, rows // 2, LANES), f32),
            pltpu.VMEM((count, 8, LANES), f32),
            pltpu.VMEM((count, 8, LANES), f32),
            pltpu.SemaphoreType.DMA((count + 1,)),
            pltpu.SemaphoreType.DMA((count + 1,)),
            pltpu.SemaphoreType.DMA((count,)),
            pltpu.SemaphoreType.DMA((count,)),
            *carried,
        ],
        compiler_params=pltpu.CompilerParams(
            vmem_limit_bytes=58 * 1024 * 1024, collective_id=number, has_side_effects=True
        ),
        name="step",
    )(
        spring, center, partner, pairs, ghosts, partial, position, velocity, charges, inv_mass, path_weight, *kept_q
    )


def second_gather_kernel(cells, *refs):
    position, source, place, ghosts, listed, raw = refs
    gather_positions(3, (position,), source, place, cells, ghosts, listed, raw)


def second_gather(cells, position, source, place):
    return pl.pallas_call(
        second_gather_kernel,
        out_shape=jax.ShapeDtypeStruct((3, GHOST_ROWS, LANES), f32),
        in_specs=[SMEM] + [VMEM] * 3,
        out_specs=VMEM,
        scratch_shapes=gather_scratch(3),
        compiler_params=params(),
        name="second_gather",
    )(cells, position, source, place)


def shifted(shard, axis, by):
    count = lax.axis_size(axis)
    pairs = [(i, i + by) for i in range(count) if 0 <= i + by < count]
    return lax.ppermute(shard, axis, pairs)


def body(positions, velocities, charges, inv_mass, path_weight, halo_index, tile_pairs, partner, bias_center, bias_spring):
    position = positions[0].reshape(3, TILES, LANES)
    velocity = velocities[0].reshape(3, TILES, LANES)
    charges = charges.reshape(TILES, LANES)
    inv_mass = inv_mass.reshape(TILES, LANES)
    path_weight = path_weight.reshape(TILES, LANES)
    pairs = tile_pairs.T
    halo = halo_index.reshape(2, GHOST_ROWS // 2, LANES).transpose(1, 0, 2).reshape(GHOST_ROWS, LANES)
    below = shifted(position, "rep", 1)
    above = shifted(position, "rep", -1)
    source, place, cells = plan(halo)
    position, ghosts, partial = first_gather(
        partner, cells, position, below, above, charges, path_weight, source, place
    )
    kept_q = ()
    for step_index in range(STEPS):
        last = step_index == STEPS - 1
        position, velocity, partial, *kept_q = step(
            step_index, last, bias_spring, bias_center, partner, pairs, ghosts, partial, position, velocity,
            charges, inv_mass, path_weight, *kept_q,
        )
        if not last:
            ghosts = second_gather(cells, position, source, place)
    atoms = TILES * LANES
    return position.reshape(1, 3, atoms), velocity.reshape(1, 3, atoms), partial


def solution(mesh):
    in_specs = (
        P("rep", None, "dom"),
        P("rep", None, "dom"),
        P("dom"),
        P("dom"),
        P("dom"),
        P(None, "dom"),
        P("dom", None),
        P("rep"),
        P("rep"),
        P("rep"),
    )
    out_specs = (P("rep", None, "dom"), P("rep", None, "dom"), P("rep"))
    return jax.shard_map(body, mesh=mesh, in_specs=in_specs, out_specs=out_specs, check_vma=False)
```

```python
import jax
import jax.numpy as jnp
from jax import lax
from jax.experimental import pallas as pl
from jax.experimental.pallas import tpu as pltpu
from jax.sharding import PartitionSpec as P

LANES = 128
STEPS = 2
TILES = 512
GHOST_ROWS = 256
GROUPS = 16
GROUP_ROWS = 32
CELLS = 32
CAPACITY = 4096
TILES_AT_ONCE = 16
time_step = 0.1
f32 = jnp.float32
bf16 = jnp.bfloat16
VMEM = pl.BlockSpec(memory_space=pltpu.VMEM)
SMEM = pl.BlockSpec(memory_space=pltpu.SMEM)


def params():
    return pltpu.CompilerParams(vmem_limit_bytes=58 * 1024 * 1024)


def plan_kernel(halo, source, place, cells, ranks, counts):
    shape = (GHOST_ROWS, LANES)
    row = lax.broadcasted_iota(jnp.int32, shape, 0)
    lane = lax.broadcasted_iota(jnp.int32, shape, 1)
    wide = (LANES, 2 * LANES)
    across = lax.broadcasted_iota(jnp.int32, wide, 1)
    ahead_lane = (lax.broadcasted_iota(jnp.int32, wide, 0) < across) | (across >= LANES)
    ahead_lane = jnp.where(ahead_lane, 1.0, 0.0).astype(bf16)
    square = (GHOST_ROWS, GHOST_ROWS)
    ahead_row = lax.broadcasted_iota(jnp.int32, square, 1) < lax.broadcasted_iota(jnp.int32, square, 0)
    ahead_row = jnp.where(ahead_row, 1.0, 0.0).astype(bf16)
    counts[...] = jnp.zeros(shape, f32)

    def count_group(group, carry):
        member = (halo[...] >> 12) == group
        within = jnp.dot(jnp.where(member, 1.0, 0.0).astype(bf16), ahead_lane, preferred_element_type=f32)
        ranks[...] = jnp.where(member, within[:, :LANES].astype(jnp.int32), ranks[...])
        counts[...] = jnp.where(lane == group, within[:, LANES:], counts[...])
        return carry

    lax.fori_loop(0, GROUPS, count_group, 0)
    earlier = jnp.dot(ahead_row, counts[...].astype(bf16), preferred_element_type=f32)
    total = (earlier[GHOST_ROWS - 1 :] + counts[GHOST_ROWS - 1 :, :]).astype(jnp.int32)
    earlier = earlier.astype(jnp.int32)
    for b in range(GHOST_ROWS // 8):
        here = slice(8 * b, 8 * b + 8)
        group_of = halo[here, :] >> 12
        rank = ranks[here, :] + jnp.take_along_axis(earlier[here], group_of, axis=1)
        ranks[here, :] = rank
        place[here, :] = rank + group_of * CAPACITY
        cells[b : b + 1, :] = earlier[8 * b : 8 * b + 1]
    cells[CELLS : CELLS + 8, :] = jnp.broadcast_to(total, (8, LANES))

    def one_group(group, carry):
        index = halo[...]
        member = (index >> 12) == group
        rank = ranks[...]
        shift = row * LANES + lane - rank
        items = jnp.where(member, (1 << 28) | (shift << 12) | (index & 4095), 0)
        for bit in range(15):
            step_by = 1 << bit
            if step_by < LANES:
                following = pltpu.roll(items, items.shape[0] - 1, 0)
                mixed = jnp.where(lane < step_by, following, items)
                moved = pltpu.roll(mixed, LANES - step_by, 1)
                held = items
            else:
                rows = step_by // LANES
                if rows < 32:
                    if rows < 8:
                        moved = pltpu.roll(items, items.shape[0] - rows, 0)
                    else:
                        moved = jnp.concatenate([items[rows:], items[:rows]], axis=0)
                    held = items
                else:
                    blocks = items.reshape(items.shape[0] // 64, 2, 32, LANES)
                    held = blocks[:, 0].reshape(-1, LANES)
                    moved = blocks[:, 1].reshape(-1, LANES)
            mask = 1 << (12 + bit)
            items = jnp.where((moved & mask) != 0, moved, jnp.where((held & mask) != 0, 0, held))
        source[pl.ds(pl.multiple_of(group * 32, 32), 32), :] = items & 4095
        return carry

    lax.fori_loop(0, GROUPS, one_group, 0)


def plan(halo):
    return pl.pallas_call(
        plan_kernel,
        out_shape=(
            jax.ShapeDtypeStruct((GROUPS * 32, LANES), jnp.int32),
            jax.ShapeDtypeStruct((GHOST_ROWS, LANES), jnp.int32),
            jax.ShapeDtypeStruct((CELLS + 8, LANES), jnp.int32),
        ),
        in_specs=[VMEM],
        out_specs=(VMEM,) * 3,
        scratch_shapes=[pltpu.VMEM((GHOST_ROWS, LANES), jnp.int32), pltpu.VMEM((GHOST_ROWS, LANES), f32)],
        compiler_params=params(),
        name="plan",
    )(halo)


def unmix(comps, raw, store):
    for c in range(comps):
        for side in range(2):
            for b in range(GHOST_ROWS // 16):
                store(c, pl.ds(side * (GHOST_ROWS // 2) + b * 8, 8), raw[c, pl.ds(b * 16 + side, 8, stride=2), :])


def gather_stages(comps, read_rows, source, place, cells, listed, out):
    zeros = (jnp.zeros((8, LANES), f32),) * comps

    for half in range(GROUPS // 8):
        first = half * 8 * GROUP_ROWS
        most = cells[CELLS, half * 8]
        for k in range(1, 8):
            most = jnp.maximum(most, cells[CELLS, half * 8 + k])

        def list_rows(pair, carry, first=first):
            spots = [pl.ds(first + 2 * pair + k, 8, stride=32) for k in range(2)]
            src = [source[spot, :] for spot in spots]
            lane = [item & 127 for item in src]
            row = [item >> 7 for item in src]
            accs = [list(zeros), list(zeros)]
            for u in range(GROUP_ROWS):
                mine = [item == u for item in row]
                for c in range(comps):
                    lines = read_rows(c, pl.ds(first + u, 8, stride=GROUP_ROWS))
                    for k in range(2):
                        accs[k][c] = jnp.where(mine[k], jnp.take_along_axis(lines, lane[k], axis=1), accs[k][c])
            for k in range(2):
                for c in range(comps):
                    listed[c, spots[k], :] = accs[k][c]
            return carry

        lax.fori_loop(0, (most + 255) >> 8, list_rows, 0)

    def slot_block(t, carry):
        here = pl.ds(pl.multiple_of(t * 8, 8), 8)
        at = place[here, :]
        lane = at & 127
        row = at >> 7

        def visit(r, accs):
            mine = row == r
            return tuple(
                jnp.where(
                    mine,
                    jnp.take_along_axis(jnp.broadcast_to(listed[c, pl.ds(r, 1), :], (8, LANES)), lane, axis=1),
                    accs[c],
                )
                for c in range(comps)
            )

        def rows_of(g):
            begin, end = cells[t, g], cells[t + 1, g]
            return g * 32 + jnp.minimum(begin >> 7, 31), g * 32 + (jnp.maximum(end - 1, begin) >> 7)

        accs = zeros
        widest = 0
        for g in range(GROUPS):
            first, last = rows_of(g)
            last = jnp.minimum(last, g * 32 + 31)
            accs = visit(first, accs)
            accs = visit(last, accs)
            widest = jnp.maximum(widest, last - first)
        for c in range(comps):
            out[c, here, :] = accs[c]

        @pl.when(widest > 1)
        def _():
            def rest(g, accs):
                first, last = rows_of(g)
                return lax.fori_loop(first, jnp.minimum(last, g * 32 + 31) + 1, visit, accs)

            more = lax.fori_loop(0, GROUPS, rest, tuple(out[c, here, :] for c in range(comps)))
            for c in range(comps):
                out[c, here, :] = more[c]

        return carry

    lax.fori_loop(0, GHOST_ROWS // 8, slot_block, 0)


def pick(partner, window, own, below, above):
    wanted = jnp.full(own.shape, partner, jnp.int32)
    return jnp.where(wanted == window - 1, below, jnp.where(wanted == window + 1, above, own))


def first_gather_kernel(
    partner, cells, own, below, above, charges, path_weight, source, place, position, ghosts, partial, listed, raw
):
    window = lax.axis_index("rep")
    for c in range(3):
        position[c] = pick(partner[0], window, own[c], below[c], above[c])
    partial[...] = jnp.sum((path_weight[...] * position[2]).reshape(64, 8, LANES), axis=0)
    gather_positions(4, (position, charges), source, place, cells, ghosts, listed, raw)


def gather_positions(comps, tables, source, place, cells, ghosts, listed, raw):
    def read_rows(c, rows):
        return tables[1][rows, :] if c == 3 else tables[0][c, rows, :]

    def store(c, rows, value):
        ghosts[c, rows, :] = value

    gather_stages(comps, read_rows, source, place, cells, listed, raw)
    unmix(comps, raw, store)


def gather_scratch(comps):
    return [pltpu.VMEM((comps, GROUPS * 32, LANES), f32), pltpu.VMEM((comps, GHOST_ROWS, LANES), f32)]


def first_gather(partner, cells, own, below, above, charges, path_weight, source, place):
    return pl.pallas_call(
        first_gather_kernel,
        out_shape=(
            jax.ShapeDtypeStruct((3, TILES, LANES), f32),
            jax.ShapeDtypeStruct((4, GHOST_ROWS, LANES), f32),
            jax.ShapeDtypeStruct((8, LANES), f32),
        ),
        in_specs=[SMEM] * 2 + [VMEM] * 7,
        out_specs=(VMEM,) * 3,
        scratch_shapes=gather_scratch(4),
        compiler_params=params(),
        name="first_gather",
    )(partner, cells, own, below, above, charges, path_weight, source, place)


def parts3(value):
    high = value.astype(bf16).astype(f32)
    rest = value - high
    middle = rest.astype(bf16).astype(f32)
    return high, middle, rest - middle


def step_kernel(
    count, windows, last, spring, center, partner, pairs, ghosts, velocity_in, mass_in, weight_in, partial, position,
    charges, *rest,
):
    if last:
        lower_q, upper_q, *rest = rest
    new_position, new_velocity, result, *rest = rest
    if last:
        kept_q = ()
    else:
        kept_q, rest = rest[:2], rest[2:]
        rest, (velocity_below, velocity_above, sent_v, got_v) = rest[:-4], rest[-4:]
    (
        rows_j, rows_i, rows_a, feat_j, feat_i, feat_a, sums, spread_a, spread_b,
        lower, upper, parts, final, sent, got, sent_last, got_last, velocity, inv_mass, path_weight, filled,
    ) = rest
    late_copies = [
        pltpu.make_async_copy(source, target, filled.at[n])
        for n, (source, target) in enumerate(((velocity_in, velocity), (mass_in, inv_mass), (weight_in, path_weight)))
    ]
    for copy in late_copies:
        copy.start()
    me = lax.axis_index("dom")
    half = GHOST_ROWS // 2
    barrier = pltpu.get_barrier_semaphore()
    for k in range(1, count):
        pl.semaphore_signal(
            barrier, inc=1, device_id={"dom": lax.rem(me + k, count)}, device_id_type=pl.DeviceIdType.MESH
        )
    if not last:
        window = lax.axis_index("rep")
        ahead, behind = lax.rem(window + 1, windows), lax.rem(window + windows - 1, windows)
        for other in (ahead, behind):
            pl.semaphore_signal(barrier, inc=1, device_id={"rep": other}, device_id_type=pl.DeviceIdType.MESH)

    zero8 = jnp.zeros((8, LANES), f32)
    one8 = jnp.ones((8, LANES), f32)
    for f in (13, 14, 15):
        rows_j[pl.ds(f, 8, stride=16), :] = zero8
    rows_j[pl.ds(12, 8, stride=16), :] = one8
    for f in (12, 13, 14, 15):
        rows_a[pl.ds(f, 8, stride=16), :] = zero8
    rows_i[...] = jnp.zeros_like(rows_i)
    for f in (9, 10, 11):
        rows_i[pl.ds(f, 8, stride=48), :] = one8

    def build(first_tile, x, y, z, q, own):
        norm = x * x + y * y + z * z
        split = [parts3(value) for value in (x, y, z)]
        for c in range(3):
            for s in range(3):
                rows_j[pl.ds(3 * s + c, 8, stride=16), :] = split[c][s]
        for s, value in enumerate(parts3(norm)):
            rows_j[pl.ds(9 + s, 8, stride=16), :] = value
        for k, value in enumerate((q, q * x, q * y, q * z)):
            for s, piece in enumerate(parts3(value)):
                rows_a[pl.ds(4 * s + k, 8, stride=16), :] = piece
        for n in range(8):
            feat_j[first_tile + n] = rows_j[16 * n : 16 * n + 16, :].astype(bf16)
            feat_a[first_tile + n] = rows_a[16 * n : 16 * n + 16, :].astype(bf16)
        if own:
            for c in range(3):
                for s in range(3):
                    value = -2.0 * split[c][s]
                    for j in range(3 - s):
                        rows_i[pl.ds(16 * s + 3 * j + c, 8, stride=48), :] = value
            for s, value in enumerate(parts3(norm + 1.0)):
                rows_i[pl.ds(16 * s + 12, 8, stride=48), :] = value
            for n in range(8):
                feat_i[first_tile + n] = rows_i[48 * n : 48 * n + 48, :].astype(bf16)

    def own_block(b, carry):
        base = pl.multiple_of(b * 8, 8)
        here = pl.ds(base, 8)
        build(base, position[0, here, :], position[1, here, :], position[2, here, :], charges[here, :], True)
        return carry

    lax.fori_loop(0, TILES // 16, own_block, 0)
    pl.semaphore_wait(barrier, count - 1 if last else count + 1)

    def send(source, target, k, sent_now, got_now):
        copy = pltpu.make_async_remote_copy(
            src_ref=source,
            dst_ref=target,
            send_sem=sent_now,
            recv_sem=got_now,
            device_id={"dom": lax.rem(me + k, count)},
            device_id_type=pl.DeviceIdType.MESH,
        )
        copy.start()
        return copy

    ghost_copies = [
        send(ghosts.at[:, pl.ds(half, half)], lower, 1, sent.at[0], got.at[0]),
        send(ghosts.at[:, pl.ds(0, half)], upper, count - 1, sent.at[count], got.at[count]),
    ]
    term_copies = [send(partial, parts.at[me], k, sent.at[k], got.at[k]) for k in range(1, count)]
    lax.fori_loop(TILES // 16, TILES // 8, own_block, 0)

    def ghost_block(values, charge, offset):
        def block(b, carry):
            base = pl.multiple_of(b * 8, 8)
            here = pl.ds(base, 8)
            build(offset + base, values[0, here, :], values[1, here, :], values[2, here, :], charge[here, :], False)
            return carry

        return block

    for copy in ghost_copies:
        copy.wait()
    velocity_copies = []
    if not last:
        for n, (other, target) in enumerate(((ahead, velocity_below), (behind, velocity_above))):
            copy = pltpu.make_async_remote_copy(
                src_ref=velocity_in,
                dst_ref=target,
                send_sem=sent_v.at[n],
                recv_sem=got_v.at[n],
                device_id={"rep": other},
                device_id_type=pl.DeviceIdType.MESH,
            )
            copy.start()
            velocity_copies.append(copy)

    if last:
        charge_of = (lower_q, upper_q)
    else:
        charge_of = (lower.at[3], upper.at[3])
        kept_q[0][...] = lower[3]
        kept_q[1][...] = upper[3]
    lax.fori_loop(0, 16, ghost_block(lower, charge_of[0], TILES), 0)
    lax.fori_loop(0, 16, ghost_block(upper, charge_of[1], TILES + 128), 0)

    def contract(a, b, left, right):
        return lax.dot_general(a, b, (((left,), (right,)), ((), ())), preferred_element_type=f32)

    def listed(tile):
        tile = jnp.minimum(tile, TILES - 1)
        return tile, pairs[0, tile], pairs[1, tile]

    def spread_of(tile):
        tile, one, two = listed(tile)
        near = jnp.concatenate([feat_j[one], feat_j[two]], axis=1)
        return contract(jnp.concatenate([near] * 3, axis=0), feat_i[tile], 0, 0)

    def force_of(tile, spread):
        tile, one, two = listed(tile)
        weight = pl.reciprocal(spread * spread, approx=True)
        high = weight.astype(bf16)
        low = (weight - high.astype(f32)).astype(bf16)
        near = jnp.concatenate([feat_a[one], feat_a[two]], axis=1)
        return contract(jnp.concatenate([near, near], axis=1), jnp.concatenate([high, low], axis=0), 1, 0)

    many = TILES_AT_ONCE
    for u in range(many):
        spread_a[u] = spread_of(u)

    def tiles(m, carry):
        for now, later, n in ((spread_a, spread_b, 2 * m), (spread_b, spread_a, 2 * m + 1)):
            done = []
            for u in range(many):
                later[u] = spread_of((n + 1) * many + u)
                done.append(force_of(n * many + u, now[u]))
            for u in range(many):
                sums[pl.ds(pl.multiple_of((n * many + u) * 16, 16), 16), :] = done[u]
        return carry

    lax.fori_loop(0, TILES // many // 2, tiles, 0)

    def total_of(terms, own, copies):
        for copy in copies:
            copy.wait()
        terms[me] = own[...]
        return jnp.sum(terms[...])

    progress = total_of(parts, partial, term_copies)
    pull = spring[0] * (progress - center[0])
    for copy in late_copies + velocity_copies:
        copy.wait()

    def velocity_at(c, here):
        own = velocity[c, here, :]
        if last:
            return own
        return pick(partner[0], window, own, velocity_below[c, here, :], velocity_above[c, here, :])

    def combine(b, part):
        base = pl.multiple_of(b * 8, 8)
        here = pl.ds(base, 8)
        total = []
        for k in range(4):
            value = sums[pl.ds(base * 16 + k, 8, stride=16), :]
            value = value + sums[pl.ds(base * 16 + 4 + k, 8, stride=16), :]
            value = value + sums[pl.ds(base * 16 + 8 + k, 8, stride=16), :]
            total.append(value)
        q = charges[here, :]
        weight = path_weight[here, :]
        rate = time_step * inv_mass[here, :]
        for c in range(3):
            old = position[c, here, :]
            force = q * (old * total[0] - total[c + 1])
            if c == 2:
                force = force - pull * weight
            moved = velocity_at(c, here) + rate * force
            placed = old + time_step * moved
            new_velocity[c, here, :] = moved
            new_position[c, here, :] = placed
        return part + weight * placed

    ending = lax.fori_loop(0, TILES // 8, combine, jnp.zeros((8, LANES), f32))
    if last:
        partial_last = spread_a.at[0, pl.ds(0, 8), :]
        spread_a[0, pl.ds(0, 8), :] = ending
        final_copies = [
            send(partial_last, final.at[me], k, sent_last.at[k], got_last.at[k]) for k in range(1, count)
        ]
        off = total_of(final, partial_last, final_copies) - center[0]
        result[0] = 0.5 * spring[0] * off * off
    else:
        result[...] = ending


def step(
    number, last, spring, center, partner, pairs, ghosts, partial, position, velocity, charges, inv_mass, path_weight, *kept_q
):
    count, windows = lax.axis_size("dom"), lax.axis_size("rep")
    comps, rows = ghosts.shape[:2]
    whole = jax.ShapeDtypeStruct((3, TILES, LANES), f32)
    side_q = jax.ShapeDtypeStruct((rows // 2, LANES), f32)
    kept = () if last else (side_q, side_q)
    carried = () if last else (
        pltpu.VMEM(velocity.shape, f32),
        pltpu.VMEM(velocity.shape, f32),
        pltpu.SemaphoreType.DMA((2,)),
        pltpu.SemaphoreType.DMA((2,)),
    )

    def kernel(*refs):
        step_kernel(count, windows, last, *refs)

    return pl.pallas_call(
        kernel,
        out_shape=(whole, whole, jax.ShapeDtypeStruct((1,) if last else (8, LANES), f32)) + kept,
        in_specs=[SMEM] * 4 + [pl.BlockSpec(memory_space=pl.ANY)] * 4 + [VMEM] * (3 + len(kept_q)),
        out_specs=(VMEM, VMEM, SMEM if last else VMEM) + (VMEM,) * len(kept),
        scratch_shapes=[
            pltpu.VMEM((8 * 16, LANES), f32),
            pltpu.VMEM((8 * 48, LANES), f32),
            pltpu.VMEM((8 * 16, LANES), f32),
            pltpu.VMEM((TILES + 256, 16, LANES), bf16),
            pltpu.VMEM((TILES, 48, LANES), bf16),
            pltpu.VMEM((TILES + 256, 16, LANES), bf16),
            pltpu.VMEM((TILES * 16, LANES), f32),
            pltpu.VMEM((TILES_AT_ONCE, 2 * LANES, LANES), f32),
            pltpu.VMEM((TILES_AT_ONCE, 2 * LANES, LANES), f32),
            pltpu.VMEM((comps, rows // 2, LANES), f32),
            pltpu.VMEM((comps, rows // 2, LANES), f32),
            pltpu.VMEM((count, 8, LANES), f32),
            pltpu.VMEM((count, 8, LANES), f32),
            pltpu.SemaphoreType.DMA((count + 1,)),
            pltpu.SemaphoreType.DMA((count + 1,)),
            pltpu.SemaphoreType.DMA((count,)),
            pltpu.SemaphoreType.DMA((count,)),
            pltpu.VMEM(velocity.shape, f32),
            pltpu.VMEM(inv_mass.shape, f32),
            pltpu.VMEM(path_weight.shape, f32),
            pltpu.SemaphoreType.DMA((3,)),
            *carried,
        ],
        compiler_params=pltpu.CompilerParams(
            vmem_limit_bytes=58 * 1024 * 1024, collective_id=number, has_side_effects=True
        ),
        name="step",
    )(
        spring, center, partner, pairs, ghosts, velocity, inv_mass, path_weight, partial, position, charges, *kept_q
    )


def second_gather_kernel(cells, *refs):
    position, source, place, ghosts, listed, raw = refs
    gather_positions(3, (position,), source, place, cells, ghosts, listed, raw)


def second_gather(cells, position, source, place):
    return pl.pallas_call(
        second_gather_kernel,
        out_shape=jax.ShapeDtypeStruct((3, GHOST_ROWS, LANES), f32),
        in_specs=[SMEM] + [VMEM] * 3,
        out_specs=VMEM,
        scratch_shapes=gather_scratch(3),
        compiler_params=params(),
        name="second_gather",
    )(cells, position, source, place)


def shifted(shard, axis, by):
    count = lax.axis_size(axis)
    pairs = [(i, i + by) for i in range(count) if 0 <= i + by < count]
    return lax.ppermute(shard, axis, pairs)


def body(positions, velocities, charges, inv_mass, path_weight, halo_index, tile_pairs, partner, bias_center, bias_spring):
    position = positions[0].reshape(3, TILES, LANES)
    velocity = velocities[0].reshape(3, TILES, LANES)
    charges = charges.reshape(TILES, LANES)
    inv_mass = inv_mass.reshape(TILES, LANES)
    path_weight = path_weight.reshape(TILES, LANES)
    pairs = tile_pairs.T
    halo = halo_index.reshape(2, GHOST_ROWS // 2, LANES).transpose(1, 0, 2).reshape(GHOST_ROWS, LANES)
    below = shifted(position, "rep", 1)
    above = shifted(position, "rep", -1)
    source, place, cells = plan(halo)
    position, ghosts, partial = first_gather(
        partner, cells, position, below, above, charges, path_weight, source, place
    )
    kept_q = ()
    for step_index in range(STEPS):
        last = step_index == STEPS - 1
        position, velocity, partial, *kept_q = step(
            step_index, last, bias_spring, bias_center, partner, pairs, ghosts, partial, position, velocity,
            charges, inv_mass, path_weight, *kept_q,
        )
        if not last:
            ghosts = second_gather(cells, position, source, place)
    atoms = TILES * LANES
    return position.reshape(1, 3, atoms), velocity.reshape(1, 3, atoms), partial


def solution(mesh):
    in_specs = (
        P("rep", None, "dom"),
        P("rep", None, "dom"),
        P("dom"),
        P("dom"),
        P("dom"),
        P(None, "dom"),
        P("dom", None),
        P("rep"),
        P("rep"),
        P("rep"),
    )
    out_specs = (P("rep", None, "dom"), P("rep", None, "dom"), P("rep"))
    return jax.shard_map(body, mesh=mesh, in_specs=in_specs, out_specs=out_specs, check_vma=False)
```

```python
import jax
import jax.numpy as jnp
from jax import lax
from jax.experimental import pallas as pl
from jax.experimental.pallas import tpu as pltpu
from jax.sharding import PartitionSpec as P

LANES = 128
STEPS = 2
TILES = 512
GHOST_ROWS = 256
GROUPS = 16
GROUP_ROWS = 32
CELLS = 32
CAPACITY = 4096
TILES_AT_ONCE = 16
time_step = 0.1
f32 = jnp.float32
bf16 = jnp.bfloat16
VMEM = pl.BlockSpec(memory_space=pltpu.VMEM)
SMEM = pl.BlockSpec(memory_space=pltpu.SMEM)


def params():
    return pltpu.CompilerParams(vmem_limit_bytes=20 * 1024 * 1024)


def plan_kernel(halo, source, place, cells, ranks, counts):
    shape = (GHOST_ROWS, LANES)
    row = lax.broadcasted_iota(jnp.int32, shape, 0)
    lane = lax.broadcasted_iota(jnp.int32, shape, 1)
    wide = (LANES, 2 * LANES)
    across = lax.broadcasted_iota(jnp.int32, wide, 1)
    ahead_lane = (lax.broadcasted_iota(jnp.int32, wide, 0) < across) | (across >= LANES)
    ahead_lane = jnp.where(ahead_lane, 1.0, 0.0).astype(bf16)
    square = (GHOST_ROWS, GHOST_ROWS)
    ahead_row = lax.broadcasted_iota(jnp.int32, square, 1) < lax.broadcasted_iota(jnp.int32, square, 0)
    ahead_row = jnp.where(ahead_row, 1.0, 0.0).astype(bf16)
    counts[...] = jnp.zeros(shape, f32)

    def count_group(group, carry):
        member = (halo[...] >> 12) == group
        within = jnp.dot(jnp.where(member, 1.0, 0.0).astype(bf16), ahead_lane, preferred_element_type=f32)
        ranks[...] = jnp.where(member, within[:, :LANES].astype(jnp.int32), ranks[...])
        counts[...] = jnp.where(lane == group, within[:, LANES:], counts[...])
        return carry

    lax.fori_loop(0, GROUPS, count_group, 0, unroll=4)
    earlier = jnp.dot(ahead_row, counts[...].astype(bf16), preferred_element_type=f32)
    total = (earlier[GHOST_ROWS - 1 :] + counts[GHOST_ROWS - 1 :, :]).astype(jnp.int32)
    earlier = earlier.astype(jnp.int32)
    for b in range(GHOST_ROWS // 8):
        here = slice(8 * b, 8 * b + 8)
        group_of = halo[here, :] >> 12
        rank = ranks[here, :] + jnp.take_along_axis(earlier[here], group_of, axis=1)
        ranks[here, :] = rank
        place[here, :] = rank + group_of * CAPACITY
        cells[b : b + 1, :] = earlier[8 * b : 8 * b + 1]
    cells[CELLS : CELLS + 8, :] = jnp.broadcast_to(total, (8, LANES))

    def one_group(group, carry):
        index = halo[...]
        member = (index >> 12) == group
        rank = ranks[...]
        shift = row * LANES + lane - rank
        items = jnp.where(member, (1 << 28) | (shift << 12) | (index & 4095), 0)
        for bit in range(15):
            step_by = 1 << bit
            if step_by < LANES:
                following = pltpu.roll(items, items.shape[0] - 1, 0)
                mixed = jnp.where(lane < step_by, following, items)
                moved = pltpu.roll(mixed, LANES - step_by, 1)
                held = items
            else:
                rows = step_by // LANES
                if rows < 32:
                    if rows < 8:
                        moved = pltpu.roll(items, items.shape[0] - rows, 0)
                    else:
                        moved = jnp.concatenate([items[rows:], items[:rows]], axis=0)
                    held = items
                else:
                    blocks = items.reshape(items.shape[0] // 64, 2, 32, LANES)
                    held = blocks[:, 0].reshape(-1, LANES)
                    moved = blocks[:, 1].reshape(-1, LANES)
            mask = 1 << (12 + bit)
            items = jnp.where((moved & mask) != 0, moved, jnp.where((held & mask) != 0, 0, held))
        source[pl.ds(pl.multiple_of(group * 32, 32), 32), :] = items & 4095
        return carry

    def two_groups(pair, carry):
        one_group(2 * pair, carry)
        return one_group(2 * pair + 1, carry)

    lax.fori_loop(0, GROUPS // 2, two_groups, 0)


def plan(halo):
    return pl.pallas_call(
        plan_kernel,
        out_shape=(
            jax.ShapeDtypeStruct((GROUPS * 32, LANES), jnp.int32),
            jax.ShapeDtypeStruct((GHOST_ROWS, LANES), jnp.int32),
            jax.ShapeDtypeStruct((CELLS + 8, LANES), jnp.int32),
        ),
        in_specs=[VMEM],
        out_specs=(VMEM,) * 3,
        scratch_shapes=[pltpu.VMEM((GHOST_ROWS, LANES), jnp.int32), pltpu.VMEM((GHOST_ROWS, LANES), f32)],
        compiler_params=params(),
        name="plan",
    )(halo)


def unmix(comps, raw, store):
    for c in range(comps):
        for side in range(2):
            for b in range(GHOST_ROWS // 16):
                store(c, pl.ds(side * (GHOST_ROWS // 2) + b * 8, 8), raw[c, pl.ds(b * 16 + side, 8, stride=2), :])


def gather_stages(comps, read_rows, source, place, cells, listed, out):
    zeros = (jnp.zeros((8, LANES), f32),) * comps

    for half in range(GROUPS // 8):
        first = half * 8 * GROUP_ROWS
        most = cells[CELLS, half * 8]
        for k in range(1, 8):
            most = jnp.maximum(most, cells[CELLS, half * 8 + k])

        def list_rows(pair, carry, first=first):
            spots = [pl.ds(first + 2 * pair + k, 8, stride=32) for k in range(2)]
            src = [source[spot, :] for spot in spots]
            lane = [item & 127 for item in src]
            row = [item >> 7 for item in src]
            accs = [list(zeros), list(zeros)]
            for u in range(GROUP_ROWS):
                mine = [item == u for item in row]
                for c in range(comps):
                    lines = read_rows(c, pl.ds(first + u, 8, stride=GROUP_ROWS))
                    for k in range(2):
                        accs[k][c] = jnp.where(mine[k], jnp.take_along_axis(lines, lane[k], axis=1), accs[k][c])
            for k in range(2):
                for c in range(comps):
                    listed[c, spots[k], :] = accs[k][c]
            return carry

        lax.fori_loop(0, (most + 255) >> 8, list_rows, 0)

    def slot_block(t):
        here = pl.ds(pl.multiple_of(t * 8, 8), 8)
        at = place[here, :]
        lane = at & 127
        row = at >> 7

        def visit(r, accs):
            mine = row == r
            return tuple(
                jnp.where(
                    mine,
                    jnp.take_along_axis(jnp.broadcast_to(listed[c, pl.ds(r, 1), :], (8, LANES)), lane, axis=1),
                    accs[c],
                )
                for c in range(comps)
            )

        def rows_of(g):
            begin, end = cells[t, g], cells[t + 1, g]
            return g * 32 + jnp.minimum(begin >> 7, 31), g * 32 + (jnp.maximum(end - 1, begin) >> 7)

        def narrow():
            accs = zeros
            widest = 0
            for g in range(GROUPS):
                first, last = rows_of(g)
                last = jnp.minimum(last, g * 32 + 31)
                accs = visit(first, accs)
                accs = visit(last, accs)
                widest = jnp.maximum(widest, last - first)
            for c in range(comps):
                out[c, here, :] = accs[c]
            return widest

        def wide():
            def rest(g, accs):
                first, last = rows_of(g)
                return lax.fori_loop(first, jnp.minimum(last, g * 32 + 31) + 1, visit, accs)

            more = lax.fori_loop(0, GROUPS, rest, tuple(out[c, here, :] for c in range(comps)))
            for c in range(comps):
                out[c, here, :] = more[c]

        return narrow, wide

    def slot_blocks(n, carry):
        blocks = [slot_block(2 * n + k) for k in range(2)]
        widest = [narrow() for narrow, _ in blocks]

        @pl.when(jnp.maximum(*widest) > 1)
        def _():
            for _, wide in blocks:
                wide()

        return carry

    lax.fori_loop(0, GHOST_ROWS // 16, slot_blocks, 0)


def pick(partner, window, own, below, above):
    wanted = jnp.full(own.shape, partner, jnp.int32)
    return jnp.where(wanted == window - 1, below, jnp.where(wanted == window + 1, above, own))


def first_gather_kernel(
    partner, cells, own, below, above, charges, path_weight, source, place, position, ghosts, partial, listed, raw
):
    window = lax.axis_index("rep")
    for c in range(3):
        position[c] = pick(partner[0], window, own[c], below[c], above[c])
    partial[...] = jnp.sum((path_weight[...] * position[2]).reshape(64, 8, LANES), axis=0)
    gather_positions(4, (position, charges), source, place, cells, ghosts, listed, raw)


def gather_positions(comps, tables, source, place, cells, ghosts, listed, raw):
    def read_rows(c, rows):
        return tables[1][rows, :] if c == 3 else tables[0][c, rows, :]

    def store(c, rows, value):
        ghosts[c, rows, :] = value

    gather_stages(comps, read_rows, source, place, cells, listed, raw)
    unmix(comps, raw, store)


def gather_scratch(comps):
    return [pltpu.VMEM((comps, GROUPS * 32, LANES), f32), pltpu.VMEM((comps, GHOST_ROWS, LANES), f32)]


def first_gather(partner, cells, own, below, above, charges, path_weight, source, place):
    return pl.pallas_call(
        first_gather_kernel,
        out_shape=(
            jax.ShapeDtypeStruct((3, TILES, LANES), f32),
            jax.ShapeDtypeStruct((4, GHOST_ROWS, LANES), f32),
            jax.ShapeDtypeStruct((8, LANES), f32),
        ),
        in_specs=[SMEM] * 2 + [VMEM] * 7,
        out_specs=(VMEM,) * 3,
        scratch_shapes=gather_scratch(4),
        compiler_params=params(),
        name="first_gather",
    )(partner, cells, own, below, above, charges, path_weight, source, place)


def parts3(value):
    high = value.astype(bf16).astype(f32)
    rest = value - high
    middle = rest.astype(bf16).astype(f32)
    return high, middle, rest - middle


def step_kernel(
    count, windows, last, spring, center, partner, pairs, ghosts, velocity_in, mass_in, weight_in, partial, position,
    charges, *rest,
):
    if last:
        lower_q, upper_q, *rest = rest
    new_position, new_velocity, result, *rest = rest
    if last:
        kept_q = ()
    else:
        kept_q, rest = rest[:2], rest[2:]
        rest, (velocity_below, velocity_above, sent_v, got_v) = rest[:-4], rest[-4:]
    (
        rows_j, rows_i, rows_a, feat_j, feat_i, feat_a, sums, spread_a, spread_b,
        lower, upper, parts, final, sent, got, sent_last, got_last, velocity, inv_mass, path_weight, filled,
    ) = rest
    late_copies = [
        pltpu.make_async_copy(source, target, filled.at[n])
        for n, (source, target) in enumerate(((velocity_in, velocity), (mass_in, inv_mass), (weight_in, path_weight)))
    ]
    for copy in late_copies:
        copy.start()
    me = lax.axis_index("dom")
    half = GHOST_ROWS // 2
    barrier = pltpu.get_barrier_semaphore()
    for k in range(1, count):
        pl.semaphore_signal(
            barrier, inc=1, device_id={"dom": lax.rem(me + k, count)}, device_id_type=pl.DeviceIdType.MESH
        )
    if not last:
        window = lax.axis_index("rep")
        ahead, behind = lax.rem(window + 1, windows), lax.rem(window + windows - 1, windows)
        for other in (ahead, behind):
            pl.semaphore_signal(barrier, inc=1, device_id={"rep": other}, device_id_type=pl.DeviceIdType.MESH)

    zero8 = jnp.zeros((8, LANES), f32)
    one8 = jnp.ones((8, LANES), f32)
    for f in (13, 14, 15):
        rows_j[pl.ds(f, 8, stride=16), :] = zero8
    rows_j[pl.ds(12, 8, stride=16), :] = one8
    for f in (12, 13, 14, 15):
        rows_a[pl.ds(f, 8, stride=16), :] = zero8
    rows_i[...] = jnp.zeros_like(rows_i)
    for f in (9, 10, 11):
        rows_i[pl.ds(f, 8, stride=48), :] = one8

    def build(first_tile, x, y, z, q, own):
        norm = x * x + y * y + z * z
        split = [parts3(value) for value in (x, y, z)]
        for c in range(3):
            for s in range(3):
                rows_j[pl.ds(3 * s + c, 8, stride=16), :] = split[c][s]
        for s, value in enumerate(parts3(norm)):
            rows_j[pl.ds(9 + s, 8, stride=16), :] = value
        for k, value in enumerate((q, q * x, q * y, q * z)):
            for s, piece in enumerate(parts3(value)):
                rows_a[pl.ds(4 * s + k, 8, stride=16), :] = piece
        for n in range(8):
            feat_j[first_tile + n] = rows_j[16 * n : 16 * n + 16, :].astype(bf16)
            feat_a[first_tile + n] = rows_a[16 * n : 16 * n + 16, :].astype(bf16)
        if own:
            for c in range(3):
                for s in range(3):
                    value = -2.0 * split[c][s]
                    for j in range(3 - s):
                        rows_i[pl.ds(16 * s + 3 * j + c, 8, stride=48), :] = value
            for s, value in enumerate(parts3(norm + 1.0)):
                rows_i[pl.ds(16 * s + 12, 8, stride=48), :] = value
            for n in range(8):
                feat_i[first_tile + n] = rows_i[48 * n : 48 * n + 48, :].astype(bf16)

    def own_block(b, carry):
        base = pl.multiple_of(b * 8, 8)
        here = pl.ds(base, 8)
        build(base, position[0, here, :], position[1, here, :], position[2, here, :], charges[here, :], True)
        return carry

    lax.fori_loop(0, TILES // 16, own_block, 0)
    pl.semaphore_wait(barrier, count - 1 if last else count + 1)

    def send(source, target, k, sent_now, got_now):
        copy = pltpu.make_async_remote_copy(
            src_ref=source,
            dst_ref=target,
            send_sem=sent_now,
            recv_sem=got_now,
            device_id={"dom": lax.rem(me + k, count)},
            device_id_type=pl.DeviceIdType.MESH,
        )
        copy.start()
        return copy

    ghost_copies = [
        send(ghosts.at[:, pl.ds(half, half)], lower, 1, sent.at[0], got.at[0]),
        send(ghosts.at[:, pl.ds(0, half)], upper, count - 1, sent.at[count], got.at[count]),
    ]
    term_copies = [send(partial, parts.at[me], k, sent.at[k], got.at[k]) for k in range(1, count)]
    lax.fori_loop(TILES // 16, TILES // 8, own_block, 0)

    def ghost_block(values, charge, offset):
        def block(b, carry):
            base = pl.multiple_of(b * 8, 8)
            here = pl.ds(base, 8)
            build(offset + base, values[0, here, :], values[1, here, :], values[2, here, :], charge[here, :], False)
            return carry

        return block

    for copy in ghost_copies:
        copy.wait()
    velocity_copies = []
    if not last:
        for n, (other, target) in enumerate(((ahead, velocity_below), (behind, velocity_above))):
            copy = pltpu.make_async_remote_copy(
                src_ref=velocity_in,
                dst_ref=target,
                send_sem=sent_v.at[n],
                recv_sem=got_v.at[n],
                device_id={"rep": other},
                device_id_type=pl.DeviceIdType.MESH,
            )
            copy.start()
            velocity_copies.append(copy)

    if last:
        charge_of = (lower_q, upper_q)
    else:
        charge_of = (lower.at[3], upper.at[3])
        kept_q[0][...] = lower[3]
        kept_q[1][...] = upper[3]
    lax.fori_loop(0, 16, ghost_block(lower, charge_of[0], TILES), 0)
    lax.fori_loop(0, 16, ghost_block(upper, charge_of[1], TILES + 128), 0)

    def contract(a, b, left, right):
        return lax.dot_general(a, b, (((left,), (right,)), ((), ())), preferred_element_type=f32)

    def listed(tile):
        tile = jnp.minimum(tile, TILES - 1)
        return tile, pairs[0, tile], pairs[1, tile]

    def spread_of(tile):
        tile, one, two = listed(tile)
        near = jnp.concatenate([feat_j[one], feat_j[two]], axis=1)
        return contract(jnp.concatenate([near] * 3, axis=0), feat_i[tile], 0, 0)

    def force_of(tile, spread):
        tile, one, two = listed(tile)
        weight = pl.reciprocal(spread * spread, approx=True)
        high = weight.astype(bf16)
        low = (weight - high.astype(f32)).astype(bf16)
        near = jnp.concatenate([feat_a[one], feat_a[two]], axis=1)
        return contract(jnp.concatenate([near, near], axis=1), jnp.concatenate([high, low], axis=0), 1, 0)

    many = TILES_AT_ONCE
    for u in range(many):
        spread_a[u] = spread_of(u)

    def tiles(m, carry):
        for now, later, n in ((spread_a, spread_b, 2 * m), (spread_b, spread_a, 2 * m + 1)):
            done = []
            for u in range(many):
                later[u] = spread_of((n + 1) * many + u)
                done.append(force_of(n * many + u, now[u]))
            for u in range(many):
                sums[pl.ds(pl.multiple_of((n * many + u) * 16, 16), 16), :] = done[u]
        return carry

    lax.fori_loop(0, TILES // many // 2, tiles, 0)

    def total_of(terms, own, copies):
        for copy in copies:
            copy.wait()
        terms[me] = own[...]
        return jnp.sum(terms[...])

    progress = total_of(parts, partial, term_copies)
    pull = spring[0] * (progress - center[0])
    for copy in late_copies + velocity_copies:
        copy.wait()

    def velocity_at(c, here):
        own = velocity[c, here, :]
        if last:
            return own
        return pick(partner[0], window, own, velocity_below[c, here, :], velocity_above[c, here, :])

    def combine(b, part):
        base = pl.multiple_of(b * 8, 8)
        here = pl.ds(base, 8)
        total = []
        for k in range(4):
            value = sums[pl.ds(base * 16 + k, 8, stride=16), :]
            value = value + sums[pl.ds(base * 16 + 4 + k, 8, stride=16), :]
            value = value + sums[pl.ds(base * 16 + 8 + k, 8, stride=16), :]
            total.append(value)
        q = charges[here, :]
        weight = path_weight[here, :]
        rate = time_step * inv_mass[here, :]
        for c in range(3):
            old = position[c, here, :]
            force = q * (old * total[0] - total[c + 1])
            if c == 2:
                force = force - pull * weight
            moved = velocity_at(c, here) + rate * force
            placed = old + time_step * moved
            new_velocity[c, here, :] = moved
            new_position[c, here, :] = placed
        return part + weight * placed

    ending = lax.fori_loop(0, TILES // 8, combine, jnp.zeros((8, LANES), f32))
    if last:
        partial_last = spread_a.at[0, pl.ds(0, 8), :]
        spread_a[0, pl.ds(0, 8), :] = ending
        final_copies = [
            send(partial_last, final.at[me], k, sent_last.at[k], got_last.at[k]) for k in range(1, count)
        ]
        off = total_of(final, partial_last, final_copies) - center[0]
        result[0] = 0.5 * spring[0] * off * off
    else:
        result[...] = ending


def step(
    number, last, spring, center, partner, pairs, ghosts, partial, position, velocity, charges, inv_mass, path_weight, *kept_q
):
    count, windows = lax.axis_size("dom"), lax.axis_size("rep")
    comps, rows = ghosts.shape[:2]
    whole = jax.ShapeDtypeStruct((3, TILES, LANES), f32)
    side_q = jax.ShapeDtypeStruct((rows // 2, LANES), f32)
    kept = () if last else (side_q, side_q)
    carried = () if last else (
        pltpu.VMEM(velocity.shape, f32),
        pltpu.VMEM(velocity.shape, f32),
        pltpu.SemaphoreType.DMA((2,)),
        pltpu.SemaphoreType.DMA((2,)),
    )

    def kernel(*refs):
        step_kernel(count, windows, last, *refs)

    return pl.pallas_call(
        kernel,
        out_shape=(whole, whole, jax.ShapeDtypeStruct((1,) if last else (8, LANES), f32)) + kept,
        in_specs=[SMEM] * 4 + [pl.BlockSpec(memory_space=pl.ANY)] * 4 + [VMEM] * (3 + len(kept_q)),
        out_specs=(VMEM, VMEM, SMEM if last else VMEM) + (VMEM,) * len(kept),
        scratch_shapes=[
            pltpu.VMEM((8 * 16, LANES), f32),
            pltpu.VMEM((8 * 48, LANES), f32),
            pltpu.VMEM((8 * 16, LANES), f32),
            pltpu.VMEM((TILES + 256, 16, LANES), bf16),
            pltpu.VMEM((TILES, 48, LANES), bf16),
            pltpu.VMEM((TILES + 256, 16, LANES), bf16),
            pltpu.VMEM((TILES * 16, LANES), f32),
            pltpu.VMEM((TILES_AT_ONCE, 2 * LANES, LANES), f32),
            pltpu.VMEM((TILES_AT_ONCE, 2 * LANES, LANES), f32),
            pltpu.VMEM((comps, rows // 2, LANES), f32),
            pltpu.VMEM((comps, rows // 2, LANES), f32),
            pltpu.VMEM((count, 8, LANES), f32),
            pltpu.VMEM((count, 8, LANES), f32),
            pltpu.SemaphoreType.DMA((count + 1,)),
            pltpu.SemaphoreType.DMA((count + 1,)),
            pltpu.SemaphoreType.DMA((count,)),
            pltpu.SemaphoreType.DMA((count,)),
            pltpu.VMEM(velocity.shape, f32),
            pltpu.VMEM(inv_mass.shape, f32),
            pltpu.VMEM(path_weight.shape, f32),
            pltpu.SemaphoreType.DMA((3,)),
            *carried,
        ],
        compiler_params=pltpu.CompilerParams(
            vmem_limit_bytes=40 * 1024 * 1024, collective_id=number, has_side_effects=True
        ),
        name="step",
    )(
        spring, center, partner, pairs, ghosts, velocity, inv_mass, path_weight, partial, position, charges, *kept_q
    )


def second_gather_kernel(cells, *refs):
    position, source, place, ghosts, listed, raw = refs
    gather_positions(3, (position,), source, place, cells, ghosts, listed, raw)


def second_gather(cells, position, source, place):
    return pl.pallas_call(
        second_gather_kernel,
        out_shape=jax.ShapeDtypeStruct((3, GHOST_ROWS, LANES), f32),
        in_specs=[SMEM] + [VMEM] * 3,
        out_specs=VMEM,
        scratch_shapes=gather_scratch(3),
        compiler_params=params(),
        name="second_gather",
    )(cells, position, source, place)


def shifted(shard, axis, by):
    count = lax.axis_size(axis)
    pairs = [(i, i + by) for i in range(count) if 0 <= i + by < count]
    return lax.ppermute(shard, axis, pairs)


def body(positions, velocities, charges, inv_mass, path_weight, halo_index, tile_pairs, partner, bias_center, bias_spring):
    position = positions[0].reshape(3, TILES, LANES)
    velocity = velocities[0].reshape(3, TILES, LANES)
    charges = charges.reshape(TILES, LANES)
    inv_mass = inv_mass.reshape(TILES, LANES)
    path_weight = path_weight.reshape(TILES, LANES)
    pairs = tile_pairs.T
    halo = halo_index.reshape(2, GHOST_ROWS // 2, LANES).transpose(1, 0, 2).reshape(GHOST_ROWS, LANES)
    below = shifted(position, "rep", 1)
    above = shifted(position, "rep", -1)
    source, place, cells = plan(halo)
    position, ghosts, partial = first_gather(
        partner, cells, position, below, above, charges, path_weight, source, place
    )
    kept_q = ()
    for step_index in range(STEPS):
        last = step_index == STEPS - 1
        position, velocity, partial, *kept_q = step(
            step_index, last, bias_spring, bias_center, partner, pairs, ghosts, partial, position, velocity,
            charges, inv_mass, path_weight, *kept_q,
        )
        if not last:
            ghosts = second_gather(cells, position, source, place)
    atoms = TILES * LANES
    return position.reshape(1, 3, atoms), velocity.reshape(1, 3, atoms), partial


def solution(mesh):
    in_specs = (
        P("rep", None, "dom"),
        P("rep", None, "dom"),
        P("dom"),
        P("dom"),
        P("dom"),
        P(None, "dom"),
        P("dom", None),
        P("rep"),
        P("rep"),
        P("rep"),
    )
    out_specs = (P("rep", None, "dom"), P("rep", None, "dom"), P("rep"))
    return jax.shard_map(body, mesh=mesh, in_specs=in_specs, out_specs=out_specs, check_vma=False)
```

```python
import jax
import jax.numpy as jnp
from jax import lax
from jax.experimental import pallas as pl
from jax.experimental.pallas import tpu as pltpu
from jax.sharding import PartitionSpec as P

LANES = 128
STEPS = 2
TILES = 512
GHOST_ROWS = 256
GROUPS = 16
GROUP_ROWS = 32
CELLS = 32
CAPACITY = 4096
TILES_AT_ONCE = 16
time_step = 0.1
f32 = jnp.float32
bf16 = jnp.bfloat16
VMEM = pl.BlockSpec(memory_space=pltpu.VMEM)
SMEM = pl.BlockSpec(memory_space=pltpu.SMEM)


def params():
    return pltpu.CompilerParams(vmem_limit_bytes=20 * 1024 * 1024)


def plan_kernel(halo, source, place, cells, ranks, counts):
    shape = (GHOST_ROWS, LANES)
    row = lax.broadcasted_iota(jnp.int32, shape, 0)
    lane = lax.broadcasted_iota(jnp.int32, shape, 1)
    wide = (LANES, 2 * LANES)
    across = lax.broadcasted_iota(jnp.int32, wide, 1)
    ahead_lane = (lax.broadcasted_iota(jnp.int32, wide, 0) < across) | (across >= LANES)
    ahead_lane = jnp.where(ahead_lane, 1.0, 0.0).astype(bf16)
    square = (GHOST_ROWS, GHOST_ROWS)
    ahead_row = lax.broadcasted_iota(jnp.int32, square, 1) < lax.broadcasted_iota(jnp.int32, square, 0)
    ahead_row = jnp.where(ahead_row, 1.0, 0.0).astype(bf16)
    counts[...] = jnp.zeros(shape, f32)

    def count_group(group, carry):
        member = (halo[...] >> 12) == group
        within = jnp.dot(jnp.where(member, 1.0, 0.0).astype(bf16), ahead_lane, preferred_element_type=f32)
        ranks[...] = jnp.where(member, within[:, :LANES].astype(jnp.int32), ranks[...])
        counts[...] = jnp.where(lane == group, within[:, LANES:], counts[...])
        return carry

    lax.fori_loop(0, GROUPS, count_group, 0, unroll=4)
    earlier = jnp.dot(ahead_row, counts[...].astype(bf16), preferred_element_type=f32)
    total = (earlier[GHOST_ROWS - 1 :] + counts[GHOST_ROWS - 1 :, :]).astype(jnp.int32)
    earlier = earlier.astype(jnp.int32)
    for b in range(GHOST_ROWS // 8):
        here = slice(8 * b, 8 * b + 8)
        group_of = halo[here, :] >> 12
        rank = ranks[here, :] + jnp.take_along_axis(earlier[here], group_of, axis=1)
        ranks[here, :] = rank
        place[here, :] = rank + group_of * CAPACITY
        cells[b : b + 1, :] = earlier[8 * b : 8 * b + 1]
    cells[CELLS : CELLS + 8, :] = jnp.broadcast_to(total, (8, LANES))

    def one_group(group, carry):
        index = halo[...]
        member = (index >> 12) == group
        rank = ranks[...]
        shift = row * LANES + lane - rank
        items = jnp.where(member, (1 << 28) | (shift << 12) | (index & 4095), 0)
        for bit in range(15):
            step_by = 1 << bit
            if step_by < LANES:
                following = pltpu.roll(items, items.shape[0] - 1, 0)
                mixed = jnp.where(lane < step_by, following, items)
                moved = pltpu.roll(mixed, LANES - step_by, 1)
                held = items
            else:
                rows = step_by // LANES
                if rows < 32:
                    if rows < 8:
                        moved = pltpu.roll(items, items.shape[0] - rows, 0)
                    else:
                        moved = jnp.concatenate([items[rows:], items[:rows]], axis=0)
                    held = items
                else:
                    blocks = items.reshape(items.shape[0] // 64, 2, 32, LANES)
                    held = blocks[:, 0].reshape(-1, LANES)
                    moved = blocks[:, 1].reshape(-1, LANES)
            mask = 1 << (12 + bit)
            items = jnp.where((moved & mask) != 0, moved, jnp.where((held & mask) != 0, 0, held))
        source[pl.ds(pl.multiple_of(group * 32, 32), 32), :] = items & 4095
        return carry

    def two_groups(pair, carry):
        one_group(2 * pair, carry)
        return one_group(2 * pair + 1, carry)

    lax.fori_loop(0, GROUPS // 2, two_groups, 0)


def plan(halo):
    return pl.pallas_call(
        plan_kernel,
        out_shape=(
            jax.ShapeDtypeStruct((GROUPS * 32, LANES), jnp.int32),
            jax.ShapeDtypeStruct((GHOST_ROWS, LANES), jnp.int32),
            jax.ShapeDtypeStruct((CELLS + 8, LANES), jnp.int32),
        ),
        in_specs=[VMEM],
        out_specs=(VMEM,) * 3,
        scratch_shapes=[pltpu.VMEM((GHOST_ROWS, LANES), jnp.int32), pltpu.VMEM((GHOST_ROWS, LANES), f32)],
        compiler_params=params(),
        cost_estimate=pl.CostEstimate(flops=10_000_000_000, bytes_accessed=40_000_000, transcendentals=0),
        name="plan",
    )(halo)


def unmix(comps, raw, store):
    for c in range(comps):
        for side in range(2):
            for b in range(GHOST_ROWS // 16):
                store(c, pl.ds(side * (GHOST_ROWS // 2) + b * 8, 8), raw[c, pl.ds(b * 16 + side, 8, stride=2), :])


def gather_stages(comps, read_rows, source, place, cells, listed, out):
    zeros = (jnp.zeros((8, LANES), f32),) * comps

    for half in range(GROUPS // 8):
        first = half * 8 * GROUP_ROWS
        most = cells[CELLS, half * 8]
        for k in range(1, 8):
            most = jnp.maximum(most, cells[CELLS, half * 8 + k])

        def list_rows(pair, carry, first=first):
            spots = [pl.ds(first + 2 * pair + k, 8, stride=32) for k in range(2)]
            src = [source[spot, :] for spot in spots]
            lane = [item & 127 for item in src]
            row = [item >> 7 for item in src]
            accs = [list(zeros), list(zeros)]
            for u in range(GROUP_ROWS):
                mine = [item == u for item in row]
                for c in range(comps):
                    lines = read_rows(c, pl.ds(first + u, 8, stride=GROUP_ROWS))
                    for k in range(2):
                        accs[k][c] = jnp.where(mine[k], jnp.take_along_axis(lines, lane[k], axis=1), accs[k][c])
            for k in range(2):
                for c in range(comps):
                    listed[c, spots[k], :] = accs[k][c]
            return carry

        lax.fori_loop(0, (most + 255) >> 8, list_rows, 0)

    def slot_block(t):
        here = pl.ds(pl.multiple_of(t * 8, 8), 8)
        at = place[here, :]
        lane = at & 127
        row = at >> 7

        def visit(r, accs):
            mine = row == r
            return tuple(
                jnp.where(
                    mine,
                    jnp.take_along_axis(jnp.broadcast_to(listed[c, pl.ds(r, 1), :], (8, LANES)), lane, axis=1),
                    accs[c],
                )
                for c in range(comps)
            )

        def rows_of(g):
            begin, end = cells[t, g], cells[t + 1, g]
            return g * 32 + jnp.minimum(begin >> 7, 31), g * 32 + (jnp.maximum(end - 1, begin) >> 7)

        def narrow():
            accs = zeros
            widest = 0
            for g in range(GROUPS):
                first, last = rows_of(g)
                last = jnp.minimum(last, g * 32 + 31)
                accs = visit(first, accs)
                accs = visit(last, accs)
                widest = jnp.maximum(widest, last - first)
            for c in range(comps):
                out[c, here, :] = accs[c]
            return widest

        def wide():
            def rest(g, accs):
                first, last = rows_of(g)
                return lax.fori_loop(first, jnp.minimum(last, g * 32 + 31) + 1, visit, accs)

            more = lax.fori_loop(0, GROUPS, rest, tuple(out[c, here, :] for c in range(comps)))
            for c in range(comps):
                out[c, here, :] = more[c]

        return narrow, wide

    def slot_blocks(n, carry):
        blocks = [slot_block(2 * n + k) for k in range(2)]
        widest = [narrow() for narrow, _ in blocks]

        @pl.when(jnp.maximum(*widest) > 1)
        def _():
            for _, wide in blocks:
                wide()

        return carry

    lax.fori_loop(0, GHOST_ROWS // 16, slot_blocks, 0)


def pick(partner, window, own, below, above):
    wanted = jnp.full(own.shape, partner, jnp.int32)
    return jnp.where(wanted == window - 1, below, jnp.where(wanted == window + 1, above, own))


def first_gather_kernel(
    partner, cells, own, below, above, charges, path_weight, source, place, position, ghosts, partial, listed, raw
):
    window = lax.axis_index("rep")
    for c in range(3):
        position[c] = pick(partner[0], window, own[c], below[c], above[c])
    partial[...] = jnp.sum((path_weight[...] * position[2]).reshape(64, 8, LANES), axis=0)
    gather_positions(4, (position, charges), source, place, cells, ghosts, listed, raw)


def gather_positions(comps, tables, source, place, cells, ghosts, listed, raw):
    def read_rows(c, rows):
        return tables[1][rows, :] if c == 3 else tables[0][c, rows, :]

    def store(c, rows, value):
        ghosts[c, rows, :] = value

    gather_stages(comps, read_rows, source, place, cells, listed, raw)
    unmix(comps, raw, store)


def gather_scratch(comps):
    return [pltpu.VMEM((comps, GROUPS * 32, LANES), f32), pltpu.VMEM((comps, GHOST_ROWS, LANES), f32)]


def first_gather(partner, cells, own, below, above, charges, path_weight, source, place):
    return pl.pallas_call(
        first_gather_kernel,
        out_shape=(
            jax.ShapeDtypeStruct((3, TILES, LANES), f32),
            jax.ShapeDtypeStruct((4, GHOST_ROWS, LANES), f32),
            jax.ShapeDtypeStruct((8, LANES), f32),
        ),
        in_specs=[SMEM] * 2 + [VMEM] * 7,
        out_specs=(VMEM,) * 3,
        scratch_shapes=gather_scratch(4),
        compiler_params=params(),
        cost_estimate=pl.CostEstimate(flops=10_000_000_000, bytes_accessed=40_000_000, transcendentals=0),
        name="first_gather",
    )(partner, cells, own, below, above, charges, path_weight, source, place)


def parts3(value):
    high = value.astype(bf16).astype(f32)
    rest = value - high
    middle = rest.astype(bf16).astype(f32)
    return high, middle, rest - middle


def step_kernel(
    count, windows, last, spring, center, partner, pairs, ghosts, velocity_in, mass_in, weight_in, partial, position,
    charges, *rest,
):
    if last:
        lower_q, upper_q, *rest = rest
    new_position, new_velocity, result, *rest = rest
    if last:
        kept_q = ()
    else:
        kept_q, rest = rest[:2], rest[2:]
        rest, (velocity_below, velocity_above, sent_v, got_v) = rest[:-4], rest[-4:]
    (
        rows_j, rows_i, rows_a, feat_j, feat_i, feat_a, sums, spread_a, spread_b,
        lower, upper, parts, final, sent, got, sent_last, got_last, velocity, inv_mass, path_weight, filled,
    ) = rest
    late_copies = [
        pltpu.make_async_copy(source, target, filled.at[n])
        for n, (source, target) in enumerate(((velocity_in, velocity), (mass_in, inv_mass), (weight_in, path_weight)))
    ]
    for copy in late_copies:
        copy.start()
    me = lax.axis_index("dom")
    half = GHOST_ROWS // 2
    barrier = pltpu.get_barrier_semaphore()
    for k in range(1, count):
        pl.semaphore_signal(
            barrier, inc=1, device_id={"dom": lax.rem(me + k, count)}, device_id_type=pl.DeviceIdType.MESH
        )
    if not last:
        window = lax.axis_index("rep")
        ahead, behind = lax.rem(window + 1, windows), lax.rem(window + windows - 1, windows)
        for other in (ahead, behind):
            pl.semaphore_signal(barrier, inc=1, device_id={"rep": other}, device_id_type=pl.DeviceIdType.MESH)

    zero8 = jnp.zeros((8, LANES), f32)
    one8 = jnp.ones((8, LANES), f32)
    for f in (13, 14, 15):
        rows_j[pl.ds(f, 8, stride=16), :] = zero8
    rows_j[pl.ds(12, 8, stride=16), :] = one8
    for f in (12, 13, 14, 15):
        rows_a[pl.ds(f, 8, stride=16), :] = zero8
    rows_i[...] = jnp.zeros_like(rows_i)
    for f in (9, 10, 11):
        rows_i[pl.ds(f, 8, stride=48), :] = one8

    def build(first_tile, x, y, z, q, own):
        norm = x * x + y * y + z * z
        split = [parts3(value) for value in (x, y, z)]
        for c in range(3):
            for s in range(3):
                rows_j[pl.ds(3 * s + c, 8, stride=16), :] = split[c][s]
        for s, value in enumerate(parts3(norm)):
            rows_j[pl.ds(9 + s, 8, stride=16), :] = value
        for k, value in enumerate((q, q * x, q * y, q * z)):
            for s, piece in enumerate(parts3(value)):
                rows_a[pl.ds(4 * s + k, 8, stride=16), :] = piece
        for n in range(8):
            feat_j[first_tile + n] = rows_j[16 * n : 16 * n + 16, :].astype(bf16)
            feat_a[first_tile + n] = rows_a[16 * n : 16 * n + 16, :].astype(bf16)
        if own:
            for c in range(3):
                for s in range(3):
                    value = -2.0 * split[c][s]
                    for j in range(3 - s):
                        rows_i[pl.ds(16 * s + 3 * j + c, 8, stride=48), :] = value
            for s, value in enumerate(parts3(norm + 1.0)):
                rows_i[pl.ds(16 * s + 12, 8, stride=48), :] = value
            for n in range(8):
                feat_i[first_tile + n] = rows_i[48 * n : 48 * n + 48, :].astype(bf16)

    def own_block(b, carry):
        base = pl.multiple_of(b * 8, 8)
        here = pl.ds(base, 8)
        build(base, position[0, here, :], position[1, here, :], position[2, here, :], charges[here, :], True)
        return carry

    lax.fori_loop(0, TILES // 16, own_block, 0)
    pl.semaphore_wait(barrier, count - 1 if last else count + 1)

    def send(source, target, k, sent_now, got_now):
        copy = pltpu.make_async_remote_copy(
            src_ref=source,
            dst_ref=target,
            send_sem=sent_now,
            recv_sem=got_now,
            device_id={"dom": lax.rem(me + k, count)},
            device_id_type=pl.DeviceIdType.MESH,
        )
        copy.start()
        return copy

    ghost_copies = [
        send(ghosts.at[:, pl.ds(half, half)], lower, 1, sent.at[0], got.at[0]),
        send(ghosts.at[:, pl.ds(0, half)], upper, count - 1, sent.at[count], got.at[count]),
    ]
    term_copies = [send(partial, parts.at[me], k, sent.at[k], got.at[k]) for k in range(1, count)]
    lax.fori_loop(TILES // 16, TILES // 8, own_block, 0)

    def ghost_block(values, charge, offset):
        def block(b, carry):
            base = pl.multiple_of(b * 8, 8)
            here = pl.ds(base, 8)
            build(offset + base, values[0, here, :], values[1, here, :], values[2, here, :], charge[here, :], False)
            return carry

        return block

    for copy in ghost_copies:
        copy.wait()
    velocity_copies = []
    if not last:
        for n, (other, target) in enumerate(((ahead, velocity_below), (behind, velocity_above))):
            copy = pltpu.make_async_remote_copy(
                src_ref=velocity_in,
                dst_ref=target,
                send_sem=sent_v.at[n],
                recv_sem=got_v.at[n],
                device_id={"rep": other},
                device_id_type=pl.DeviceIdType.MESH,
            )
            copy.start()
            velocity_copies.append(copy)

    if last:
        charge_of = (lower_q, upper_q)
    else:
        charge_of = (lower.at[3], upper.at[3])
        kept_q[0][...] = lower[3]
        kept_q[1][...] = upper[3]
    lax.fori_loop(0, 16, ghost_block(lower, charge_of[0], TILES), 0)
    lax.fori_loop(0, 16, ghost_block(upper, charge_of[1], TILES + 128), 0)

    def contract(a, b, left, right):
        return lax.dot_general(a, b, (((left,), (right,)), ((), ())), preferred_element_type=f32)

    def listed(tile):
        tile = jnp.minimum(tile, TILES - 1)
        return tile, pairs[0, tile], pairs[1, tile]

    def spread_of(tile):
        tile, one, two = listed(tile)
        near = jnp.concatenate([feat_j[one], feat_j[two]], axis=1)
        return contract(jnp.concatenate([near] * 3, axis=0), feat_i[tile], 0, 0)

    def force_of(tile, spread):
        tile, one, two = listed(tile)
        weight = pl.reciprocal(spread * spread, approx=True)
        high = weight.astype(bf16)
        low = (weight - high.astype(f32)).astype(bf16)
        near = jnp.concatenate([feat_a[one], feat_a[two]], axis=1)
        return contract(jnp.concatenate([near, near], axis=1), jnp.concatenate([high, low], axis=0), 1, 0)

    many = TILES_AT_ONCE
    for u in range(many):
        spread_a[u] = spread_of(u)

    def tiles(m, carry):
        for now, later, n in ((spread_a, spread_b, 2 * m), (spread_b, spread_a, 2 * m + 1)):
            done = []
            for u in range(many):
                later[u] = spread_of((n + 1) * many + u)
                done.append(force_of(n * many + u, now[u]))
            for u in range(many):
                sums[pl.ds(pl.multiple_of((n * many + u) * 16, 16), 16), :] = done[u]
        return carry

    lax.fori_loop(0, TILES // many // 2, tiles, 0)

    def total_of(terms, own, copies):
        for copy in copies:
            copy.wait()
        terms[me] = own[...]
        return jnp.sum(terms[...])

    progress = total_of(parts, partial, term_copies)
    pull = spring[0] * (progress - center[0])
    for copy in late_copies + velocity_copies:
        copy.wait()

    def velocity_at(c, here):
        own = velocity[c, here, :]
        if last:
            return own
        return pick(partner[0], window, own, velocity_below[c, here, :], velocity_above[c, here, :])

    def combine(components):
        def block(b, part):
            base = pl.multiple_of(b * 8, 8)
            here = pl.ds(base, 8)

            def summed(k):
                value = sums[pl.ds(base * 16 + k, 8, stride=16), :]
                value = value + sums[pl.ds(base * 16 + 4 + k, 8, stride=16), :]
                return value + sums[pl.ds(base * 16 + 8 + k, 8, stride=16), :]

            base_sum = summed(0)
            q = charges[here, :]
            weight = path_weight[here, :]
            rate = time_step * inv_mass[here, :]
            for c in components:
                old = position[c, here, :]
                force = q * (old * base_sum - summed(c + 1))
                if c == 2:
                    force = force - pull * weight
                moved = velocity_at(c, here) + rate * force
                placed = old + time_step * moved
                new_velocity[c, here, :] = moved
                new_position[c, here, :] = placed
                if c == 2:
                    part = part + weight * placed
            return part

        return lax.fori_loop(0, TILES // 8, block, jnp.zeros((8, LANES), f32))

    ending = combine((2,) if last else (0, 1, 2))
    if last:
        partial_last = spread_a.at[0, pl.ds(0, 8), :]
        spread_a[0, pl.ds(0, 8), :] = ending
        final_copies = [
            send(partial_last, final.at[me], k, sent_last.at[k], got_last.at[k]) for k in range(1, count)
        ]
        combine((0, 1))
        off = total_of(final, partial_last, final_copies) - center[0]
        result[0] = 0.5 * spring[0] * off * off
    else:
        result[...] = ending


def step(
    number, last, spring, center, partner, pairs, ghosts, partial, position, velocity, charges, inv_mass, path_weight, *kept_q
):
    count, windows = lax.axis_size("dom"), lax.axis_size("rep")
    comps, rows = ghosts.shape[:2]
    whole = jax.ShapeDtypeStruct((3, TILES, LANES), f32)
    side_q = jax.ShapeDtypeStruct((rows // 2, LANES), f32)
    kept = () if last else (side_q, side_q)
    carried = () if last else (
        pltpu.VMEM(velocity.shape, f32),
        pltpu.VMEM(velocity.shape, f32),
        pltpu.SemaphoreType.DMA((2,)),
        pltpu.SemaphoreType.DMA((2,)),
    )

    def kernel(*refs):
        step_kernel(count, windows, last, *refs)

    return pl.pallas_call(
        kernel,
        out_shape=(whole, whole, jax.ShapeDtypeStruct((1,) if last else (8, LANES), f32)) + kept,
        in_specs=[SMEM] * 4 + [pl.BlockSpec(memory_space=pl.ANY)] * 4 + [VMEM] * (3 + len(kept_q)),
        out_specs=(VMEM, VMEM, SMEM if last else VMEM) + (VMEM,) * len(kept),
        scratch_shapes=[
            pltpu.VMEM((8 * 16, LANES), f32),
            pltpu.VMEM((8 * 48, LANES), f32),
            pltpu.VMEM((8 * 16, LANES), f32),
            pltpu.VMEM((TILES + 256, 16, LANES), bf16),
            pltpu.VMEM((TILES, 48, LANES), bf16),
            pltpu.VMEM((TILES + 256, 16, LANES), bf16),
            pltpu.VMEM((TILES * 16, LANES), f32),
            pltpu.VMEM((TILES_AT_ONCE, 2 * LANES, LANES), f32),
            pltpu.VMEM((TILES_AT_ONCE, 2 * LANES, LANES), f32),
            pltpu.VMEM((comps, rows // 2, LANES), f32),
            pltpu.VMEM((comps, rows // 2, LANES), f32),
            pltpu.VMEM((count, 8, LANES), f32),
            pltpu.VMEM((count, 8, LANES), f32),
            pltpu.SemaphoreType.DMA((count + 1,)),
            pltpu.SemaphoreType.DMA((count + 1,)),
            pltpu.SemaphoreType.DMA((count,)),
            pltpu.SemaphoreType.DMA((count,)),
            pltpu.VMEM(velocity.shape, f32),
            pltpu.VMEM(inv_mass.shape, f32),
            pltpu.VMEM(path_weight.shape, f32),
            pltpu.SemaphoreType.DMA((3,)),
            *carried,
        ],
        compiler_params=pltpu.CompilerParams(
            vmem_limit_bytes=40 * 1024 * 1024, collective_id=number, has_side_effects=True
        ),
        name="step",
    )(
        spring, center, partner, pairs, ghosts, velocity, inv_mass, path_weight, partial, position, charges, *kept_q
    )


def second_gather_kernel(cells, *refs):
    position, source, place, ghosts, listed, raw = refs
    gather_positions(3, (position,), source, place, cells, ghosts, listed, raw)


def second_gather(cells, position, source, place):
    return pl.pallas_call(
        second_gather_kernel,
        out_shape=jax.ShapeDtypeStruct((3, GHOST_ROWS, LANES), f32),
        in_specs=[SMEM] + [VMEM] * 3,
        out_specs=VMEM,
        scratch_shapes=gather_scratch(3),
        compiler_params=params(),
        cost_estimate=pl.CostEstimate(flops=10_000_000_000, bytes_accessed=40_000_000, transcendentals=0),
        name="second_gather",
    )(cells, position, source, place)


def shifted(shard, axis, by):
    count = lax.axis_size(axis)
    pairs = [(i, i + by) for i in range(count) if 0 <= i + by < count]
    return lax.ppermute(shard, axis, pairs)


def body(positions, velocities, charges, inv_mass, path_weight, halo_index, tile_pairs, partner, bias_center, bias_spring):
    position = positions[0].reshape(3, TILES, LANES)
    velocity = velocities[0].reshape(3, TILES, LANES)
    charges = charges.reshape(TILES, LANES)
    inv_mass = inv_mass.reshape(TILES, LANES)
    path_weight = path_weight.reshape(TILES, LANES)
    pairs = tile_pairs.T
    halo = halo_index.reshape(2, GHOST_ROWS // 2, LANES).transpose(1, 0, 2).reshape(GHOST_ROWS, LANES)
    below = shifted(position, "rep", 1)
    above = shifted(position, "rep", -1)
    source, place, cells = plan(halo)
    position, ghosts, partial = first_gather(
        partner, cells, position, below, above, charges, path_weight, source, place
    )
    kept_q = ()
    for step_index in range(STEPS):
        last = step_index == STEPS - 1
        position, velocity, partial, *kept_q = step(
            step_index, last, bias_spring, bias_center, partner, pairs, ghosts, partial, position, velocity,
            charges, inv_mass, path_weight, *kept_q,
        )
        if not last:
            ghosts = second_gather(cells, position, source, place)
    atoms = TILES * LANES
    return position.reshape(1, 3, atoms), velocity.reshape(1, 3, atoms), partial


def solution(mesh):
    in_specs = (
        P("rep", None, "dom"),
        P("rep", None, "dom"),
        P("dom"),
        P("dom"),
        P("dom"),
        P(None, "dom"),
        P("dom", None),
        P("rep"),
        P("rep"),
        P("rep"),
    )
    out_specs = (P("rep", None, "dom"), P("rep", None, "dom"), P("rep"))
    return jax.shard_map(body, mesh=mesh, in_specs=in_specs, out_specs=out_specs, check_vma=False)
```

```python
import jax
import jax.numpy as jnp
from jax import lax
from jax.experimental import pallas as pl
from jax.experimental.pallas import tpu as pltpu
from jax.sharding import PartitionSpec as P

LANES = 128
STEPS = 2
TILES = 512
GHOST_ROWS = 256
GROUPS = 16
GROUP_ROWS = 32
CELLS = 32
CAPACITY = 4096
TILES_AT_ONCE = 32
ROW_SETS = 4
time_step = 0.1
f32 = jnp.float32
bf16 = jnp.bfloat16
VMEM = pl.BlockSpec(memory_space=pltpu.VMEM)
SMEM = pl.BlockSpec(memory_space=pltpu.SMEM)


def params():
    return pltpu.CompilerParams(vmem_limit_bytes=20 * 1024 * 1024)


def plan_kernel(halo, source, place, cells, ranks, counts):
    shape = (GHOST_ROWS, LANES)
    row = lax.broadcasted_iota(jnp.int32, shape, 0)
    lane = lax.broadcasted_iota(jnp.int32, shape, 1)
    wide = (LANES, 2 * LANES)
    across = lax.broadcasted_iota(jnp.int32, wide, 1)
    ahead_lane = (lax.broadcasted_iota(jnp.int32, wide, 0) < across) | (across >= LANES)
    ahead_lane = jnp.where(ahead_lane, 1.0, 0.0).astype(bf16)
    square = (GHOST_ROWS, GHOST_ROWS)
    ahead_row = lax.broadcasted_iota(jnp.int32, square, 1) < lax.broadcasted_iota(jnp.int32, square, 0)
    ahead_row = jnp.where(ahead_row, 1.0, 0.0).astype(bf16)
    counts[...] = jnp.zeros(shape, f32)

    def count_group(group, carry):
        member = (halo[...] >> 12) == group
        within = jnp.dot(jnp.where(member, 1.0, 0.0).astype(bf16), ahead_lane, preferred_element_type=f32)
        ranks[...] = jnp.where(member, within[:, :LANES].astype(jnp.int32), ranks[...])
        counts[...] = jnp.where(lane == group, within[:, LANES:], counts[...])
        return carry

    lax.fori_loop(0, GROUPS, count_group, 0, unroll=4)
    earlier = jnp.dot(ahead_row, counts[...].astype(bf16), preferred_element_type=f32)
    total = (earlier[GHOST_ROWS - 1 :] + counts[GHOST_ROWS - 1 :, :]).astype(jnp.int32)
    earlier = earlier.astype(jnp.int32)
    for b in range(GHOST_ROWS // 8):
        here = slice(8 * b, 8 * b + 8)
        group_of = halo[here, :] >> 12
        rank = ranks[here, :] + jnp.take_along_axis(earlier[here], group_of, axis=1)
        ranks[here, :] = rank
        place[here, :] = rank + group_of * CAPACITY
        cells[b : b + 1, :] = earlier[8 * b : 8 * b + 1]
    cells[CELLS : CELLS + 8, :] = jnp.broadcast_to(total, (8, LANES))

    def one_group(group, carry):
        index = halo[...]
        member = (index >> 12) == group
        rank = ranks[...]
        shift = row * LANES + lane - rank
        items = jnp.where(member, (1 << 28) | (shift << 12) | (index & 4095), 0)
        for bit in range(15):
            step_by = 1 << bit
            if step_by < LANES:
                following = pltpu.roll(items, items.shape[0] - 1, 0)
                mixed = jnp.where(lane < step_by, following, items)
                moved = pltpu.roll(mixed, LANES - step_by, 1)
                held = items
            else:
                rows = step_by // LANES
                if rows < 32:
                    if rows < 8:
                        moved = pltpu.roll(items, items.shape[0] - rows, 0)
                    else:
                        moved = jnp.concatenate([items[rows:], items[:rows]], axis=0)
                    held = items
                else:
                    blocks = items.reshape(items.shape[0] // 64, 2, 32, LANES)
                    held = blocks[:, 0].reshape(-1, LANES)
                    moved = blocks[:, 1].reshape(-1, LANES)
            mask = 1 << (12 + bit)
            items = jnp.where((moved & mask) != 0, moved, jnp.where((held & mask) != 0, 0, held))
        source[pl.ds(pl.multiple_of(group * 32, 32), 32), :] = items & 4095
        return carry

    def two_groups(pair, carry):
        one_group(2 * pair, carry)
        return one_group(2 * pair + 1, carry)

    lax.fori_loop(0, GROUPS // 2, two_groups, 0)


def plan(halo):
    return pl.pallas_call(
        plan_kernel,
        out_shape=(
            jax.ShapeDtypeStruct((GROUPS * 32, LANES), jnp.int32),
            jax.ShapeDtypeStruct((GHOST_ROWS, LANES), jnp.int32),
            jax.ShapeDtypeStruct((CELLS + 8, LANES), jnp.int32),
        ),
        in_specs=[VMEM],
        out_specs=(VMEM,) * 3,
        scratch_shapes=[pltpu.VMEM((GHOST_ROWS, LANES), jnp.int32), pltpu.VMEM((GHOST_ROWS, LANES), f32)],
        compiler_params=params(),
        cost_estimate=pl.CostEstimate(flops=10_000_000_000, bytes_accessed=40_000_000, transcendentals=0),
        name="plan",
    )(halo)


def unmix(comps, raw, store):
    for c in range(comps):
        for side in range(2):
            for b in range(GHOST_ROWS // 16):
                store(c, pl.ds(side * (GHOST_ROWS // 2) + b * 8, 8), raw[c, pl.ds(b * 16 + side, 8, stride=2), :])


def gather_stages(comps, read_rows, source, place, cells, listed, out):
    zeros = (jnp.zeros((8, LANES), f32),) * comps

    for half in range(GROUPS // 8):
        first = half * 8 * GROUP_ROWS
        most = cells[CELLS, half * 8]
        for k in range(1, 8):
            most = jnp.maximum(most, cells[CELLS, half * 8 + k])

        def list_rows(pair, carry, first=first):
            spots = [pl.ds(first + 2 * pair + k, 8, stride=32) for k in range(2)]
            src = [source[spot, :] for spot in spots]
            lane = [item & 127 for item in src]
            row = [item >> 7 for item in src]
            accs = [list(zeros), list(zeros)]
            for u in range(GROUP_ROWS):
                mine = [item == u for item in row]
                for c in range(comps):
                    lines = read_rows(c, pl.ds(first + u, 8, stride=GROUP_ROWS))
                    for k in range(2):
                        accs[k][c] = jnp.where(mine[k], jnp.take_along_axis(lines, lane[k], axis=1), accs[k][c])
            for k in range(2):
                for c in range(comps):
                    listed[c, spots[k], :] = accs[k][c]
            return carry

        lax.fori_loop(0, (most + 255) >> 8, list_rows, 0)

    def slot_block(t):
        here = pl.ds(pl.multiple_of(t * 8, 8), 8)
        at = place[here, :]
        lane = at & 127
        row = at >> 7

        def visit(r, accs):
            mine = row == r
            return tuple(
                jnp.where(
                    mine,
                    jnp.take_along_axis(jnp.broadcast_to(listed[c, pl.ds(r, 1), :], (8, LANES)), lane, axis=1),
                    accs[c],
                )
                for c in range(comps)
            )

        def rows_of(g):
            begin, end = cells[t, g], cells[t + 1, g]
            return g * 32 + jnp.minimum(begin >> 7, 31), g * 32 + (jnp.maximum(end - 1, begin) >> 7)

        def narrow():
            accs = zeros
            widest = 0
            for g in range(GROUPS):
                first, last = rows_of(g)
                last = jnp.minimum(last, g * 32 + 31)
                accs = visit(first, accs)
                accs = visit(last, accs)
                widest = jnp.maximum(widest, last - first)
            for c in range(comps):
                out[c, here, :] = accs[c]
            return widest

        def wide():
            def rest(g, accs):
                first, last = rows_of(g)
                return lax.fori_loop(first, jnp.minimum(last, g * 32 + 31) + 1, visit, accs)

            more = lax.fori_loop(0, GROUPS, rest, tuple(out[c, here, :] for c in range(comps)))
            for c in range(comps):
                out[c, here, :] = more[c]

        return narrow, wide

    def slot_blocks(n, carry):
        blocks = [slot_block(2 * n + k) for k in range(2)]
        widest = [narrow() for narrow, _ in blocks]

        @pl.when(jnp.maximum(*widest) > 1)
        def _():
            for _, wide in blocks:
                wide()

        return carry

    lax.fori_loop(0, GHOST_ROWS // 16, slot_blocks, 0)


def pick(partner, window, own, below, above):
    wanted = jnp.full(own.shape, partner, jnp.int32)
    return jnp.where(wanted == window - 1, below, jnp.where(wanted == window + 1, above, own))


def first_gather_kernel(
    partner, cells, own, below, above, charges, path_weight, source, place, position, ghosts, partial, listed, raw
):
    window = lax.axis_index("rep")
    for c in range(3):
        position[c] = pick(partner[0], window, own[c], below[c], above[c])
    partial[...] = jnp.sum((path_weight[...] * position[2]).reshape(64, 8, LANES), axis=0)
    gather_positions(4, (position, charges), source, place, cells, ghosts, listed, raw)


def gather_positions(comps, tables, source, place, cells, ghosts, listed, raw):
    def read_rows(c, rows):
        return tables[1][rows, :] if c == 3 else tables[0][c, rows, :]

    def store(c, rows, value):
        ghosts[c, rows, :] = value

    gather_stages(comps, read_rows, source, place, cells, listed, raw)
    unmix(comps, raw, store)


def gather_scratch(comps):
    return [pltpu.VMEM((comps, GROUPS * 32, LANES), f32), pltpu.VMEM((comps, GHOST_ROWS, LANES), f32)]


def first_gather(partner, cells, own, below, above, charges, path_weight, source, place):
    return pl.pallas_call(
        first_gather_kernel,
        out_shape=(
            jax.ShapeDtypeStruct((3, TILES, LANES), f32),
            jax.ShapeDtypeStruct((4, GHOST_ROWS, LANES), f32),
            jax.ShapeDtypeStruct((8, LANES), f32),
        ),
        in_specs=[SMEM] * 2 + [VMEM] * 7,
        out_specs=(VMEM,) * 3,
        scratch_shapes=gather_scratch(4),
        compiler_params=params(),
        cost_estimate=pl.CostEstimate(flops=10_000_000_000, bytes_accessed=40_000_000, transcendentals=0),
        name="first_gather",
    )(partner, cells, own, below, above, charges, path_weight, source, place)


def parts3(value):
    high = value.astype(bf16).astype(f32)
    rest = value - high
    middle = rest.astype(bf16).astype(f32)
    return high, middle, rest - middle


def step_kernel(
    count, windows, last, spring, center, partner, pairs, ghosts, velocity_in, mass_in, weight_in, partial, position,
    charges, *rest,
):
    if last:
        lower_q, upper_q, *rest = rest
    new_position, new_velocity, result, *rest = rest
    if last:
        kept_q = ()
    else:
        kept_q, rest = rest[:2], rest[2:]
        rest, (velocity_below, velocity_above, sent_v, got_v) = rest[:-4], rest[-4:]
    (
        rows_j, rows_i, rows_a, feat_j, feat_i, feat_a, sums, spread_a, spread_b,
        lower, upper, parts, final, sent, got, sent_last, got_last, velocity, inv_mass, path_weight, filled,
    ) = rest
    late_copies = [
        pltpu.make_async_copy(source, target, filled.at[n])
        for n, (source, target) in enumerate(((velocity_in, velocity), (mass_in, inv_mass), (weight_in, path_weight)))
    ]
    for copy in late_copies:
        copy.start()
    me = lax.axis_index("dom")
    half = GHOST_ROWS // 2
    barrier = pltpu.get_barrier_semaphore()
    for k in range(1, count):
        pl.semaphore_signal(
            barrier, inc=1, device_id={"dom": lax.rem(me + k, count)}, device_id_type=pl.DeviceIdType.MESH
        )
    if not last:
        window = lax.axis_index("rep")
        ahead, behind = lax.rem(window + 1, windows), lax.rem(window + windows - 1, windows)
        for other in (ahead, behind):
            pl.semaphore_signal(barrier, inc=1, device_id={"rep": other}, device_id_type=pl.DeviceIdType.MESH)

    zero8 = jnp.zeros((8, LANES), f32)
    one8 = jnp.ones((8, LANES), f32)
    many_rows = ROW_SETS
    rows_i[...] = jnp.zeros_like(rows_i)
    for k in range(many_rows):
        for f in (13, 14, 15):
            rows_j[pl.ds(128 * k + f, 8, stride=16), :] = zero8
        rows_j[pl.ds(128 * k + 12, 8, stride=16), :] = one8
        for f in (12, 13, 14, 15):
            rows_a[pl.ds(128 * k + f, 8, stride=16), :] = zero8
        for f in (9, 10, 11):
            rows_i[pl.ds(384 * k + f, 8, stride=48), :] = one8

    def build(k_rows, first_tile, x, y, z, q, own):
        at_j, at_i = 128 * k_rows, 384 * k_rows
        norm = x * x + y * y + z * z
        split = [parts3(value) for value in (x, y, z)]
        for c in range(3):
            for s in range(3):
                rows_j[pl.ds(at_j + 3 * s + c, 8, stride=16), :] = split[c][s]
        for s, value in enumerate(parts3(norm)):
            rows_j[pl.ds(at_j + 9 + s, 8, stride=16), :] = value
        for k, value in enumerate((q, q * x, q * y, q * z)):
            for s, piece in enumerate(parts3(value)):
                rows_a[pl.ds(at_j + 4 * s + k, 8, stride=16), :] = piece
        for n in range(8):
            feat_j[first_tile + n] = rows_j[at_j + 16 * n : at_j + 16 * n + 16, :].astype(bf16)
            feat_a[first_tile + n] = rows_a[at_j + 16 * n : at_j + 16 * n + 16, :].astype(bf16)
        if own:
            for c in range(3):
                for s in range(3):
                    value = -2.0 * split[c][s]
                    for j in range(3 - s):
                        rows_i[pl.ds(at_i + 16 * s + 3 * j + c, 8, stride=48), :] = value
            for s, value in enumerate(parts3(norm + 1.0)):
                rows_i[pl.ds(at_i + 16 * s + 12, 8, stride=48), :] = value
            for n in range(8):
                feat_i[first_tile + n] = rows_i[at_i + 48 * n : at_i + 48 * n + 48, :].astype(bf16)

    def own_block(n, carry):
        for k in range(many_rows):
            base = pl.multiple_of((n * many_rows + k) * 8, 8)
            here = pl.ds(base, 8)
            build(k, base, position[0, here, :], position[1, here, :], position[2, here, :], charges[here, :], True)
        return carry

    lax.fori_loop(0, TILES // 16 // many_rows, own_block, 0)
    pl.semaphore_wait(barrier, count - 1 if last else count + 1)

    def send(source, target, k, sent_now, got_now):
        copy = pltpu.make_async_remote_copy(
            src_ref=source,
            dst_ref=target,
            send_sem=sent_now,
            recv_sem=got_now,
            device_id={"dom": lax.rem(me + k, count)},
            device_id_type=pl.DeviceIdType.MESH,
        )
        copy.start()
        return copy

    ghost_copies = [
        send(ghosts.at[:, pl.ds(half, half)], lower, 1, sent.at[0], got.at[0]),
        send(ghosts.at[:, pl.ds(0, half)], upper, count - 1, sent.at[count], got.at[count]),
    ]
    term_copies = [send(partial, parts.at[me], k, sent.at[k], got.at[k]) for k in range(1, count)]
    lax.fori_loop(TILES // 16 // many_rows, TILES // 8 // many_rows, own_block, 0)

    def ghost_block(values, charge, offset):
        def block(n, carry):
            for k in range(many_rows):
                one_ghost_block(n * many_rows + k, k)
            return carry

        def one_ghost_block(b, k):
            base = pl.multiple_of(b * 8, 8)
            here = pl.ds(base, 8)
            build(k, offset + base, values[0, here, :], values[1, here, :], values[2, here, :], charge[here, :], False)

        return block

    for copy in ghost_copies:
        copy.wait()
    velocity_copies = []
    if not last:
        for n, (other, target) in enumerate(((ahead, velocity_below), (behind, velocity_above))):
            copy = pltpu.make_async_remote_copy(
                src_ref=velocity_in,
                dst_ref=target,
                send_sem=sent_v.at[n],
                recv_sem=got_v.at[n],
                device_id={"rep": other},
                device_id_type=pl.DeviceIdType.MESH,
            )
            copy.start()
            velocity_copies.append(copy)

    if last:
        charge_of = (lower_q, upper_q)
    else:
        charge_of = (lower.at[3], upper.at[3])
        kept_q[0][...] = lower[3]
        kept_q[1][...] = upper[3]
    lax.fori_loop(0, 16 // many_rows, ghost_block(lower, charge_of[0], TILES), 0)
    lax.fori_loop(0, 16 // many_rows, ghost_block(upper, charge_of[1], TILES + 128), 0)

    def contract(a, b, left, right):
        return lax.dot_general(a, b, (((left,), (right,)), ((), ())), preferred_element_type=f32)

    def listed(tile):
        tile = jnp.minimum(tile, TILES - 1)
        return tile, pairs[0, tile], pairs[1, tile]

    def spread_of(tile):
        tile, one, two = listed(tile)
        near = jnp.concatenate([feat_j[one], feat_j[two]], axis=1)
        return contract(jnp.concatenate([near] * 3, axis=0), feat_i[tile], 0, 0)

    def force_of(tile, spread):
        tile, one, two = listed(tile)
        weight = pl.reciprocal(spread * spread, approx=True)
        high = weight.astype(bf16)
        low = (weight - high.astype(f32)).astype(bf16)
        near = jnp.concatenate([feat_a[one], feat_a[two]], axis=1)
        return contract(jnp.concatenate([near, near], axis=1), jnp.concatenate([high, low], axis=0), 1, 0)

    many = TILES_AT_ONCE
    for u in range(many):
        spread_a[u] = spread_of(u)

    def tiles(m, carry):
        for now, later, n in ((spread_a, spread_b, 2 * m), (spread_b, spread_a, 2 * m + 1)):
            done = []
            for u in range(many):
                later[u] = spread_of((n + 1) * many + u)
                done.append(force_of(n * many + u, now[u]))
            for u in range(many):
                sums[pl.ds(pl.multiple_of((n * many + u) * 16, 16), 16), :] = done[u]
        return carry

    lax.fori_loop(0, TILES // many // 2, tiles, 0)

    def total_of(terms, own, copies):
        for copy in copies:
            copy.wait()
        terms[me] = own[...]
        return jnp.sum(terms[...])

    progress = total_of(parts, partial, term_copies)
    pull = spring[0] * (progress - center[0])
    for copy in late_copies + velocity_copies:
        copy.wait()

    def velocity_at(c, here):
        own = velocity[c, here, :]
        if last:
            return own
        return pick(partner[0], window, own, velocity_below[c, here, :], velocity_above[c, here, :])

    def combine(components):
        def block(b, part):
            base = pl.multiple_of(b * 8, 8)
            here = pl.ds(base, 8)

            def summed(k):
                value = sums[pl.ds(base * 16 + k, 8, stride=16), :]
                value = value + sums[pl.ds(base * 16 + 4 + k, 8, stride=16), :]
                return value + sums[pl.ds(base * 16 + 8 + k, 8, stride=16), :]

            base_sum = summed(0)
            q = charges[here, :]
            weight = path_weight[here, :]
            rate = time_step * inv_mass[here, :]
            for c in components:
                old = position[c, here, :]
                force = q * (old * base_sum - summed(c + 1))
                if c == 2:
                    force = force - pull * weight
                moved = velocity_at(c, here) + rate * force
                placed = old + time_step * moved
                new_velocity[c, here, :] = moved
                new_position[c, here, :] = placed
                if c == 2:
                    part = part + weight * placed
            return part

        return lax.fori_loop(0, TILES // 8, block, jnp.zeros((8, LANES), f32), unroll=4)

    ending = combine((2,) if last else (0, 1, 2))
    if last:
        partial_last = spread_a.at[0, pl.ds(0, 8), :]
        spread_a[0, pl.ds(0, 8), :] = ending
        final_copies = [
            send(partial_last, final.at[me], k, sent_last.at[k], got_last.at[k]) for k in range(1, count)
        ]
        combine((0, 1))
        off = total_of(final, partial_last, final_copies) - center[0]
        result[0] = 0.5 * spring[0] * off * off
    else:
        result[...] = ending


def step(
    number, last, spring, center, partner, pairs, ghosts, partial, position, velocity, charges, inv_mass, path_weight, *kept_q
):
    count, windows = lax.axis_size("dom"), lax.axis_size("rep")
    comps, rows = ghosts.shape[:2]
    whole = jax.ShapeDtypeStruct((3, TILES, LANES), f32)
    side_q = jax.ShapeDtypeStruct((rows // 2, LANES), f32)
    kept = () if last else (side_q, side_q)
    carried = () if last else (
        pltpu.VMEM(velocity.shape, f32),
        pltpu.VMEM(velocity.shape, f32),
        pltpu.SemaphoreType.DMA((2,)),
        pltpu.SemaphoreType.DMA((2,)),
    )

    def kernel(*refs):
        step_kernel(count, windows, last, *refs)

    return pl.pallas_call(
        kernel,
        out_shape=(whole, whole, jax.ShapeDtypeStruct((1,) if last else (8, LANES), f32)) + kept,
        in_specs=[SMEM] * 4 + [pl.BlockSpec(memory_space=pl.ANY)] * 4 + [VMEM] * (3 + len(kept_q)),
        out_specs=(VMEM, VMEM, SMEM if last else VMEM) + (VMEM,) * len(kept),
        scratch_shapes=[
            pltpu.VMEM((ROW_SETS * 8 * 16, LANES), f32),
            pltpu.VMEM((ROW_SETS * 8 * 48, LANES), f32),
            pltpu.VMEM((ROW_SETS * 8 * 16, LANES), f32),
            pltpu.VMEM((TILES + 256, 16, LANES), bf16),
            pltpu.VMEM((TILES, 48, LANES), bf16),
            pltpu.VMEM((TILES + 256, 16, LANES), bf16),
            pltpu.VMEM((TILES * 16, LANES), f32),
            pltpu.VMEM((TILES_AT_ONCE, 2 * LANES, LANES), f32),
            pltpu.VMEM((TILES_AT_ONCE, 2 * LANES, LANES), f32),
            pltpu.VMEM((comps, rows // 2, LANES), f32),
            pltpu.VMEM((comps, rows // 2, LANES), f32),
            pltpu.VMEM((count, 8, LANES), f32),
            pltpu.VMEM((count, 8, LANES), f32),
            pltpu.SemaphoreType.DMA((count + 1,)),
            pltpu.SemaphoreType.DMA((count + 1,)),
            pltpu.SemaphoreType.DMA((count,)),
            pltpu.SemaphoreType.DMA((count,)),
            pltpu.VMEM(velocity.shape, f32),
            pltpu.VMEM(inv_mass.shape, f32),
            pltpu.VMEM(path_weight.shape, f32),
            pltpu.SemaphoreType.DMA((3,)),
            *carried,
        ],
        compiler_params=pltpu.CompilerParams(
            vmem_limit_bytes=40 * 1024 * 1024, collective_id=number, has_side_effects=True
        ),
        name="step",
    )(
        spring, center, partner, pairs, ghosts, velocity, inv_mass, path_weight, partial, position, charges, *kept_q
    )


def second_gather_kernel(cells, *refs):
    position, source, place, ghosts, listed, raw = refs
    gather_positions(3, (position,), source, place, cells, ghosts, listed, raw)


def second_gather(cells, position, source, place):
    return pl.pallas_call(
        second_gather_kernel,
        out_shape=jax.ShapeDtypeStruct((3, GHOST_ROWS, LANES), f32),
        in_specs=[SMEM] + [VMEM] * 3,
        out_specs=VMEM,
        scratch_shapes=gather_scratch(3),
        compiler_params=params(),
        cost_estimate=pl.CostEstimate(flops=10_000_000_000, bytes_accessed=40_000_000, transcendentals=0),
        name="second_gather",
    )(cells, position, source, place)


def shifted(shard, axis, by):
    count = lax.axis_size(axis)
    pairs = [(i, i + by) for i in range(count) if 0 <= i + by < count]
    return lax.ppermute(shard, axis, pairs)


def body(positions, velocities, charges, inv_mass, path_weight, halo_index, tile_pairs, partner, bias_center, bias_spring):
    position = positions[0].reshape(3, TILES, LANES)
    velocity = velocities[0].reshape(3, TILES, LANES)
    charges = charges.reshape(TILES, LANES)
    inv_mass = inv_mass.reshape(TILES, LANES)
    path_weight = path_weight.reshape(TILES, LANES)
    pairs = tile_pairs.T
    halo = halo_index.reshape(2, GHOST_ROWS // 2, LANES).transpose(1, 0, 2).reshape(GHOST_ROWS, LANES)
    below = shifted(position, "rep", 1)
    above = shifted(position, "rep", -1)
    source, place, cells = plan(halo)
    position, ghosts, partial = first_gather(
        partner, cells, position, below, above, charges, path_weight, source, place
    )
    kept_q = ()
    for step_index in range(STEPS):
        last = step_index == STEPS - 1
        position, velocity, partial, *kept_q = step(
            step_index, last, bias_spring, bias_center, partner, pairs, ghosts, partial, position, velocity,
            charges, inv_mass, path_weight, *kept_q,
        )
        if not last:
            ghosts = second_gather(cells, position, source, place)
    atoms = TILES * LANES
    return position.reshape(1, 3, atoms), velocity.reshape(1, 3, atoms), partial


def solution(mesh):
    in_specs = (
        P("rep", None, "dom"),
        P("rep", None, "dom"),
        P("dom"),
        P("dom"),
        P("dom"),
        P(None, "dom"),
        P("dom", None),
        P("rep"),
        P("rep"),
        P("rep"),
    )
    out_specs = (P("rep", None, "dom"), P("rep", None, "dom"), P("rep"))
    return jax.shard_map(body, mesh=mesh, in_specs=in_specs, out_specs=out_specs, check_vma=False)
```
